256 devices in a mesh: dp: 4 (over y_hi, core), row: 8 (over z), col: 8 (over x, y_lo).
Axes of the slice: x: 4, y: 4 (y_hi: 2, y_lo: 2; y = y_hi * 2 + y_lo), z: 8, core: 2. Of those that a mesh axis runs over, the one named last changes fastest.
Arguments:
- events: bfloat16 [4096, 4096], P(('dp', 'row'), 'col'), may hold values from -6 to 6
- out_grad: bfloat16 [4096, 4096], P(('dp', 'row'), 'col'), may hold values from -6 to 6
- w_uvqk: bfloat16 [4096, 16384], P('col', 'row'), may hold values from -0.09375 to 0.09375
- w_output: bfloat16 [4096, 4096], P('row', 'col'), may hold values from -0.09375 to 0.09375
- hist_len: int32 [32, 8], replicated, may hold values from 1 to 64, 128 in all within a row
- token_slot: int32 [4096], replicated, may hold values from 0 to 4095, as said below
Outputs:
- layer_out: bfloat16 [4096, 4096], P(('dp', 'row'), 'col')
- event_grad: bfloat16 [4096, 4096], P(('dp', 'row'), 'col')
- uvqk_grad: float32 [4096, 16384], P('col', 'row')
- output_grad: float32 [4096, 4096], P('row', 'col')
The draws below stay inside these ranges and needn't reach their ends.
Inputs may be any that keep to these rules, and one draw needn't show every extreme that they name: `token_slot`: A permutation. An event goes to an owner with the same row index as the device that holds it, and every device sends exactly 32 events to every owner of its row index.
All inputs are finite; a program needn't handle non-finite values.
Results may differ from the reference program's by a relative error of at most 0.04.
Values may be sent and summed in bfloat16 or wider, within the bound.
No kernel may reach another device: no remote copies, remote signals or barrier semaphores. Data moves between devices by JAX's collectives and lax.ppermute only.
A program may use at most 128 MiB of HBM per device.

```python
import math
import jax
import jax.numpy as jnp
import numpy as np
from jax import lax

D = 4096
HEADS = 32
HEADDIM = 128
TOK_OWN = 128
NH = 8
HD = 4096
HMAX = 64
SEND = 32
OWNERS = 32
TOKENS = 4096
N_DP = 4
N_ROW = 8
N_COL = 8


def draw_token_slot(key, part):
    key = jax.random.fold_in(key, 11)
    first_key, second_key = jax.random.split(key)
    owner_keys = jax.random.split(first_key, N_DP * N_ROW)
    orders = jax.vmap(lambda single: jax.random.permutation(single, TOK_OWN))(owner_keys)
    orders = orders.reshape(N_DP, N_ROW, TOK_OWN).astype(jnp.int32)
    source = jnp.arange(N_DP, dtype=jnp.int32)[:, None, None]
    row_pos = jnp.arange(N_ROW, dtype=jnp.int32)[None, :, None]
    within = jnp.arange(TOK_OWN, dtype=jnp.int32)[None, None, :]
    target = within // SEND
    offset = within % SEND
    picked = orders[target, row_pos, source * SEND + offset]
    slots = (target * N_ROW + row_pos) * TOK_OWN + picked
    shuffle_keys = jax.random.split(second_key, N_DP * N_ROW)
    shuffles = jax.vmap(lambda single: jax.random.permutation(single, TOK_OWN))(shuffle_keys)
    shuffles = shuffles.reshape(N_DP, N_ROW, TOK_OWN).astype(jnp.int32)
    slots = jnp.take_along_axis(slots, shuffles, axis=2)
    return slots.reshape(-1).astype(jnp.int32)


def steps_of(own_key, shape, cuts, low, top_value):
    loudness, own = 1.0, jax.random.fold_in(own_key, 6)
    for position, shards_of in cuts:
        draws = jnp.exp(jax.random.uniform(jax.random.fold_in(own, position), (shards_of,), jnp.float32, low / len(cuts), top_value / len(cuts)))
        loudness = loudness * jnp.repeat(draws, shape[position] // shards_of).reshape([-1 if axis == position else 1 for axis in range(len(shape))])
    return loudness


def length_profile(count, total, reach, skew):
    weights = [(1 << 20) // math.isqrt(grade ** skew) + 1 for grade in range(2, count + 1)]
    rest, holding = total - reach - (count - 1), [1] * (count - 1)
    while rest > 0:
        free = [i for i in range(count - 1) if holding[i] < reach]
        whole, remaining = sum([weights[i] for i in free]), rest
        for i in free:
            extra = min(reach - holding[i], max(1, remaining * weights[i] // whole), rest)
            holding[i] = holding[i] + extra
            rest = rest - extra
    return np.array([reach] + holding)


def ragged(own_key, amount, total, reach, skew):
    if amount == 2:
        one = jax.random.randint(own_key, (), max(1, total - reach), min(reach, total - 1) + 1)
        return jnp.stack([one, total - one])
    sizes = jnp.asarray(length_profile(amount, total, reach, skew), jnp.int32)
    couples = (amount - 1) // 2
    source_of, sink = sizes[1:1 + 2 * couples:2], sizes[2:2 + 2 * couples:2]
    slack = jnp.minimum(source_of - 1, reach - sink)
    moved = jax.random.randint(jax.random.fold_in(own_key, 1), (couples,), 0, 1 << 20) % (slack + 1)
    sizes = sizes.at[1:1 + 2 * couples:2].set(source_of - moved).at[2:2 + 2 * couples:2].set(sink + moved)
    return sizes[jax.random.permutation(jax.random.fold_in(own_key, 2), amount)]


def scatter_about(rng, extent, deviation, reach, cuts=(), kind=jnp.bfloat16):
    level = steps_of(rng, extent, cuts, -0.22, 0.18) if cuts else 1.0
    drawn = jax.random.normal(rng, extent, jnp.float32) * deviation * level
    return jnp.minimum(jnp.maximum(drawn, -reach), reach).astype(kind)


def setup_inputs(seed: int = 0) -> dict:
    key_of = jax.random.split(jax.random.key(seed), 7)
    return {
        "events": scatter_about(key_of[0], (TOKENS, D), 1.0, 6.0, ((0, 32), (1, 8))),
        "out_grad": scatter_about(key_of[1], (TOKENS, D), 1.0, 6.0, ((0, 32), (1, 8))),
        "w_uvqk": scatter_about(key_of[2], (D, 4 * HD), D ** -0.5, 0.09375, ((0, 8), (1, 8))),
        "w_output": scatter_about(key_of[3], (HD, D), HD ** -0.5, 0.09375, ((0, 8), (1, 8))),
        "hist_len": jax.vmap(lambda own: ragged(own, NH, TOK_OWN, HMAX, 2))(jax.random.split(key_of[4], OWNERS)).reshape((OWNERS, NH)).astype(jnp.int32),
        "token_slot": draw_token_slot(jax.random.fold_in(key_of[6], 71), 0),
    }


EPS = 1e-06

def silu_slope(inputs):
    sigma = jax.nn.sigmoid(inputs)
    return sigma * (1.0 + inputs * (1.0 - sigma))

def history_mask(lengths, width):
    history_ends = jnp.cumsum(lengths, axis=1)
    places = jnp.arange(width, dtype=jnp.int32)
    earlier = (history_ends[:, None, :] <= places[None, :, None]).astype(jnp.int32)
    starts = lax.optimization_barrier(jnp.sum(lengths[:, None, :] * earlier, axis=2))
    causal = places[None, :] <= places[:, None]
    return causal[None] & (places[None, None, :] >= starts[:, :, None])

def rounded_sum(left, right, pieces, right_axis):
    width = left.shape[1] // pieces
    total = jnp.zeros((left.shape[0], right.shape[1 - right_axis]), jnp.float32)
    for block in range(pieces):
        piece = left[:, block * width:(block + 1) * width]
        weight = lax.slice_in_dim(right, block * width, (block + 1) * width, axis=right_axis)
        term = lax.dot_general(piece, weight, (((1,), (right_axis,)), ((), ())), preferred_element_type=jnp.float32)
        total = total + lax.optimization_barrier(term.astype(jnp.bfloat16)).astype(jnp.float32)
    return total

def reference(events, out_grad, w_uvqk, w_output, hist_len, token_slot):
    scaling = HEADDIM ** (-0.5)
    x_own = jnp.zeros_like(events).at[token_slot].set(events)
    g_own = jnp.zeros_like(out_grad).at[token_slot].set(out_grad)
    preact = rounded_sum(x_own, w_uvqk, N_COL, 0)
    activated = jax.nn.silu(preact).astype(jnp.bfloat16).reshape(OWNERS, TOK_OWN, HEADS, 4, HEADDIM)
    gate_u = activated[:, :, :, 0].astype(jnp.float32)
    values = activated[:, :, :, 1].astype(jnp.float32)
    queries = activated[:, :, :, 2].astype(jnp.float32)
    keys_k = activated[:, :, :, 3].astype(jnp.float32)
    visible = history_mask(hist_len, TOK_OWN)[:, None]
    logits = jnp.einsum('bqhe,bkhe->bhqk', queries, keys_k) * scaling
    attn_probs = jnp.where(visible, jax.nn.silu(logits) / HMAX, 0.0).astype(jnp.bfloat16)
    attended = jnp.einsum('bhqk,bkhe->bqhe', attn_probs.astype(jnp.float32), values).reshape(TOKENS, HD)
    first_sum = lax.optimization_barrier(jnp.sum(attended, axis=1, keepdims=True))
    second_sum = lax.optimization_barrier(jnp.sum(attended * attended, axis=1, keepdims=True))
    mean_val = first_sum / HD
    rstd = lax.rsqrt(second_sum / HD - mean_val * mean_val + EPS)
    normed = (attended - mean_val) * rstd
    gate_flat = gate_u.reshape(TOKENS, HD)
    mixed = (normed * gate_flat).astype(jnp.bfloat16)
    y_own = (rounded_sum(mixed, w_output, N_ROW, 0) + x_own.astype(jnp.float32)).astype(jnp.bfloat16)
    contract_first = (((0,), (0,)), ((), ()))
    d_mixed = rounded_sum(g_own, w_output, N_COL, 1)
    output_grad = lax.dot_general(mixed, g_own, contract_first, preferred_element_type=jnp.float32)
    d_gate = d_mixed * normed
    d_norm = d_mixed * gate_flat
    grad_one = lax.optimization_barrier(jnp.sum(d_norm, axis=1, keepdims=True))
    grad_two = lax.optimization_barrier(jnp.sum(d_norm * normed, axis=1, keepdims=True))
    d_att = (rstd * (d_norm - grad_one / HD - normed * grad_two / HD)).astype(jnp.bfloat16)
    d_att = d_att.reshape(OWNERS, TOK_OWN, HEADS, HEADDIM).astype(jnp.float32)
    d_probs = jnp.einsum('bqhe,bkhe->bhqk', d_att, values)
    d_values = jnp.einsum('bhqk,bqhe->bkhe', attn_probs.astype(jnp.float32), d_att)
    d_logits = jnp.where(visible, d_probs * silu_slope(logits) * (scaling / HMAX), 0.0).astype(jnp.bfloat16)
    d_logits = d_logits.astype(jnp.float32)
    d_query = jnp.einsum('bhqk,bkhe->bqhe', d_logits, keys_k)
    d_keys = jnp.einsum('bhqk,bqhe->bkhe', d_logits, queries)
    d_act = jnp.stack([d_gate.reshape(OWNERS, TOK_OWN, HEADS, HEADDIM), d_values, d_query, d_keys], axis=3)
    d_pre = (d_act.reshape(TOKENS, 4 * HD) * silu_slope(preact)).astype(jnp.bfloat16)
    uvqk_grad = lax.dot_general(x_own, d_pre, contract_first, preferred_element_type=jnp.float32)
    dx_own = (rounded_sum(d_pre, w_uvqk, N_ROW, 1) + g_own.astype(jnp.float32)).astype(jnp.bfloat16)
    return (y_own[token_slot], dx_own[token_slot], uvqk_grad, output_grad)
```

```python
import jax
import jax.numpy as jnp
from jax import lax
from jax.sharding import PartitionSpec as P

HEADDIM = 128
HMAX = 64
EPS = 1e-06
LAST = (((1,), (1,)), ((), ()))
FIRST = (((0,), (0,)), ((), ()))
BF = jnp.bfloat16
F32 = jnp.float32

N_X = 4
N_Z = 8


def x_shift(value, step):
    pairs = [(c, (c // 2 + step) % N_X * 2 + c % 2) for c in range(2 * N_X)]
    return lax.ppermute(value, "col", pairs)


def z_shift(value, step):
    return lax.ppermute(value, "row", [(r, (r + step) % N_Z) for r in range(N_Z)])


def ylo_swap(value):
    return lax.ppermute(value, "col", [(c, c ^ 1) for c in range(2 * N_X)])


def dp_swap(value, bits):
    return lax.ppermute(value, "dp", [(d, d ^ bits) for d in range(4)])


def y_shift(value, step):
    pairs = []
    for d in range(4):
        for c in range(2 * N_X):
            y = (d // 2 * 2 + c % 2 + step) % 4
            pairs.append((d * 2 * N_X + c, (y // 2 * 2 + d % 2) * 2 * N_X + c // 2 * 2 + y % 2))
    return lax.ppermute(value, ("dp", "col"), pairs)


def ring_gather(block, shift, size, at):
    half = block.shape[0] // 2
    out = jnp.zeros((size,) + block.shape, block.dtype)
    out = lax.dynamic_update_slice(out, block[None], (at, 0, 0))
    up = down = block
    for step in range(1, size // 2):
        up, down = shift(up, 1), shift(down, -1)
        out = lax.dynamic_update_slice(out, up[None], ((at + size - step) % size, 0, 0))
        out = lax.dynamic_update_slice(out, down[None], ((at + step) % size, 0, 0))
    up, down = shift(up[:half], 1), shift(down[half:], -1)
    far = jnp.concatenate([up, down], axis=0)
    out = lax.dynamic_update_slice(out, far[None], ((at + size // 2) % size, 0, 0))
    return out.reshape((size * block.shape[0],) + block.shape[1:]), far


def ring_scatter(term, shift, size):
    far = term(size // 2).astype(BF)
    half = far.shape[0] // 2
    up, down = shift(far[:half], 1), shift(far[half:], -1)
    for k in range(size // 2 - 1, 0, -1):
        to_up, to_down = term(k), term(-k)
        if k == size // 2 - 1:
            to_up = jnp.concatenate([to_up[:half] + up.astype(F32), to_up[half:]], axis=0)
            to_down = jnp.concatenate([to_down[:half], to_down[half:] + down.astype(F32)], axis=0)
        else:
            to_up, to_down = to_up + up.astype(F32), to_down + down.astype(F32)
        up, down = shift(to_up.astype(BF), 1), shift(to_down.astype(BF), -1)
    return term(0) + up.astype(F32) + down.astype(F32)


def silu_slope(inputs):
    sigma = jax.nn.sigmoid(inputs)
    return sigma * (1.0 + inputs * (1.0 - sigma))


def history_mask(lengths, width):
    history_ends = jnp.cumsum(lengths, axis=1)
    places = jnp.arange(width, dtype=jnp.int32)
    earlier = (history_ends[:, None, :] <= places[None, :, None]).astype(jnp.int32)
    starts = jnp.sum(lengths[:, None, :] * earlier, axis=2)
    causal = places[None, :] <= places[:, None]
    return causal[None] & (places[None, None, :] >= starts[:, :, None])


def dot(left, right, dims=(((1,), (0,)), ((), ()))):
    return lax.dot_general(left, right, dims, preferred_element_type=F32)


def halves(array, which, axis):
    size = array.shape[axis] // 2
    return (
        lax.dynamic_slice_in_dim(array, which * size, size, axis),
        lax.dynamic_slice_in_dim(array, (1 - which) * size, size, axis),
    )


def dp_exchange(value, count):
    parts = [value[:count]]
    parts += [dp_swap(value[j * count : (j + 1) * count], j) for j in range(1, 4)]
    return jnp.concatenate(parts, axis=0)


def after(value, other):
    return lax.optimization_barrier((value, other))[0]


def local(events, out_grad, w_uvqk, w_output, hist_len, token_slot):
    n_dp, n_row, n_col = 4, N_Z, 2 * N_X
    tok_own, feat = events.shape
    send_count = tok_own // n_dp
    dp_at = lax.axis_index("dp")
    row_at = lax.axis_index("row")
    col_at = lax.axis_index("col")
    x_at, ylo_at, core_at = col_at // 2, col_at % 2, dp_at % 2
    owner_self = dp_at * n_row + row_at
    places = jnp.arange(tok_own, dtype=jnp.int32)

    events_other = ylo_swap(events)
    slots = token_slot.reshape(n_dp, n_row, tok_own)
    src_slots = lax.dynamic_index_in_dim(slots, row_at, 1, keepdims=False)
    own_slots = lax.dynamic_index_in_dim(src_slots, dp_at, 0, keepdims=False)
    send_rank = jnp.sum((own_slots[None, :] < own_slots[:, None]).astype(jnp.int32), axis=1)
    target = own_slots // (tok_own * n_row)
    send_place = (target ^ dp_at) * send_count + send_rank - target * send_count
    send_pick = (send_place[None, :] == places[:, None]).astype(BF)
    x_send = dot(send_pick, jnp.concatenate([events, events_other, out_grad], axis=1)).astype(BF)
    xg_recv = dp_exchange(x_send, send_count)
    sources = jnp.arange(n_dp, dtype=jnp.int32)
    to_self = src_slots // tok_own == owner_self
    before = jnp.sum(
        (to_self[:, None, :] & (src_slots[:, None, :] < src_slots[:, :, None])).astype(jnp.int32),
        axis=2,
    )
    recv_row = (sources ^ dp_at)[:, None] * send_count + before
    local_place = src_slots - owner_self * tok_own
    hits = to_self[:, :, None] & (recv_row[:, :, None] == places[None, None, :])
    row_place = jnp.sum(jnp.where(hits, local_place[:, :, None], 0), axis=(0, 1))
    own_pick = (row_place[None, :] == places[:, None]).astype(BF)
    x_own = dot(own_pick, xg_recv[:, : 2 * feat]).astype(BF)
    g_own = dot(own_pick, xg_recv[:, 2 * feat :]).astype(BF)

    w_keep, w_send = halves(w_uvqk, ylo_at, 1)
    w_pair = jnp.concatenate([w_keep, ylo_swap(after(w_send, xg_recv))], axis=0)

    x_panel, x_far = ring_gather(x_own, z_shift, n_row, row_at)
    g_panel, _ = ring_gather(after(g_own, x_far), z_shift, n_row, row_at)

    rows_pair = 2 * tok_own

    def x_chunk(panel, k):
        return lax.dynamic_slice_in_dim(panel, (x_at + k) % N_X * rows_pair, rows_pair, 0)

    preact = ring_scatter(lambda k: dot(x_chunk(x_panel, k), w_pair), x_shift, N_X)

    wo_keep, wo_send = halves(w_output, ylo_at, 0)
    d_other = ylo_swap(dot(g_panel, wo_send, LAST).astype(BF)).astype(F32)
    d_pair = dot(g_panel, wo_keep, LAST) + d_other
    d_mixed = ring_scatter(lambda k: x_chunk(d_pair, k), x_shift, N_X)

    heads_here = preact.shape[1] // (4 * HEADDIM)
    head_cols = heads_here * HEADDIM
    total_width = head_cols * n_row * 2
    scaling = HEADDIM ** (-0.5)
    lengths = lax.dynamic_slice_in_dim(hist_len, dp_at * n_row + x_at * 2, 2, 0)
    visible = history_mask(lengths, tok_own)[:, None]
    activated = jax.nn.silu(preact).astype(BF).reshape(2, tok_own, heads_here, 4, HEADDIM)
    gate_u = activated[:, :, :, 0]
    values = activated[:, :, :, 1]
    queries = activated[:, :, :, 2]
    keys_k = activated[:, :, :, 3]
    logits = jnp.einsum("bqhe,bkhe->bhqk", queries, keys_k, preferred_element_type=F32) * scaling
    attn_probs = jnp.where(visible, jax.nn.silu(logits) / HMAX, 0.0).astype(BF)
    attended = jnp.einsum(
        "bhqk,bkhe->bqhe", attn_probs, values, preferred_element_type=F32
    ).reshape(rows_pair, head_cols)
    gate_flat = gate_u.reshape(rows_pair, head_cols).astype(F32)
    d_norm = d_mixed * gate_flat
    sums = jnp.stack(
        [
            jnp.sum(attended, axis=1),
            jnp.sum(attended * attended, axis=1),
            jnp.sum(d_norm, axis=1),
            jnp.sum(d_norm * attended, axis=1),
        ],
        axis=0,
    )
    sums = sums + ylo_swap(sums)
    sums = sums + sum(z_shift(sums, step) for step in range(1, n_row))
    means = sums / total_width
    mean_val, second, grad_one, grad_att = [means[i][:, None] for i in range(4)]
    rstd = lax.rsqrt(second - mean_val * mean_val + EPS)
    grad_two = (grad_att - mean_val * grad_one) * rstd
    normed = (attended - mean_val) * rstd
    mixed = (normed * gate_flat).astype(BF)
    d_gate = d_mixed * normed
    d_att = (rstd * (d_norm - grad_one - normed * grad_two)).astype(BF)
    d_att = d_att.reshape(2, tok_own, heads_here, HEADDIM)
    d_probs = jnp.einsum("bqhe,bkhe->bhqk", d_att, values, preferred_element_type=F32)
    d_values = jnp.einsum("bhqk,bqhe->bkhe", attn_probs, d_att, preferred_element_type=F32)
    d_logits = jnp.where(visible, d_probs * silu_slope(logits) * (scaling / HMAX), 0.0).astype(BF)
    d_query = jnp.einsum("bhqk,bkhe->bqhe", d_logits, keys_k, preferred_element_type=F32)
    d_keys = jnp.einsum("bhqk,bqhe->bkhe", d_logits, queries, preferred_element_type=F32)
    d_act = jnp.stack(
        [d_gate.reshape(2, tok_own, heads_here, HEADDIM), d_values, d_query, d_keys], axis=3
    )
    d_pre = (d_act.reshape(rows_pair, 4 * head_cols) * silu_slope(preact)).astype(BF)

    mixed_here, _ = ring_gather(mixed, x_shift, N_X, x_at)
    mixed_there = ylo_swap(mixed_here)
    mixed_all = jnp.where(
        ylo_at == 0,
        jnp.concatenate([mixed_here, mixed_there], axis=1),
        jnp.concatenate([mixed_there, mixed_here], axis=1),
    )
    d_pre_all, _ = ring_gather(d_pre, x_shift, N_X, x_at)

    def z_chunk(panel, k):
        return lax.dynamic_slice_in_dim(panel, (row_at + k) % n_row * tok_own, tok_own, 0)

    out_rows = ring_scatter(lambda k: dot(z_chunk(mixed_all, k), w_output), z_shift, n_row)
    y_own = (out_rows + x_own[:, :feat].astype(F32)).astype(BF)
    y_back = dot(own_pick, y_own, FIRST).astype(BF)
    y_home = dp_exchange(y_back, send_count)
    layer_out = dot(send_pick, y_home, FIRST).astype(BF)

    dx_rows = ring_scatter(lambda k: dot(z_chunk(d_pre_all, k), w_pair, LAST), z_shift, n_row)
    dx_other = ylo_swap(dx_rows[:, feat:].astype(BF)).astype(F32)
    dx_own = (dx_rows[:, :feat] + dx_other + g_own.astype(F32)).astype(BF)
    dx_back = dot(own_pick, dx_own, FIRST).astype(BF)
    dx_home = dp_exchange(dx_back, send_count)
    event_grad = dot(send_pick, dx_home, FIRST).astype(BF)

    def opposite(value):
        half = value.shape[0] // 2
        up = y_shift(y_shift(value[:half], 1), 1)
        down = y_shift(y_shift(value[half:], -1), -1)
        return jnp.concatenate([up, down], axis=0).astype(F32)

    g_keep, g_send = halves(g_panel, core_at, 1)
    og_sum = dot(mixed_all, g_keep, FIRST) + dp_swap(
        dot(mixed_all, g_send, FIRST).astype(BF), 1
    ).astype(F32)
    og_half = (og_sum + opposite(og_sum.astype(BF))).astype(BF)
    og_there = dp_swap(og_half, 1)
    output_grad = jnp.where(
        core_at == 0,
        jnp.concatenate([og_half, og_there], axis=1),
        jnp.concatenate([og_there, og_half], axis=1),
    ).astype(F32)

    d_keep, d_send = halves(d_pre_all, core_at, 1)
    ug_sum = dot(x_panel, d_keep, FIRST) + dp_swap(
        dot(x_panel, d_send, FIRST).astype(BF), 1
    ).astype(F32)
    ug_cross = ug_sum[feat:].astype(BF)
    ug_cross = y_shift(ug_cross, 1).astype(F32) + y_shift(ug_cross, -1).astype(F32)
    ug_stay = ug_sum[:feat] + opposite(ug_sum[:feat].astype(BF))
    ug_half = jnp.stack([ug_stay.astype(BF), ug_cross.astype(BF)], axis=1)
    ug_there = dp_swap(ug_half, 1)
    ug = jnp.where(
        core_at == 0,
        jnp.stack([ug_half, ug_there], axis=2),
        jnp.stack([ug_there, ug_half], axis=2),
    )
    ug = jnp.where(ylo_at == 0, ug, ug[:, ::-1])
    uvqk_grad = ug.reshape(feat, w_uvqk.shape[1]).astype(F32)
    return (layer_out, event_grad, uvqk_grad, output_grad)


def solution(mesh):
    in_specs = (
        P(("dp", "row"), "col"),
        P(("dp", "row"), "col"),
        P("col", "row"),
        P("row", "col"),
        P(),
        P(),
    )
    out_specs = (P(("dp", "row"), "col"), P(("dp", "row"), "col"), P("col", "row"), P("row", "col"))
    return jax.shard_map(local, mesh=mesh, in_specs=in_specs, out_specs=out_specs, check_vma=False)
```

```python
import jax
import jax.numpy as jnp
from jax import lax
from jax.experimental import pallas as pl
from jax.experimental.pallas import tpu as pltpu
from jax.sharding import PartitionSpec as P

HEADDIM = 128
HMAX = 64
EPS = 1e-06
LAST = (((1,), (1,)), ((), ()))
FIRST = (((0,), (0,)), ((), ()))
BF = jnp.bfloat16
F32 = jnp.float32

N_X = 4
N_Z = 8


def x_shift(value, step):
    pairs = [(c, (c // 2 + step) % N_X * 2 + c % 2) for c in range(2 * N_X)]
    return lax.ppermute(value, "col", pairs)


def z_shift(value, step):
    return lax.ppermute(value, "row", [(r, (r + step) % N_Z) for r in range(N_Z)])


def ylo_swap(value):
    return lax.ppermute(value, "col", [(c, c ^ 1) for c in range(2 * N_X)])


def dp_swap(value, bits):
    return lax.ppermute(value, "dp", [(d, d ^ bits) for d in range(4)])


def y_shift(value, step):
    pairs = []
    for d in range(4):
        for c in range(2 * N_X):
            y = (d // 2 * 2 + c % 2 + step) % 4
            pairs.append((d * 2 * N_X + c, (y // 2 * 2 + d % 2) * 2 * N_X + c // 2 * 2 + y % 2))
    return lax.ppermute(value, ("dp", "col"), pairs)


def ring_gather(block, shift, size, at):
    half = block.shape[0] // 2
    out = jnp.zeros((size,) + block.shape, block.dtype)
    out = lax.dynamic_update_slice(out, block[None], (at, 0, 0))
    up = down = block
    for step in range(1, size // 2):
        up, down = shift(up, 1), shift(down, -1)
        out = lax.dynamic_update_slice(out, up[None], ((at + size - step) % size, 0, 0))
        out = lax.dynamic_update_slice(out, down[None], ((at + step) % size, 0, 0))
    up, down = shift(up[:half], 1), shift(down[half:], -1)
    far = jnp.concatenate([up, down], axis=0)
    out = lax.dynamic_update_slice(out, far[None], ((at + size // 2) % size, 0, 0))
    return out.reshape((size * block.shape[0],) + block.shape[1:]), far


def ring_scatter(term, shift, size):
    far = term(size // 2).astype(BF)
    half = far.shape[0] // 2
    up, down = shift(far[:half], 1), shift(far[half:], -1)
    for k in range(size // 2 - 1, 0, -1):
        to_up, to_down = term(k), term(-k)
        if k == size // 2 - 1:
            to_up = jnp.concatenate([to_up[:half] + up.astype(F32), to_up[half:]], axis=0)
            to_down = jnp.concatenate([to_down[:half], to_down[half:] + down.astype(F32)], axis=0)
        else:
            to_up, to_down = to_up + up.astype(F32), to_down + down.astype(F32)
        up, down = shift(to_up.astype(BF), 1), shift(to_down.astype(BF), -1)
    return term(0) + up.astype(F32) + down.astype(F32)


def silu_slope(inputs):
    sigma = jax.nn.sigmoid(inputs)
    return sigma * (1.0 + inputs * (1.0 - sigma))


def history_starts(lengths, width):
    history_ends = jnp.cumsum(lengths, axis=1)
    places = jnp.arange(width, dtype=jnp.int32)
    earlier = (history_ends[:, None, :] <= places[None, :, None]).astype(jnp.int32)
    return jnp.sum(lengths[:, None, :] * earlier, axis=2)


def dot(left, right, dims=(((1,), (0,)), ((), ())), precision=None):
    return lax.dot_general(left, right, dims, precision=precision, preferred_element_type=F32)


def forward_kernel(starts_ref, pre_ref, dmix_ref, pre_out, act_out, logit_out, prob_out, att_out, dmix_out, sum_out):
    n_part, tok, width = pre_ref.shape
    heads = width // (4 * HEADDIM)
    pre = pre_ref[0].astype(F32)
    dmix = dmix_ref[0].astype(F32)
    for part in range(1, n_part):
        pre = pre + pre_ref[part].astype(F32)
        dmix = dmix + dmix_ref[part].astype(F32)
    pre_out[...] = pre
    dmix_out[...] = dmix
    act = (pre / (1.0 + jnp.exp(-pre))).astype(BF)
    act_out[...] = act
    query = lax.broadcasted_iota(jnp.int32, (tok, tok), 0)
    key = lax.broadcasted_iota(jnp.int32, (tok, tok), 1)
    visible = (key <= query) & (key >= starts_ref[...])
    line = lax.broadcasted_iota(jnp.int32, (8, HEADDIM), 0)
    sums = jnp.zeros((8, tok), F32)
    for head in range(heads):
        at = head * 4 * HEADDIM
        gate, value, quer, keyk = [act[:, at + i * HEADDIM : at + (i + 1) * HEADDIM] for i in range(4)]
        logit = dot(quer, keyk, LAST) * HEADDIM ** (-0.5)
        logit_out[head] = logit
        prob = jnp.where(visible, logit / (1.0 + jnp.exp(-logit)) * (1.0 / HMAX), 0.0).astype(BF)
        prob_out[head] = prob
        att = dot(prob, value)
        own = pl.ds(head * HEADDIM, HEADDIM)
        att_out[:, own] = att
        dnorm = dmix[:, head * HEADDIM : (head + 1) * HEADDIM] * gate.astype(F32)
        for i, term in enumerate((att, att * att, dnorm, dnorm * att)):
            sums = sums + dot((line == i).astype(F32), term, LAST, lax.Precision.HIGHEST)
    sum_out[...] = sums


def backward_kernel(total_width, sum_ref, act_ref, slope_ref, lslope_ref, prob_ref, att_ref, dmix_ref, mixed_out, dpre_out):
    tok, width = act_ref.shape
    heads = width // (4 * HEADDIM)
    means = sum_ref[0]
    for part in range(1, sum_ref.shape[0]):
        means = means + sum_ref[part]
    means = means * (1.0 / total_width)
    row = lax.broadcasted_iota(jnp.int32, (tok, tok), 0)
    col = lax.broadcasted_iota(jnp.int32, (tok, tok), 1)
    cols = dot((row == col).astype(F32), means, LAST, lax.Precision.HIGHEST)
    mean, second, grad_one, grad_att = [cols[:, i : i + 1] for i in range(4)]
    rstd = lax.rsqrt(second - mean * mean + EPS)
    grad_two = (grad_att - mean * grad_one) * rstd
    for head in range(heads):
        at = head * 4 * HEADDIM
        gate, value, quer, keyk = [act_ref[:, at + i * HEADDIM : at + (i + 1) * HEADDIM] for i in range(4)]
        own = pl.ds(head * HEADDIM, HEADDIM)
        normed = (att_ref[:, own] - mean) * rstd
        dmix = dmix_ref[:, own]
        gate = gate.astype(F32)
        mixed_out[:, own] = (normed * gate).astype(BF)
        datt = (rstd * (dmix * gate - grad_one - normed * grad_two)).astype(BF)
        dvalue = dot(prob_ref[head], datt, FIRST)
        dlogit = (dot(datt, value, LAST) * lslope_ref[head]).astype(BF)
        dquer = dot(dlogit, keyk)
        dkey = dot(dlogit, quer, FIRST)
        for i, term in enumerate((dmix * normed, dvalue, dquer, dkey)):
            place = pl.ds(at + i * HEADDIM, HEADDIM)
            dpre_out[:, place] = (term * slope_ref[:, place]).astype(BF)


def attention_forward(starts, pre_parts, dmix_parts, tok):
    n_part, rows, width = pre_parts.shape
    heads = width // (4 * HEADDIM)
    head_cols = heads * HEADDIM
    owners = rows // tok
    square = lambda kind: jax.ShapeDtypeStruct((owners, heads, tok, tok), kind)
    square_spec = pl.BlockSpec((None, heads, tok, tok), lambda b: (b, 0, 0, 0))
    wide_spec = pl.BlockSpec((tok, width), lambda b: (b, 0))
    thin_spec = pl.BlockSpec((tok, head_cols), lambda b: (b, 0))
    return pl.pallas_call(
        forward_kernel,
        grid=(owners,),
        in_specs=[
            pl.BlockSpec((tok, 1), lambda b: (b, 0)),
            pl.BlockSpec((n_part, tok, width), lambda b: (0, b, 0)),
            pl.BlockSpec((n_part, tok, head_cols), lambda b: (0, b, 0)),
        ],
        out_specs=[wide_spec, wide_spec, square_spec, square_spec, thin_spec, thin_spec, pl.BlockSpec((8, tok), lambda b: (0, b))],
        out_shape=[
            jax.ShapeDtypeStruct((rows, width), F32),
            jax.ShapeDtypeStruct((rows, width), BF),
            square(F32),
            square(BF),
            jax.ShapeDtypeStruct((rows, head_cols), F32),
            jax.ShapeDtypeStruct((rows, head_cols), F32),
            jax.ShapeDtypeStruct((8, rows), F32),
        ],
        cost_estimate=pl.CostEstimate(flops=4 * rows * tok * head_cols, bytes_accessed=8 << 20, transcendentals=rows * width),
    )(starts, pre_parts, dmix_parts)


def attention_backward(sums, act, slope, lslope, prob, att, dmix, tok, total_width):
    rows, width = act.shape
    heads = width // (4 * HEADDIM)
    head_cols = heads * HEADDIM
    owners = rows // tok
    square_spec = pl.BlockSpec((None, heads, tok, tok), lambda b: (b, 0, 0, 0))
    wide_spec = pl.BlockSpec((tok, width), lambda b: (b, 0))
    thin_spec = pl.BlockSpec((tok, head_cols), lambda b: (b, 0))
    return pl.pallas_call(
        lambda *refs: backward_kernel(total_width, *refs),
        grid=(owners,),
        in_specs=[
            pl.BlockSpec((sums.shape[0], 8, tok), lambda b: (0, 0, b)),
            wide_spec, wide_spec, square_spec, square_spec, thin_spec, thin_spec,
        ],
        out_specs=[thin_spec, wide_spec],
        out_shape=[jax.ShapeDtypeStruct((rows, head_cols), BF), jax.ShapeDtypeStruct((rows, width), BF)],
        cost_estimate=pl.CostEstimate(flops=8 * rows * tok * head_cols, bytes_accessed=4 << 20, transcendentals=rows),
    )(sums, act, slope, lslope, prob, att, dmix)


def assemble_kernel(place_ref, mine_ref, there_ref, out_ref):
    mine = pl.program_id(0) % 2 == place_ref[0]

    @pl.when(mine)
    def _():
        out_ref[...] = mine_ref[...].astype(F32)

    @pl.when(jnp.logical_not(mine))
    def _():
        out_ref[...] = there_ref[...].astype(F32)


def assemble(place, mine, there):
    rows, width = mine.shape
    spec = pl.BlockSpec((rows, width // 2), lambda j, place: (0, (j // 2) ^ place[1]))
    return pl.pallas_call(
        assemble_kernel,
        grid_spec=pltpu.PrefetchScalarGridSpec(
            num_scalar_prefetch=1,
            grid=(4,),
            in_specs=[spec, spec],
            out_specs=pl.BlockSpec((rows, width // 2), lambda j, place: (0, j)),
        ),
        out_shape=jax.ShapeDtypeStruct((rows, 2 * width), F32),
        cost_estimate=pl.CostEstimate(flops=0, bytes_accessed=rows * width * 16, transcendentals=0),
    )(place, mine, there)


def x_exchange(blocks):
    groups = [[2 * x + y for x in range(N_X)] for y in range(2)]
    return lax.all_to_all(blocks, "col", 0, 0, axis_index_groups=groups, tiled=True)


def head_groups_gather(value):
    groups = [[r * 2 * N_X + 2 * x + y for r in range(N_Z) for y in range(2)] for x in range(N_X)]
    copies = jnp.broadcast_to(value[None], (2 * N_Z,) + value.shape)
    return lax.all_to_all(copies, ("row", "col"), 0, 0, axis_index_groups=groups, tiled=True)


def halves(array, which, axis):
    size = array.shape[axis] // 2
    return (
        lax.dynamic_slice_in_dim(array, which * size, size, axis),
        lax.dynamic_slice_in_dim(array, (1 - which) * size, size, axis),
    )


def dp_exchange(value, count):
    parts = [value[:count]]
    parts += [dp_swap(value[j * count : (j + 1) * count], j) for j in range(1, 4)]
    return jnp.concatenate(parts, axis=0)


def after(value, other):
    return lax.optimization_barrier((value, other))[0]


def local(events, out_grad, w_uvqk, w_output, hist_len, token_slot):
    n_dp, n_row, n_col = 4, N_Z, 2 * N_X
    tok_own, feat = events.shape
    send_count = tok_own // n_dp
    dp_at = lax.axis_index("dp")
    row_at = lax.axis_index("row")
    col_at = lax.axis_index("col")
    x_at, ylo_at, core_at = col_at // 2, col_at % 2, dp_at % 2
    owner_self = dp_at * n_row + row_at
    places = jnp.arange(tok_own, dtype=jnp.int32)

    events_other = ylo_swap(events)
    slots = token_slot.reshape(n_dp, n_row, tok_own)
    src_slots = lax.dynamic_index_in_dim(slots, row_at, 1, keepdims=False)
    own_slots = lax.dynamic_index_in_dim(src_slots, dp_at, 0, keepdims=False)
    send_rank = jnp.sum((own_slots[None, :] < own_slots[:, None]).astype(jnp.int32), axis=1)
    target = own_slots // (tok_own * n_row)
    send_place = (target ^ dp_at) * send_count + send_rank - target * send_count
    send_pick = (send_place[None, :] == places[:, None]).astype(BF)
    x_send = dot(send_pick, jnp.concatenate([events, events_other, out_grad], axis=1)).astype(BF)
    xg_recv = dp_exchange(x_send, send_count)
    sources = jnp.arange(n_dp, dtype=jnp.int32)
    to_self = src_slots // tok_own == owner_self
    before = jnp.sum(
        (to_self[:, None, :] & (src_slots[:, None, :] < src_slots[:, :, None])).astype(jnp.int32),
        axis=2,
    )
    recv_row = (sources ^ dp_at)[:, None] * send_count + before
    local_place = src_slots - owner_self * tok_own
    hits = to_self[:, :, None] & (recv_row[:, :, None] == places[None, None, :])
    row_place = jnp.sum(jnp.where(hits, local_place[:, :, None], 0), axis=(0, 1))
    own_pick = (row_place[None, :] == places[:, None]).astype(BF)
    x_own = dot(own_pick, xg_recv[:, : 2 * feat]).astype(BF)
    g_own = dot(own_pick, xg_recv[:, 2 * feat :]).astype(BF)

    w_keep, w_send = halves(w_uvqk, ylo_at, 1)
    w_pair = jnp.concatenate([w_keep, ylo_swap(after(w_send, xg_recv))], axis=0)

    g_panel = lax.all_gather(g_own, "row", axis=0, tiled=True)
    x_panel, _ = ring_gather(x_own, z_shift, n_row, row_at)

    rows_pair = 2 * tok_own
    pre_parts = x_exchange(dot(x_panel, w_pair).astype(BF).reshape(N_X, rows_pair, -1))

    wo_keep, wo_send = halves(w_output, ylo_at, 0)
    d_other = ylo_swap(dot(g_panel, wo_send, LAST).astype(BF)).astype(F32)
    d_pair = (dot(g_panel, wo_keep, LAST) + d_other).astype(BF)
    dmix_parts = x_exchange(d_pair.reshape(N_X, rows_pair, -1))

    lengths = lax.dynamic_slice_in_dim(hist_len, dp_at * n_row + x_at * 2, 2, 0)
    starts = history_starts(lengths, tok_own).reshape(rows_pair, 1)
    preact, act, logits, probs, att, d_mixed, sums = attention_forward(
        starts, pre_parts, dmix_parts, tok_own
    )
    sums = head_groups_gather(sums)
    slope = silu_slope(preact)
    keys = jnp.arange(tok_own, dtype=jnp.int32)
    visible = (keys[None, None, :] >= starts.reshape(2, tok_own, 1)) & (
        keys[None, None, :] <= keys[None, :, None]
    )
    lslope = jnp.where(
        visible[:, None], silu_slope(logits) * (HEADDIM ** (-0.5) / HMAX), 0.0
    )
    total_width = att.shape[1] * n_row * 2
    mixed, d_pre = attention_backward(
        sums, act, slope, lslope, probs, att, d_mixed, tok_own, total_width
    )

    mixed_here = x_exchange(jnp.broadcast_to(mixed[None], (N_X,) + mixed.shape))
    mixed_here = mixed_here.reshape(n_row * tok_own, mixed.shape[1])
    mixed_there = ylo_swap(mixed_here)
    mixed_all = jnp.where(
        ylo_at == 0,
        jnp.concatenate([mixed_here, mixed_there], axis=1),
        jnp.concatenate([mixed_there, mixed_here], axis=1),
    )
    d_pre_all, _ = ring_gather(d_pre, x_shift, N_X, x_at)

    def z_chunk(panel, k):
        return lax.dynamic_slice_in_dim(panel, (row_at + k) % n_row * tok_own, tok_own, 0)

    out_rows = ring_scatter(lambda k: dot(z_chunk(mixed_all, k), w_output), z_shift, n_row)
    y_own = (out_rows + x_own[:, :feat].astype(F32)).astype(BF)
    y_back = dot(own_pick, y_own, FIRST).astype(BF)
    y_home = dp_exchange(y_back, send_count)
    layer_out = dot(send_pick, y_home, FIRST).astype(BF)

    dx_rows = ring_scatter(lambda k: dot(z_chunk(d_pre_all, k), w_pair, LAST), z_shift, n_row)
    dx_other = ylo_swap(dx_rows[:, feat:].astype(BF)).astype(F32)
    dx_own = (dx_rows[:, :feat] + dx_other + g_own.astype(F32)).astype(BF)
    dx_back = dot(own_pick, dx_own, FIRST).astype(BF)
    dx_home = dp_exchange(dx_back, send_count)
    event_grad = dot(send_pick, dx_home, FIRST).astype(BF)

    g_keep, g_send = halves(g_panel, core_at, 1)
    mixed_t = lax.optimization_barrier(mixed_all.T)
    og_sum = dot(mixed_t, g_keep) + dp_swap(dot(mixed_t, g_send).astype(BF), 1).astype(F32)
    half = og_sum.shape[0] // 2
    og_low, og_high = og_sum[:half].astype(BF), og_sum[half:].astype(BF)
    og_low, og_high = y_shift(y_shift(og_low, -1), -1), y_shift(y_shift(og_high, 1), 1)
    og_half = (og_sum + jnp.concatenate([og_low, og_high], axis=0).astype(F32)).astype(BF)
    og_there = dp_swap(og_half, 1)
    output_grad = jnp.where(
        core_at == 0,
        jnp.concatenate([og_half, og_there], axis=1),
        jnp.concatenate([og_there, og_half], axis=1),
    ).astype(F32)

    half = feat // 2
    x_t = x_panel.T
    x_t = jnp.concatenate([x_t[:half], x_t[feat:], x_t[half:feat]], axis=0)
    x_t = lax.optimization_barrier(x_t)
    d_keep, d_send = halves(d_pre_all, core_at, 1)
    ug_sum = dot(x_t, d_keep) + dp_swap(dot(x_t, d_send).astype(BF), 1).astype(F32)
    ug_bf = ug_sum.astype(BF)
    up, down = y_shift(ug_bf[half:], 1), y_shift(ug_bf[: half + feat], -1)
    ug_cross = up[:feat].astype(F32) + down[half:].astype(F32)
    far_low, far_high = y_shift(down[:half], -1), y_shift(up[feat:], 1)
    ug_stay = jnp.concatenate(
        [ug_sum[:half] + far_low.astype(F32), ug_sum[half + feat :] + far_high.astype(F32)], axis=0
    )
    ug_half = jnp.concatenate([ug_stay.astype(BF), ug_cross.astype(BF)], axis=1)
    ug_there = dp_swap(ug_half, 1)
    uvqk_grad = assemble(jnp.stack([core_at, ylo_at]).astype(jnp.int32), ug_half, ug_there)
    return (layer_out, event_grad, uvqk_grad, output_grad)


def solution(mesh):
    in_specs = (
        P(("dp", "row"), "col"),
        P(("dp", "row"), "col"),
        P("col", "row"),
        P("row", "col"),
        P(),
        P(),
    )
    out_specs = (P(("dp", "row"), "col"), P(("dp", "row"), "col"), P("col", "row"), P("row", "col"))
    return jax.shard_map(local, mesh=mesh, in_specs=in_specs, out_specs=out_specs, check_vma=False)
```

```python
import jax
import jax.numpy as jnp
from jax import lax
from jax.experimental import pallas as pl
from jax.experimental.pallas import tpu as pltpu
from jax.sharding import PartitionSpec as P

HEADDIM = 128
HMAX = 64
EPS = 1e-06
LAST = (((1,), (1,)), ((), ()))
FIRST = (((0,), (0,)), ((), ()))
BF = jnp.bfloat16
F32 = jnp.float32

N_X = 4
N_Z = 8


def x_shift(value, step):
    pairs = [(c, (c // 2 + step) % N_X * 2 + c % 2) for c in range(2 * N_X)]
    return lax.ppermute(value, "col", pairs)


def z_shift(value, step):
    return lax.ppermute(value, "row", [(r, (r + step) % N_Z) for r in range(N_Z)])


def ylo_swap(value):
    return lax.ppermute(value, "col", [(c, c ^ 1) for c in range(2 * N_X)])


def dp_swap(value, bits):
    return lax.ppermute(value, "dp", [(d, d ^ bits) for d in range(4)])


def y_shift(value, step):
    pairs = []
    for d in range(4):
        for c in range(2 * N_X):
            y = (d // 2 * 2 + c % 2 + step) % 4
            pairs.append((d * 2 * N_X + c, (y // 2 * 2 + d % 2) * 2 * N_X + c // 2 * 2 + y % 2))
    return lax.ppermute(value, ("dp", "col"), pairs)


def ring_gather(block, shift, size, at, panels, cuts):
    rows = block.shape[0]
    half = rows // 2

    def put(panels, piece, place, offset=0):
        start = place % size * rows + offset
        return [
            lax.dynamic_update_slice(panel, piece[:, low:high], (start, 0))
            for panel, (low, high) in zip(panels, cuts)
        ]

    panels = put(panels, block, at)
    up = down = block
    for step in range(1, size // 2):
        up, down = shift(up, 1), shift(down, -1)
        panels = put(panels, up, at + size - step)
        panels = put(panels, down, at + step)
    up, down = shift(up[:half], 1), shift(down[half:], -1)
    panels = put(panels, up, at + size // 2)
    return put(panels, down, at + size // 2, half)


def silu_slope(inputs):
    sigma = jax.nn.sigmoid(inputs)
    return sigma * (1.0 + inputs * (1.0 - sigma))


def history_starts(lengths, width):
    history_ends = jnp.cumsum(lengths, axis=1)
    places = jnp.arange(width, dtype=jnp.int32)
    earlier = (history_ends[:, None, :] <= places[None, :, None]).astype(jnp.int32)
    return jnp.sum(lengths[:, None, :] * earlier, axis=2)


def dot(left, right, dims=(((1,), (0,)), ((), ())), precision=None):
    return lax.dot_general(left, right, dims, precision=precision, preferred_element_type=F32)


def forward_kernel(starts_ref, pre_ref, *refs):
    n_part, tok, width = pre_ref.shape
    heads = width // (4 * HEADDIM)
    dmix_refs, outs = refs[:n_part], refs[n_part:]
    pre_out, act_out, logit_out, prob_out, att_out, dmix_out, sum_out = outs
    pre = pre_ref[0].astype(F32)
    dmix = dmix_refs[0][...].astype(F32)
    for part in range(1, n_part):
        pre = pre + pre_ref[part].astype(F32)
        dmix = dmix + dmix_refs[part][...].astype(F32)
    pre_out[...] = pre
    dmix_out[...] = dmix
    act = (pre / (1.0 + jnp.exp(-pre))).astype(BF)
    act_out[...] = act
    query = lax.broadcasted_iota(jnp.int32, (tok, tok), 0)
    key = lax.broadcasted_iota(jnp.int32, (tok, tok), 1)
    visible = (key <= query) & (key >= starts_ref[...])
    totals = [0.0, 0.0, 0.0, 0.0]
    for head in range(heads):
        at = head * 4 * HEADDIM
        gate, value, quer, keyk = [act[:, at + i * HEADDIM : at + (i + 1) * HEADDIM] for i in range(4)]
        logit = dot(quer, keyk, LAST) * HEADDIM ** (-0.5)
        logit_out[head] = logit
        prob = jnp.where(visible, logit / (1.0 + jnp.exp(-logit)) * (1.0 / HMAX), 0.0).astype(BF)
        prob_out[head] = prob
        att = dot(prob, value)
        own = pl.ds(head * HEADDIM, HEADDIM)
        att_out[:, own] = att
        dnorm = dmix[:, head * HEADDIM : (head + 1) * HEADDIM] * gate.astype(F32)
        for i, term in enumerate((att, att * att, dnorm, dnorm * att)):
            totals[i] = totals[i] + term
    table = jnp.zeros((tok, tok), F32)
    for i, total in enumerate(totals):
        table = jnp.where(key == i, jnp.sum(total, axis=1, keepdims=True), table)
    sums = table.T[:8]
    for copy in range(sum_out.shape[0]):
        sum_out[copy] = sums


def backward_kernel(total_width, sum_ref, act_ref, slope_ref, lslope_ref, prob_ref, att_ref, dmix_ref, mixed_out, dpre_out):
    tok, width = act_ref.shape
    heads = width // (4 * HEADDIM)
    means = sum_ref[0]
    for part in range(1, sum_ref.shape[0]):
        means = means + sum_ref[part]
    means = means * (1.0 / total_width)
    row = lax.broadcasted_iota(jnp.int32, (tok, tok), 0)
    col = lax.broadcasted_iota(jnp.int32, (tok, tok), 1)
    cols = dot((row == col).astype(F32), means, LAST, lax.Precision.HIGHEST)
    mean, second, grad_one, grad_att = [cols[:, i : i + 1] for i in range(4)]
    rstd = lax.rsqrt(second - mean * mean + EPS)
    grad_two = (grad_att - mean * grad_one) * rstd
    for head in range(heads):
        at = head * 4 * HEADDIM
        gate, value, quer, keyk = [act_ref[:, at + i * HEADDIM : at + (i + 1) * HEADDIM] for i in range(4)]
        own = pl.ds(head * HEADDIM, HEADDIM)
        normed = (att_ref[:, own] - mean) * rstd
        dmix = dmix_ref[:, own]
        gate = gate.astype(F32)
        mixed = (normed * gate).astype(BF)
        for copy in range(mixed_out.shape[0]):
            mixed_out[copy, :, own] = mixed
        datt = (rstd * (dmix * gate - grad_one - normed * grad_two)).astype(BF)
        dvalue = dot(prob_ref[head], datt, FIRST)
        dlogit = (dot(datt, value, LAST) * lslope_ref[head]).astype(BF)
        dquer = dot(dlogit, keyk)
        dkey = dot(dlogit, quer, FIRST)
        for i, term in enumerate((dmix * normed, dvalue, dquer, dkey)):
            place = pl.ds(at + i * HEADDIM, HEADDIM)
            dpre_out[:, place] = (term * slope_ref[:, place]).astype(BF)


def attention_forward(starts, pre_parts, dmix_parts, tok, copies):
    n_part, rows, width = pre_parts.shape
    heads = width // (4 * HEADDIM)
    head_cols = heads * HEADDIM
    owners = rows // tok
    square = lambda kind: jax.ShapeDtypeStruct((owners, heads, tok, tok), kind)
    square_spec = pl.BlockSpec((None, heads, tok, tok), lambda b: (b, 0, 0, 0))
    wide_spec = pl.BlockSpec((tok, width), lambda b: (b, 0))
    thin_spec = pl.BlockSpec((tok, head_cols), lambda b: (b, 0))
    return pl.pallas_call(
        forward_kernel,
        grid=(owners,),
        in_specs=[
            pl.BlockSpec((tok, 1), lambda b: (b, 0)),
            pl.BlockSpec((n_part, tok, width), lambda b: (0, b, 0)),
        ]
        + [thin_spec] * n_part,
        out_specs=[wide_spec, wide_spec, square_spec, square_spec, thin_spec, thin_spec, pl.BlockSpec((copies, 8, tok), lambda b: (0, 0, b))],
        out_shape=[
            jax.ShapeDtypeStruct((rows, width), F32),
            jax.ShapeDtypeStruct((rows, width), BF),
            square(F32),
            square(BF),
            jax.ShapeDtypeStruct((rows, head_cols), F32),
            jax.ShapeDtypeStruct((rows, head_cols), F32),
            jax.ShapeDtypeStruct((copies, 8, rows), F32),
        ],
        cost_estimate=pl.CostEstimate(flops=4 * rows * tok * head_cols, bytes_accessed=8 << 20, transcendentals=rows * width),
    )(starts, pre_parts, *dmix_parts)


def attention_backward(sums, act, slope, lslope, prob, att, dmix, tok, total_width):
    rows, width = act.shape
    heads = width // (4 * HEADDIM)
    head_cols = heads * HEADDIM
    owners = rows // tok
    square_spec = pl.BlockSpec((None, heads, tok, tok), lambda b: (b, 0, 0, 0))
    wide_spec = pl.BlockSpec((tok, width), lambda b: (b, 0))
    thin_spec = pl.BlockSpec((tok, head_cols), lambda b: (b, 0))
    return pl.pallas_call(
        lambda *refs: backward_kernel(total_width, *refs),
        grid=(owners,),
        in_specs=[
            pl.BlockSpec((sums.shape[0], 8, tok), lambda b: (0, 0, b)),
            wide_spec, wide_spec, square_spec, square_spec, thin_spec, thin_spec,
        ],
        out_specs=[pl.BlockSpec((N_X, tok, head_cols), lambda b: (0, b, 0)), wide_spec],
        out_shape=[
            jax.ShapeDtypeStruct((N_X, rows, head_cols), BF),
            jax.ShapeDtypeStruct((rows, width), BF),
        ],
        cost_estimate=pl.CostEstimate(flops=8 * rows * tok * head_cols, bytes_accessed=4 << 20, transcendentals=rows),
    )(sums, act, slope, lslope, prob, att, dmix)


def widen_kernel(place_ref, half_ref, *refs):
    refs[-1][...] = half_ref[...].astype(F32)


def place_halves(place, value, into=None):
    rows, width = value.shape
    extra = [] if into is None else [into]
    return pl.pallas_call(
        widen_kernel,
        grid_spec=pltpu.PrefetchScalarGridSpec(
            num_scalar_prefetch=1,
            grid=(2,),
            in_specs=[pl.BlockSpec((rows, width // 2), lambda h, place: (0, h ^ place[1]))]
            + [pl.BlockSpec(memory_space=pl.ANY)] * len(extra),
            out_specs=pl.BlockSpec((rows, width // 2), lambda h, place: (0, 2 * h + place[0])),
        ),
        out_shape=jax.ShapeDtypeStruct((rows, 2 * width), F32),
        input_output_aliases={2: 0} if extra else {},
        cost_estimate=pl.CostEstimate(flops=0, bytes_accessed=rows * width * 6, transcendentals=0),
    )(place, value, *extra)


def grad_kernel(core_ref, x_ref, d_ref, *refs):
    out = refs[-1]
    grad = dot(x_ref[...], d_ref[...])
    if len(refs) == 1:
        out[...] = grad.astype(BF)
    else:
        there_ref, low_ref, high_ref = refs[:3]
        low, mid = low_ref.shape[0], grad.shape[0]
        out[:low] = low_ref[...]
        out[low : low + mid] = (grad + there_ref[...].astype(F32)).astype(BF)
        out[low + mid :] = high_ref[...]


def grad_columns(core, x_t, d_all, *more):
    depth, width = d_all.shape
    step = width // 4
    rows = x_t.shape[0] + sum(piece.shape[0] for piece in more[1:])
    return pl.pallas_call(
        grad_kernel,
        grid_spec=pltpu.PrefetchScalarGridSpec(
            num_scalar_prefetch=1,
            grid=(2,),
            in_specs=[
                pl.BlockSpec(x_t.shape, lambda i, core: (0, 0)),
                pl.BlockSpec((depth, step), lambda i, core: (0, core[0] * 2 + i)),
            ]
            + [pl.BlockSpec((piece.shape[0], step), lambda i, core: (0, i)) for piece in more],
            out_specs=pl.BlockSpec((rows, step), lambda i, core: (0, i)),
        ),
        out_shape=jax.ShapeDtypeStruct((rows, 2 * step), BF),
        compiler_params=pltpu.CompilerParams(vmem_limit_bytes=24 << 20),
        cost_estimate=pl.CostEstimate(
            flops=4 * x_t.size * step, bytes_accessed=4 << 20, transcendentals=0
        ),
    )(core, x_t, d_all, *more)


def x_exchange(blocks):
    groups = [[2 * x + y for x in range(N_X)] for y in range(2)]
    return lax.all_to_all(blocks, "col", 0, 0, axis_index_groups=groups, tiled=True)


def head_groups_gather(value):
    groups = [[r * 2 * N_X + 2 * x + y for r in range(N_Z) for y in range(2)] for x in range(N_X)]
    return lax.all_to_all(value, ("row", "col"), 0, 0, axis_index_groups=groups, tiled=True)


def halves(array, which, axis):
    size = array.shape[axis] // 2
    return (
        lax.dynamic_slice_in_dim(array, which * size, size, axis),
        lax.dynamic_slice_in_dim(array, (1 - which) * size, size, axis),
    )


def dp_exchange(value, count):
    parts = [value[:count]]
    parts += [dp_swap(value[j * count : (j + 1) * count], j) for j in range(1, 4)]
    return jnp.concatenate(parts, axis=0)


def after(value, other):
    return lax.optimization_barrier((value, other))[0]


def local(events, out_grad, w_uvqk, w_output, hist_len, token_slot):
    n_dp, n_row, n_col = 4, N_Z, 2 * N_X
    tok_own, feat = events.shape
    send_count = tok_own // n_dp
    dp_at = lax.axis_index("dp")
    row_at = lax.axis_index("row")
    col_at = lax.axis_index("col")
    x_at, ylo_at, core_at = col_at // 2, col_at % 2, dp_at % 2
    owner_self = dp_at * n_row + row_at
    places = jnp.arange(tok_own, dtype=jnp.int32)

    events_other = ylo_swap(events)
    slots = token_slot.reshape(n_dp, n_row, tok_own)
    src_slots = lax.dynamic_index_in_dim(slots, row_at, 1, keepdims=False)
    own_slots = lax.dynamic_index_in_dim(src_slots, dp_at, 0, keepdims=False)
    send_rank = jnp.sum((own_slots[None, :] < own_slots[:, None]).astype(jnp.int32), axis=1)
    target = own_slots // (tok_own * n_row)
    send_place = (target ^ dp_at) * send_count + send_rank - target * send_count
    send_pick = (send_place[None, :] == places[:, None]).astype(BF)
    x_send = dot(send_pick, jnp.concatenate([events, events_other, out_grad], axis=1)).astype(BF)
    xg_recv = dp_exchange(x_send, send_count)
    sources = jnp.arange(n_dp, dtype=jnp.int32)
    to_self = src_slots // tok_own == owner_self
    before = jnp.sum(
        (to_self[:, None, :] & (src_slots[:, None, :] < src_slots[:, :, None])).astype(jnp.int32),
        axis=2,
    )
    recv_row = (sources ^ dp_at)[:, None] * send_count + before
    local_place = src_slots - owner_self * tok_own
    hits = to_self[:, :, None] & (recv_row[:, :, None] == places[None, None, :])
    row_place = jnp.sum(jnp.where(hits, local_place[:, :, None], 0), axis=(0, 1))
    own_pick = (row_place[None, :] == places[:, None]).astype(BF)
    xg_own = dot(own_pick, xg_recv).astype(BF)
    x_own, g_own = xg_own[:, :feat], xg_own[:, 2 * feat :]

    w_keep, w_send = halves(w_uvqk, ylo_at, 1)
    w_pair = jnp.concatenate([w_keep, ylo_swap(after(w_send, xg_recv))], axis=0)

    tokens = n_row * tok_own
    x_panel, g_panel = ring_gather(
        xg_own,
        z_shift,
        n_row,
        row_at,
        [jnp.zeros((tokens, 2 * feat), BF), jnp.zeros((tokens, feat), BF)],
        [(0, 2 * feat), (2 * feat, 3 * feat)],
    )
    rows_pair = 2 * tok_own

    def x_chunk(panel, k):
        return lax.dynamic_slice_in_dim(panel, (x_at + k) % N_X * rows_pair, rows_pair, 0)

    wo_keep, wo_send = halves(w_output, ylo_at, 0)
    d_send = dot(g_panel, wo_send, LAST).astype(BF)
    x_later, d_send = lax.optimization_barrier((x_panel, d_send))
    d_other = ylo_swap(d_send).astype(F32)
    pre_part = dot(x_later, w_pair).astype(BF)
    pre_parts = x_exchange(pre_part.reshape(N_X, rows_pair, -1))
    d_pair = (dot(g_panel, wo_keep, LAST) + d_other).astype(BF)
    d_pair, _ = lax.optimization_barrier((d_pair, pre_part))
    dmix_parts = [x_chunk(d_pair, 0)] + [x_shift(x_chunk(d_pair, k), k) for k in (1, -1, 2)]

    lengths = lax.dynamic_slice_in_dim(hist_len, dp_at * n_row + x_at * 2, 2, 0)
    starts = history_starts(lengths, tok_own).reshape(rows_pair, 1)
    preact, act, logits, probs, att, d_mixed, sums = attention_forward(
        starts, pre_parts, dmix_parts, tok_own, 2 * n_row
    )
    sums = head_groups_gather(sums)
    slope = silu_slope(preact)
    keys = jnp.arange(tok_own, dtype=jnp.int32)
    visible = (keys[None, None, :] >= starts.reshape(2, tok_own, 1)) & (
        keys[None, None, :] <= keys[None, :, None]
    )
    lslope = jnp.where(
        visible[:, None], silu_slope(logits) * (HEADDIM ** (-0.5) / HMAX), 0.0
    )
    total_width = att.shape[1] * n_row * 2
    mixed, d_pre = attention_backward(
        sums, act, slope, lslope, probs, att, d_mixed, tok_own, total_width
    )

    mixed_here = x_exchange(mixed).reshape(tokens, mixed.shape[2])
    (d_pre_all,) = ring_gather(
        d_pre, x_shift, N_X, x_at, [pre_parts.reshape(tokens, -1)], [(0, d_pre.shape[1])]
    )
    mixed_there = ylo_swap(mixed_here)
    mixed_all = jnp.where(
        ylo_at == 0,
        jnp.concatenate([mixed_here, mixed_there], axis=1),
        jnp.concatenate([mixed_there, mixed_here], axis=1),
    )

    def z_chunk(panel, k):
        return lax.dynamic_slice_in_dim(panel, (row_at + k) % n_row * tok_own, tok_own, 0)

    out_all = dot(mixed_all, w_output).astype(BF)
    far = jnp.concatenate(
        [dot(z_chunk(d_pre_all, 4), w_pair, LAST).astype(BF), z_chunk(out_all, 4)], axis=1
    )
    mid = far.shape[1] // 2
    up, down = z_shift(far[:, :mid], 1), z_shift(far[:, mid:], -1)

    half = feat // 2
    x_t = x_panel.T
    x_t = jnp.concatenate([x_t[:half], x_t[feat:], x_t[half:feat]], axis=0)
    x_t = lax.optimization_barrier(x_t)
    core = core_at.astype(jnp.int32)[None]
    ug_there = dp_swap(grad_columns(1 - core, x_t, after(d_pre_all, far)), 1)
    m_keep, m_send = halves(mixed_all, core_at, 1)
    og_there = dp_swap(dot(m_send.T, g_panel).astype(BF), 1)
    og_sum = dot(m_keep.T, g_panel) + og_there.astype(F32)
    og_mid = og_sum.shape[0] // 2
    og_low, og_high = og_sum[:og_mid].astype(BF), og_sum[og_mid:].astype(BF)
    grads = grad_columns(core, x_t, d_pre_all, ug_there, og_low, og_high)

    dx_all = dot(d_pre_all, w_pair, LAST).astype(BF)

    def term(k):
        return jnp.concatenate([z_chunk(dx_all, k), z_chunk(out_all, k)], axis=1).astype(F32)

    to_up, to_down = term(3), term(-3)
    to_up = jnp.concatenate([to_up[:, :mid] + up.astype(F32), to_up[:, mid:]], axis=1)
    to_down = jnp.concatenate([to_down[:, :mid], to_down[:, mid:] + down.astype(F32)], axis=1)
    up, down = z_shift(to_up.astype(BF), 1), z_shift(to_down.astype(BF), -1)
    y_up, y_down = grads[og_mid + half :], grads[: og_mid + half + feat]
    up, down = after(up, y_up), after(down, y_down)
    y_up, y_down = y_shift(y_up, 1), y_shift(y_down, -1)
    to_up, to_down = term(2) + up.astype(F32), term(-2) + down.astype(F32)
    up, down = z_shift(to_up.astype(BF), 1), z_shift(to_down.astype(BF), -1)
    to_up, to_down = term(1) + up.astype(F32), term(-1) + down.astype(F32)
    up, down = z_shift(to_up.astype(BF), 1), z_shift(to_down.astype(BF), -1)
    far_up, far_down = y_shift(y_up[feat:], 1), y_shift(y_down[: og_mid + half], -1)
    ug_cross = y_up[:feat].astype(F32) + y_down[og_mid + half :].astype(F32)
    rows = term(0) + up.astype(F32) + down.astype(F32)

    dx_other = ylo_swap(rows[:, feat : 2 * feat].astype(BF))
    ug_stay = jnp.concatenate(
        [
            grads[og_mid : og_mid + half].astype(F32) + far_down[og_mid:].astype(F32),
            grads[og_mid + half + feat : -og_mid].astype(F32) + far_up[:half].astype(F32),
        ],
        axis=0,
    )
    ug_half = jnp.concatenate([ug_stay.astype(BF), ug_cross.astype(BF)], axis=1)
    og_half = jnp.concatenate(
        [
            og_sum[:og_mid] + far_down[:og_mid].astype(F32),
            og_sum[og_mid:] + far_up[half:].astype(F32),
        ],
        axis=0,
    ).astype(BF)
    ug_there, og_there = dp_swap(ug_half, 1), dp_swap(og_half, 1)
    dx_own = (rows[:, :feat] + dx_other.astype(F32) + g_own.astype(F32)).astype(BF)
    y_own = (rows[:, 2 * feat :] + x_own.astype(F32)).astype(BF)
    back = dot(own_pick, jnp.concatenate([y_own, dx_own], axis=1), FIRST).astype(BF)
    home = dp_exchange(back, send_count)
    layer_out = dot(send_pick, home[:, :feat], FIRST).astype(BF)
    event_grad = dot(send_pick, home[:, feat:], FIRST).astype(BF)
    output_grad = jnp.where(
        core_at == 0,
        jnp.concatenate([og_half, og_there], axis=0),
        jnp.concatenate([og_there, og_half], axis=0),
    ).astype(F32)
    ylo = ylo_at.astype(jnp.int32)[None]
    uvqk_grad = place_halves(jnp.concatenate([core, ylo]), ug_half)
    uvqk_grad = place_halves(jnp.concatenate([1 - core, ylo]), ug_there, uvqk_grad)
    return (layer_out, event_grad, uvqk_grad, output_grad)


def solution(mesh):
    in_specs = (
        P(("dp", "row"), "col"),
        P(("dp", "row"), "col"),
        P("col", "row"),
        P("row", "col"),
        P(),
        P(),
    )
    out_specs = (P(("dp", "row"), "col"), P(("dp", "row"), "col"), P("col", "row"), P("row", "col"))
    return jax.shard_map(local, mesh=mesh, in_specs=in_specs, out_specs=out_specs, check_vma=False)
```

```python
import jax
import jax.numpy as jnp
from jax import lax
from jax.experimental import pallas as pl
from jax.experimental.pallas import tpu as pltpu
from jax.sharding import PartitionSpec as P

HEADDIM = 128
HMAX = 64
EPS = 1e-06
LAST = (((1,), (1,)), ((), ()))
FIRST = (((0,), (0,)), ((), ()))
BF = jnp.bfloat16
F32 = jnp.float32

N_X = 4
N_Z = 8


def x_shift(value, step):
    pairs = [(c, (c // 2 + step) % N_X * 2 + c % 2) for c in range(2 * N_X)]
    return lax.ppermute(value, "col", pairs)


def z_shift(value, step):
    return lax.ppermute(value, "row", [(r, (r + step) % N_Z) for r in range(N_Z)])


def ylo_swap(value):
    return lax.ppermute(value, "col", [(c, c ^ 1) for c in range(2 * N_X)])


def dp_swap(value, bits):
    return lax.ppermute(value, "dp", [(d, d ^ bits) for d in range(4)])


def y_shift(value, step):
    pairs = []
    for d in range(4):
        for c in range(2 * N_X):
            y = (d // 2 * 2 + c % 2 + step) % 4
            pairs.append((d * 2 * N_X + c, (y // 2 * 2 + d % 2) * 2 * N_X + c // 2 * 2 + y % 2))
    return lax.ppermute(value, ("dp", "col"), pairs)


def place_kernel(count, at_ref, *refs):
    blocks, outs = refs[:count], refs[-2:]
    cut = outs[0].shape[1]
    k = pl.program_id(0)
    for i, block in enumerate(blocks):

        @pl.when(k == i)
        def _(block=block):
            outs[0][...] = block[:, :cut]
            outs[1][...] = block[:, cut:]

    @pl.when(k == count)
    def _():
        outs[0][...] = jnp.zeros(outs[0].shape, BF)
        outs[1][...] = jnp.zeros(outs[1].shape, BF)


def place_blocks(at, blocks, cut):
    rows, width = blocks[0].shape
    size = len(blocks) + 1
    order = blocks[:4] + blocks[4:]

    def where(k, at):
        return ((at[0] + jnp.where(k < 4, k, jnp.where(k < size - 1, k + 1, 4))) % size, 0)

    return pl.pallas_call(
        lambda *refs: place_kernel(len(order), *refs),
        grid_spec=pltpu.PrefetchScalarGridSpec(
            num_scalar_prefetch=1,
            grid=(size,),
            in_specs=[pl.BlockSpec((rows, width), lambda k, at: (0, 0)) for _ in order],
            out_specs=[pl.BlockSpec((rows, cut), where), pl.BlockSpec((rows, width - cut), where)],
        ),
        out_shape=[
            jax.ShapeDtypeStruct((size * rows, cut), BF),
            jax.ShapeDtypeStruct((size * rows, width - cut), BF),
        ],
        cost_estimate=pl.CostEstimate(flops=0, bytes_accessed=2 * size * rows * width * 2, transcendentals=0),
    )(at, *order)


def place_far_kernel(at_ref, low_ref, high_ref, x_in, g_in, x_out, g_out):
    half, cut = low_ref.shape[0], x_out.shape[1]
    x_out[:half], x_out[half:] = low_ref[:, :cut], high_ref[:, :cut]
    g_out[:half], g_out[half:] = low_ref[:, cut:], high_ref[:, cut:]


def place_far(at, low, high, panels):
    rows, width = 2 * low.shape[0], low.shape[1]
    size = panels[0].shape[0] // rows
    where = lambda i, at: ((at[0] + size // 2) % size, 0)
    return pl.pallas_call(
        place_far_kernel,
        grid_spec=pltpu.PrefetchScalarGridSpec(
            num_scalar_prefetch=1,
            grid=(1,),
            in_specs=[pl.BlockSpec(low.shape, lambda i, at: (0, 0))] * 2
            + [pl.BlockSpec(memory_space=pl.ANY)] * 2,
            out_specs=[pl.BlockSpec((rows, panel.shape[1]), where) for panel in panels],
        ),
        out_shape=[jax.ShapeDtypeStruct(panel.shape, BF) for panel in panels],
        input_output_aliases={3: 0, 4: 1},
        cost_estimate=pl.CostEstimate(flops=0, bytes_accessed=4 * rows * width, transcendentals=0),
    )(at, low, high, *panels)


def product_kernel(left_ref, right_ref, out_ref):
    out_ref[...] = dot(left_ref[...], right_ref[...]).astype(BF)


def product(left, right, step=256):
    rows, depth = left.shape
    columns = right.shape[1]
    return pl.pallas_call(
        product_kernel,
        grid=(columns // step,),
        in_specs=[
            pl.BlockSpec((rows, depth), lambda i: (0, 0)),
            pl.BlockSpec((depth, step), lambda i: (0, i)),
        ],
        out_specs=pl.BlockSpec((rows, step), lambda i: (0, i)),
        out_shape=jax.ShapeDtypeStruct((rows, columns), BF),
        compiler_params=pltpu.CompilerParams(vmem_limit_bytes=24 << 20),
        cost_estimate=pl.CostEstimate(
            flops=2 * rows * depth * columns, bytes_accessed=6 << 20, transcendentals=0
        ),
    )(left, right)


def silu_slope(inputs):
    sigma = jax.nn.sigmoid(inputs)
    return sigma * (1.0 + inputs * (1.0 - sigma))


def history_starts(lengths, width):
    history_ends = jnp.cumsum(lengths, axis=1)
    places = jnp.arange(width, dtype=jnp.int32)
    earlier = (history_ends[:, None, :] <= places[None, :, None]).astype(jnp.int32)
    return jnp.sum(lengths[:, None, :] * earlier, axis=2)


def dot(left, right, dims=(((1,), (0,)), ((), ())), precision=None):
    return lax.dot_general(left, right, dims, precision=precision, preferred_element_type=F32)


def forward_kernel(starts_ref, pre_ref, *refs):
    n_part, tok, width = pre_ref.shape
    heads = width // (4 * HEADDIM)
    dmix_refs, outs = refs[:n_part], refs[n_part:]
    pre_out, act_out, logit_out, prob_out, att_out, dmix_out, sum_out = outs
    pre = pre_ref[0].astype(F32)
    dmix = dmix_refs[0][...].astype(F32)
    for part in range(1, n_part):
        pre = pre + pre_ref[part].astype(F32)
        dmix = dmix + dmix_refs[part][...].astype(F32)
    pre_out[...] = pre
    dmix_out[...] = dmix
    act = (pre / (1.0 + jnp.exp(-pre))).astype(BF)
    act_out[...] = act
    query = lax.broadcasted_iota(jnp.int32, (tok, tok), 0)
    key = lax.broadcasted_iota(jnp.int32, (tok, tok), 1)
    visible = (key <= query) & (key >= starts_ref[...])
    totals = [0.0, 0.0, 0.0, 0.0]
    for head in range(heads):
        at = head * 4 * HEADDIM
        gate, value, quer, keyk = [act[:, at + i * HEADDIM : at + (i + 1) * HEADDIM] for i in range(4)]
        logit = dot(quer, keyk, LAST) * HEADDIM ** (-0.5)
        logit_out[head] = logit
        prob = jnp.where(visible, logit / (1.0 + jnp.exp(-logit)) * (1.0 / HMAX), 0.0).astype(BF)
        prob_out[head] = prob
        att = dot(prob, value)
        own = pl.ds(head * HEADDIM, HEADDIM)
        att_out[:, own] = att
        dnorm = dmix[:, head * HEADDIM : (head + 1) * HEADDIM] * gate.astype(F32)
        for i, term in enumerate((att, att * att, dnorm, dnorm * att)):
            totals[i] = totals[i] + term
    table = jnp.zeros((tok, tok), F32)
    for i, total in enumerate(totals):
        table = jnp.where(key == i, jnp.sum(total, axis=1, keepdims=True), table)
    sums = table.T[:8]
    for copy in range(sum_out.shape[0]):
        sum_out[copy] = sums


def backward_kernel(total_width, sum_ref, act_ref, slope_ref, lslope_ref, prob_ref, att_ref, dmix_ref, mixed_out, dpre_out):
    tok, width = act_ref.shape
    heads = width // (4 * HEADDIM)
    means = sum_ref[0]
    for part in range(1, sum_ref.shape[0]):
        means = means + sum_ref[part]
    means = means * (1.0 / total_width)
    row = lax.broadcasted_iota(jnp.int32, (tok, tok), 0)
    col = lax.broadcasted_iota(jnp.int32, (tok, tok), 1)
    cols = dot((row == col).astype(F32), means, LAST, lax.Precision.HIGHEST)
    mean, second, grad_one, grad_att = [cols[:, i : i + 1] for i in range(4)]
    rstd = lax.rsqrt(second - mean * mean + EPS)
    grad_two = (grad_att - mean * grad_one) * rstd
    for head in range(heads):
        at = head * 4 * HEADDIM
        gate, value, quer, keyk = [act_ref[:, at + i * HEADDIM : at + (i + 1) * HEADDIM] for i in range(4)]
        own = pl.ds(head * HEADDIM, HEADDIM)
        normed = (att_ref[:, own] - mean) * rstd
        dmix = dmix_ref[:, own]
        gate = gate.astype(F32)
        mixed = (normed * gate).astype(BF)
        for copy in range(mixed_out.shape[0]):
            mixed_out[copy, :, own] = mixed
        datt = (rstd * (dmix * gate - grad_one - normed * grad_two)).astype(BF)
        dvalue = dot(prob_ref[head], datt, FIRST)
        dlogit = (dot(datt, value, LAST) * lslope_ref[head]).astype(BF)
        dquer = dot(dlogit, keyk)
        dkey = dot(dlogit, quer, FIRST)
        for i, term in enumerate((dmix * normed, dvalue, dquer, dkey)):
            place = pl.ds(at + i * HEADDIM, HEADDIM)
            dpre_out[:, place] = (term * slope_ref[:, place]).astype(BF)


def attention_forward(starts, pre_parts, dmix_parts, tok, copies):
    n_part, rows, width = pre_parts.shape
    heads = width // (4 * HEADDIM)
    head_cols = heads * HEADDIM
    owners = rows // tok
    square = lambda kind: jax.ShapeDtypeStruct((owners, heads, tok, tok), kind)
    square_spec = pl.BlockSpec((None, heads, tok, tok), lambda b: (b, 0, 0, 0))
    wide_spec = pl.BlockSpec((tok, width), lambda b: (b, 0))
    thin_spec = pl.BlockSpec((tok, head_cols), lambda b: (b, 0))
    return pl.pallas_call(
        forward_kernel,
        grid=(owners,),
        in_specs=[
            pl.BlockSpec((tok, 1), lambda b: (b, 0)),
            pl.BlockSpec((n_part, tok, width), lambda b: (0, b, 0)),
        ]
        + [thin_spec] * n_part,
        out_specs=[wide_spec, wide_spec, square_spec, square_spec, thin_spec, thin_spec, pl.BlockSpec((copies, 8, tok), lambda b: (0, 0, b))],
        out_shape=[
            jax.ShapeDtypeStruct((rows, width), F32),
            jax.ShapeDtypeStruct((rows, width), BF),
            square(F32),
            square(BF),
            jax.ShapeDtypeStruct((rows, head_cols), F32),
            jax.ShapeDtypeStruct((rows, head_cols), F32),
            jax.ShapeDtypeStruct((copies, 8, rows), F32),
        ],
        cost_estimate=pl.CostEstimate(flops=4 * rows * tok * head_cols, bytes_accessed=8 << 20, transcendentals=rows * width),
    )(starts, pre_parts, *dmix_parts)


def attention_backward(sums, act, slope, lslope, prob, att, dmix, tok, total_width):
    rows, width = act.shape
    heads = width // (4 * HEADDIM)
    head_cols = heads * HEADDIM
    owners = rows // tok
    square_spec = pl.BlockSpec((None, heads, tok, tok), lambda b: (b, 0, 0, 0))
    wide_spec = pl.BlockSpec((tok, width), lambda b: (b, 0))
    thin_spec = pl.BlockSpec((tok, head_cols), lambda b: (b, 0))
    return pl.pallas_call(
        lambda *refs: backward_kernel(total_width, *refs),
        grid=(owners,),
        in_specs=[
            pl.BlockSpec((sums.shape[0], 8, tok), lambda b: (0, 0, b)),
            wide_spec, wide_spec, square_spec, square_spec, thin_spec, thin_spec,
        ],
        out_specs=[pl.BlockSpec((N_X, tok, head_cols), lambda b: (0, b, 0)), wide_spec],
        out_shape=[
            jax.ShapeDtypeStruct((N_X, rows, head_cols), BF),
            jax.ShapeDtypeStruct((rows, width), BF),
        ],
        cost_estimate=pl.CostEstimate(flops=8 * rows * tok * head_cols, bytes_accessed=4 << 20, transcendentals=rows),
    )(sums, act, slope, lslope, prob, att, dmix)


def widen_kernel(place_ref, half_ref, *refs):
    refs[-1][...] = half_ref[...].astype(F32)


def place_halves(place, value, into=None):
    rows, width = value.shape
    extra = [] if into is None else [into]
    return pl.pallas_call(
        widen_kernel,
        grid_spec=pltpu.PrefetchScalarGridSpec(
            num_scalar_prefetch=1,
            grid=(2,),
            in_specs=[pl.BlockSpec((rows, width // 2), lambda h, place: (0, h ^ place[1]))]
            + [pl.BlockSpec(memory_space=pl.ANY)] * len(extra),
            out_specs=pl.BlockSpec((rows, width // 2), lambda h, place: (0, 2 * h + place[0])),
        ),
        out_shape=jax.ShapeDtypeStruct((rows, 2 * width), F32),
        input_output_aliases={2: 0} if extra else {},
        cost_estimate=pl.CostEstimate(flops=0, bytes_accessed=rows * width * 6, transcendentals=0),
    )(place, value, *extra)


def grad_kernel(core_ref, x_ref, d_ref, *refs):
    out = refs[-1]
    grad = dot(x_ref[...], d_ref[...])
    if len(refs) == 1:
        out[...] = grad.astype(BF)
    else:
        there_ref, low_ref, high_ref = refs[:3]
        low, mid = low_ref.shape[0], grad.shape[0]
        out[:low] = low_ref[...]
        out[low : low + mid] = (grad + there_ref[...].astype(F32)).astype(BF)
        out[low + mid :] = high_ref[...]


def grad_columns(core, x_t, d_all, *more):
    depth, width = d_all.shape
    step = width // 4
    rows = x_t.shape[0] + sum(piece.shape[0] for piece in more[1:])
    return pl.pallas_call(
        grad_kernel,
        grid_spec=pltpu.PrefetchScalarGridSpec(
            num_scalar_prefetch=1,
            grid=(2,),
            in_specs=[
                pl.BlockSpec(x_t.shape, lambda i, core: (0, 0)),
                pl.BlockSpec((depth, step), lambda i, core: (0, core[0] * 2 + i)),
            ]
            + [pl.BlockSpec((piece.shape[0], step), lambda i, core: (0, i)) for piece in more],
            out_specs=pl.BlockSpec((rows, step), lambda i, core: (0, i)),
        ),
        out_shape=jax.ShapeDtypeStruct((rows, 2 * step), BF),
        compiler_params=pltpu.CompilerParams(vmem_limit_bytes=24 << 20),
        cost_estimate=pl.CostEstimate(
            flops=4 * x_t.size * step, bytes_accessed=4 << 20, transcendentals=0
        ),
    )(core, x_t, d_all, *more)


def x_exchange(blocks):
    groups = [[2 * x + y for x in range(N_X)] for y in range(2)]
    return lax.all_to_all(blocks, "col", 0, 0, axis_index_groups=groups, tiled=True)


def head_groups_gather(value):
    groups = [[r * 2 * N_X + 2 * x + y for r in range(N_Z) for y in range(2)] for x in range(N_X)]
    return lax.all_to_all(value, ("row", "col"), 0, 0, axis_index_groups=groups, tiled=True)


def halves(array, which, axis):
    size = array.shape[axis] // 2
    return (
        lax.dynamic_slice_in_dim(array, which * size, size, axis),
        lax.dynamic_slice_in_dim(array, (1 - which) * size, size, axis),
    )


def dp_exchange(value, count):
    parts = [value[:count]]
    parts += [dp_swap(value[j * count : (j + 1) * count], j) for j in range(1, 4)]
    return jnp.concatenate(parts, axis=0)


def local(events, out_grad, w_uvqk, w_output, hist_len, token_slot):
    n_dp, n_row, n_col = 4, N_Z, 2 * N_X
    tok_own, feat = events.shape
    send_count = tok_own // n_dp
    dp_at = lax.axis_index("dp")
    row_at = lax.axis_index("row")
    col_at = lax.axis_index("col")
    x_at, ylo_at, core_at = col_at // 2, col_at % 2, dp_at % 2
    owner_self = dp_at * n_row + row_at
    places = jnp.arange(tok_own, dtype=jnp.int32)

    events_other = ylo_swap(events)
    slots = token_slot.reshape(n_dp, n_row, tok_own)
    src_slots = lax.dynamic_index_in_dim(slots, row_at, 1, keepdims=False)
    own_slots = lax.dynamic_index_in_dim(src_slots, dp_at, 0, keepdims=False)
    send_rank = jnp.sum((own_slots[None, :] < own_slots[:, None]).astype(jnp.int32), axis=1)
    target = own_slots // (tok_own * n_row)
    send_place = (target ^ dp_at) * send_count + send_rank - target * send_count
    send_pick = (send_place[None, :] == places[:, None]).astype(BF)
    x_send = dot(send_pick, jnp.concatenate([events, events_other, out_grad], axis=1)).astype(BF)
    xg_recv = dp_exchange(x_send, send_count)
    sources = jnp.arange(n_dp, dtype=jnp.int32)
    to_self = src_slots // tok_own == owner_self
    before = jnp.sum(
        (to_self[:, None, :] & (src_slots[:, None, :] < src_slots[:, :, None])).astype(jnp.int32),
        axis=2,
    )
    recv_row = (sources ^ dp_at)[:, None] * send_count + before
    local_place = src_slots - owner_self * tok_own
    hits = to_self[:, :, None] & (recv_row[:, :, None] == places[None, None, :])
    row_place = jnp.sum(jnp.where(hits, local_place[:, :, None], 0), axis=(0, 1))
    own_pick = (row_place[None, :] == places[:, None]).astype(BF)
    xg_recv, w_later = lax.optimization_barrier((xg_recv, w_uvqk))
    xg_own = dot(own_pick, xg_recv).astype(BF)
    x_own, g_own = xg_own[:, :feat], xg_own[:, 2 * feat :]

    w_keep, w_send = halves(w_later, ylo_at, 1)
    w_pair = jnp.concatenate([w_keep, ylo_swap(w_send)], axis=0)

    tokens = n_row * tok_own
    rows_half = tok_own // 2
    ups, downs = [xg_own], [xg_own]
    for _ in range(3):
        ups, downs = ups + [z_shift(ups[-1], 1)], downs + [z_shift(downs[-1], -1)]
    far_low, far_high = z_shift(ups[3][:rows_half], 1), z_shift(downs[3][rows_half:], -1)
    row_place_at = row_at.astype(jnp.int32)[None]
    near_panels = place_blocks(row_place_at, [xg_own] + downs[1:] + ups[:0:-1], 2 * feat)
    wo_keep, wo_send = halves(w_output, ylo_at, 0)
    d_other = ylo_swap(dot(near_panels[1], wo_send, LAST).astype(BF))
    x_panel, g_panel = place_far(row_place_at, far_low, far_high, near_panels)
    g_far = jnp.concatenate([far_low[:, 2 * feat :], far_high[:, 2 * feat :]], axis=0)
    d_far = ylo_swap(dot(g_far, wo_send, LAST).astype(BF))
    rows_pair = 2 * tok_own

    def x_chunk(panel, k):
        return lax.dynamic_slice_in_dim(panel, (x_at + k) % N_X * rows_pair, rows_pair, 0)

    pre_part = product(x_panel, w_pair)
    pre_parts = x_exchange(pre_part.reshape(N_X, rows_pair, -1))
    far_here = jnp.arange(n_row) == (row_at + n_row // 2) % n_row
    d_far = jnp.where(far_here[:, None, None], d_far[None].astype(F32), 0.0)
    d_pair = dot(g_panel, wo_keep, LAST) + d_other.astype(F32) + d_far.reshape(d_other.shape)
    d_pair = d_pair.astype(BF)
    dmix_parts = [x_chunk(d_pair, 0)] + [x_shift(x_chunk(d_pair, k), k) for k in (1, -1, 2)]

    lengths = lax.dynamic_slice_in_dim(hist_len, dp_at * n_row + x_at * 2, 2, 0)
    starts = history_starts(lengths, tok_own).reshape(rows_pair, 1)
    preact, act, logits, probs, att, d_mixed, sums = attention_forward(
        starts, pre_parts, dmix_parts, tok_own, 2 * n_row
    )
    sums = head_groups_gather(sums)
    slope = silu_slope(preact)
    keys = jnp.arange(tok_own, dtype=jnp.int32)
    visible = (keys[None, None, :] >= starts.reshape(2, tok_own, 1)) & (
        keys[None, None, :] <= keys[None, :, None]
    )
    lslope = jnp.where(
        visible[:, None], silu_slope(logits) * (HEADDIM ** (-0.5) / HMAX), 0.0
    )
    total_width = att.shape[1] * n_row * 2
    mixed, d_pre = attention_backward(
        sums, act, slope, lslope, probs, att, d_mixed, tok_own, total_width
    )

    mixed_here = x_exchange(mixed).reshape(tokens, mixed.shape[2])
    x_up, x_down = x_shift(d_pre, 1), x_shift(d_pre, -1)
    x_up, x_down, mixed_here = lax.optimization_barrier((x_up, x_down, mixed_here))
    far_low, far_high = x_shift(x_up[:tok_own], 1), x_shift(x_down[tok_own:], -1)
    d_pre_all = pre_parts
    for k, piece in ((0, d_pre), (3, x_up), (1, x_down)):
        d_pre_all = lax.dynamic_update_slice(d_pre_all, piece[None], ((x_at + k) % N_X, 0, 0))
    d_far = jnp.concatenate([far_low, far_high], axis=0)
    d_pre_all = lax.dynamic_update_slice(d_pre_all, d_far[None], ((x_at + 2) % N_X, 0, 0))
    d_pre_all = d_pre_all.reshape(tokens, -1)
    mixed_there = ylo_swap(mixed_here)
    mixed_all = jnp.where(
        ylo_at == 0,
        jnp.concatenate([mixed_here, mixed_there], axis=1),
        jnp.concatenate([mixed_there, mixed_here], axis=1),
    )

    def z_chunk(panel, k):
        return lax.dynamic_slice_in_dim(panel, (row_at + k) % n_row * tok_own, tok_own, 0)

    out_all = dot(mixed_all, w_output).astype(BF)
    far = jnp.concatenate(
        [dot(z_chunk(d_pre_all, 4), w_pair, LAST).astype(BF), z_chunk(out_all, 4)], axis=1
    )
    far, d_pre_all = lax.optimization_barrier((far, d_pre_all))
    mid = far.shape[1] // 2
    up, down = z_shift(far[:, :mid], 1), z_shift(far[:, mid:], -1)

    half = feat // 2
    x_t = x_panel.T
    x_t = jnp.concatenate([x_t[:half], x_t[feat:], x_t[half:feat]], axis=0)
    x_t = lax.optimization_barrier(x_t)
    core = core_at.astype(jnp.int32)[None]
    ug_there = dp_swap(grad_columns(1 - core, x_t, d_pre_all), 1)
    m_keep, m_send = halves(mixed_all, core_at, 1)
    og_there = dp_swap(dot(m_send.T, g_panel).astype(BF), 1)
    og_sum = dot(m_keep.T, g_panel) + og_there.astype(F32)
    og_mid = og_sum.shape[0] // 2
    og_low, og_high = og_sum[:og_mid].astype(BF), og_sum[og_mid:].astype(BF)
    grads = grad_columns(core, x_t, d_pre_all, ug_there, og_low, og_high)

    dx_all = dot(d_pre_all, w_pair, LAST).astype(BF)

    def term(k):
        return jnp.concatenate([z_chunk(dx_all, k), z_chunk(out_all, k)], axis=1).astype(F32)

    to_up, to_down = term(3), term(-3)
    to_up = jnp.concatenate([to_up[:, :mid] + up.astype(F32), to_up[:, mid:]], axis=1)
    to_down = jnp.concatenate([to_down[:, :mid], to_down[:, mid:] + down.astype(F32)], axis=1)
    up, down = z_shift(to_up.astype(BF), 1), z_shift(to_down.astype(BF), -1)
    y_up, y_down = grads[og_mid + half :], grads[: og_mid + half + feat]
    y_up, y_down = y_shift(y_up, 1), y_shift(y_down, -1)
    up, down, grads = lax.optimization_barrier((up, down, grads))
    to_up, to_down = term(2) + up.astype(F32), term(-2) + down.astype(F32)
    up, down = z_shift(to_up.astype(BF), 1), z_shift(to_down.astype(BF), -1)
    to_up, to_down = term(1) + up.astype(F32), term(-1) + down.astype(F32)
    up, down = z_shift(to_up.astype(BF), 1), z_shift(to_down.astype(BF), -1)
    far_up, far_down = y_shift(y_up[feat:], 1), y_shift(y_down[: og_mid + half], -1)
    up, down, y_up, y_down = lax.optimization_barrier((up, down, y_up, y_down))
    ug_cross = y_up[:feat].astype(F32) + y_down[og_mid + half :].astype(F32)
    rows = term(0) + up.astype(F32) + down.astype(F32)

    dx_other = ylo_swap(rows[:, feat : 2 * feat].astype(BF))
    ug_stay = jnp.concatenate(
        [
            grads[og_mid : og_mid + half].astype(F32) + far_down[og_mid:].astype(F32),
            grads[og_mid + half + feat : -og_mid].astype(F32) + far_up[:half].astype(F32),
        ],
        axis=0,
    )
    ug_half = jnp.concatenate([ug_stay.astype(BF), ug_cross.astype(BF)], axis=1)
    og_half = jnp.concatenate(
        [
            og_sum[:og_mid] + far_down[:og_mid].astype(F32),
            og_sum[og_mid:] + far_up[half:].astype(F32),
        ],
        axis=0,
    ).astype(BF)
    ug_there, og_there = dp_swap(ug_half, 1), dp_swap(og_half, 1)
    dx_own = (rows[:, :feat] + dx_other.astype(F32) + g_own.astype(F32)).astype(BF)
    y_own = (rows[:, 2 * feat :] + x_own.astype(F32)).astype(BF)
    back = dot(own_pick, jnp.concatenate([y_own, dx_own], axis=1), FIRST).astype(BF)
    home = dp_exchange(back, send_count)
    layer_out = dot(send_pick, home[:, :feat], FIRST).astype(BF)
    event_grad = dot(send_pick, home[:, feat:], FIRST).astype(BF)
    output_grad = jnp.where(
        core_at == 0,
        jnp.concatenate([og_half, og_there], axis=0),
        jnp.concatenate([og_there, og_half], axis=0),
    ).astype(F32)
    ylo = ylo_at.astype(jnp.int32)[None]
    uvqk_grad = place_halves(jnp.concatenate([core, ylo]), ug_half)
    uvqk_grad = place_halves(jnp.concatenate([1 - core, ylo]), ug_there, uvqk_grad)
    return (layer_out, event_grad, uvqk_grad, output_grad)


def solution(mesh):
    in_specs = (
        P(("dp", "row"), "col"),
        P(("dp", "row"), "col"),
        P("col", "row"),
        P("row", "col"),
        P(),
        P(),
    )
    out_specs = (P(("dp", "row"), "col"), P(("dp", "row"), "col"), P("col", "row"), P("row", "col"))
    return jax.shard_map(local, mesh=mesh, in_specs=in_specs, out_specs=out_specs, check_vma=False)
```

```python
import jax
import jax.numpy as jnp
from jax import lax
from jax.experimental import pallas as pl
from jax.experimental.pallas import tpu as pltpu
from jax.sharding import PartitionSpec as P

HEADDIM = 128
HMAX = 64
EPS = 1e-06
LAST = (((1,), (1,)), ((), ()))
FIRST = (((0,), (0,)), ((), ()))
BF = jnp.bfloat16
F32 = jnp.float32

N_X = 4
N_Z = 8


def x_shift(value, step):
    pairs = [(c, (c // 2 + step) % N_X * 2 + c % 2) for c in range(2 * N_X)]
    return lax.ppermute(value, "col", pairs)


def z_shift(value, step):
    return lax.ppermute(value, "row", [(r, (r + step) % N_Z) for r in range(N_Z)])


def ylo_swap(value):
    return lax.ppermute(value, "col", [(c, c ^ 1) for c in range(2 * N_X)])


def dp_swap(value, bits):
    return lax.ppermute(value, "dp", [(d, d ^ bits) for d in range(4)])


def y_shift(value, step):
    pairs = []
    for d in range(4):
        for c in range(2 * N_X):
            y = (d // 2 * 2 + c % 2 + step) % 4
            pairs.append((d * 2 * N_X + c, (y // 2 * 2 + d % 2) * 2 * N_X + c // 2 * 2 + y % 2))
    return lax.ppermute(value, ("dp", "col"), pairs)


def place_kernel(count, at_ref, *refs):
    blocks, outs = refs[:count], refs[-2:]
    cut = outs[0].shape[1]
    k = pl.program_id(0)
    for i, block in enumerate(blocks):

        @pl.when(k == i)
        def _(block=block):
            outs[0][...] = block[:, :cut]
            outs[1][...] = block[:, cut:]

    @pl.when(k == count)
    def _():
        outs[0][...] = jnp.zeros(outs[0].shape, BF)
        outs[1][...] = jnp.zeros(outs[1].shape, BF)


def place_blocks(at, blocks, cut):
    rows, width = blocks[0].shape
    size = len(blocks) + 1
    order = blocks[:4] + blocks[4:]

    def where(k, at):
        return ((at[0] + jnp.where(k < 4, k, jnp.where(k < size - 1, k + 1, 4))) % size, 0)

    return pl.pallas_call(
        lambda *refs: place_kernel(len(order), *refs),
        grid_spec=pltpu.PrefetchScalarGridSpec(
            num_scalar_prefetch=1,
            grid=(size,),
            in_specs=[pl.BlockSpec((rows, width), lambda k, at: (0, 0)) for _ in order],
            out_specs=[pl.BlockSpec((rows, cut), where), pl.BlockSpec((rows, width - cut), where)],
        ),
        out_shape=[
            jax.ShapeDtypeStruct((size * rows, cut), BF),
            jax.ShapeDtypeStruct((size * rows, width - cut), BF),
        ],
        cost_estimate=pl.CostEstimate(flops=0, bytes_accessed=2 * size * rows * width * 2, transcendentals=0),
    )(at, *order)


def place_far_kernel(at_ref, low_ref, high_ref, x_in, g_in, x_out, g_out):
    half, cut = low_ref.shape[0], x_out.shape[1]
    x_out[:half], x_out[half:] = low_ref[:, :cut], high_ref[:, :cut]
    g_out[:half], g_out[half:] = low_ref[:, cut:], high_ref[:, cut:]


def place_far(at, low, high, panels):
    rows, width = 2 * low.shape[0], low.shape[1]
    size = panels[0].shape[0] // rows
    where = lambda i, at: ((at[0] + size // 2) % size, 0)
    return pl.pallas_call(
        place_far_kernel,
        grid_spec=pltpu.PrefetchScalarGridSpec(
            num_scalar_prefetch=1,
            grid=(1,),
            in_specs=[pl.BlockSpec(low.shape, lambda i, at: (0, 0))] * 2
            + [pl.BlockSpec(memory_space=pl.ANY)] * 2,
            out_specs=[pl.BlockSpec((rows, panel.shape[1]), where) for panel in panels],
        ),
        out_shape=[jax.ShapeDtypeStruct(panel.shape, BF) for panel in panels],
        input_output_aliases={3: 0, 4: 1},
        cost_estimate=pl.CostEstimate(flops=0, bytes_accessed=4 * rows * width, transcendentals=0),
    )(at, low, high, *panels)


def product_kernel(left_ref, right_ref, out_ref):
    out_ref[...] = dot(left_ref[...], right_ref[...]).astype(BF)


def product(left, right, step=256):
    rows, depth = left.shape
    columns = right.shape[1]
    return pl.pallas_call(
        product_kernel,
        grid=(columns // step,),
        in_specs=[
            pl.BlockSpec((rows, depth), lambda i: (0, 0)),
            pl.BlockSpec((depth, step), lambda i: (0, i)),
        ],
        out_specs=pl.BlockSpec((rows, step), lambda i: (0, i)),
        out_shape=jax.ShapeDtypeStruct((rows, columns), BF),
        compiler_params=pltpu.CompilerParams(vmem_limit_bytes=24 << 20),
        cost_estimate=pl.CostEstimate(
            flops=2 * rows * depth * columns, bytes_accessed=6 << 20, transcendentals=0
        ),
    )(left, right)


def silu_slope(inputs):
    sigma = jax.nn.sigmoid(inputs)
    return sigma * (1.0 + inputs * (1.0 - sigma))


def history_starts(lengths, width):
    history_ends = jnp.cumsum(lengths, axis=1)
    places = jnp.arange(width, dtype=jnp.int32)
    earlier = (history_ends[:, None, :] <= places[None, :, None]).astype(jnp.int32)
    return jnp.sum(lengths[:, None, :] * earlier, axis=2)


def dot(left, right, dims=(((1,), (0,)), ((), ())), precision=None):
    return lax.dot_general(left, right, dims, precision=precision, preferred_element_type=F32)


def forward_kernel(starts_ref, pre_ref, *refs):
    n_part, tok, width = pre_ref.shape
    heads = width // (4 * HEADDIM)
    dmix_refs, outs = refs[:n_part], refs[n_part:]
    pre_out, act_out, logit_out, prob_out, att_out, dmix_out, sum_out = outs
    pre = pre_ref[0].astype(F32)
    dmix = dmix_refs[0][...].astype(F32)
    for part in range(1, n_part):
        pre = pre + pre_ref[part].astype(F32)
        dmix = dmix + dmix_refs[part][...].astype(F32)
    pre_out[...] = pre
    dmix_out[...] = dmix
    act = (pre / (1.0 + jnp.exp(-pre))).astype(BF)
    act_out[...] = act
    query = lax.broadcasted_iota(jnp.int32, (tok, tok), 0)
    key = lax.broadcasted_iota(jnp.int32, (tok, tok), 1)
    visible = (key <= query) & (key >= starts_ref[...])
    totals = [0.0, 0.0, 0.0, 0.0]
    for head in range(heads):
        at = head * 4 * HEADDIM
        gate, value, quer, keyk = [act[:, at + i * HEADDIM : at + (i + 1) * HEADDIM] for i in range(4)]
        logit = dot(quer, keyk, LAST) * HEADDIM ** (-0.5)
        logit_out[head] = logit
        prob = jnp.where(visible, logit / (1.0 + jnp.exp(-logit)) * (1.0 / HMAX), 0.0).astype(BF)
        prob_out[head] = prob
        att = dot(prob, value)
        own = pl.ds(head * HEADDIM, HEADDIM)
        att_out[:, own] = att
        dnorm = dmix[:, head * HEADDIM : (head + 1) * HEADDIM] * gate.astype(F32)
        for i, term in enumerate((att, att * att, dnorm, dnorm * att)):
            totals[i] = totals[i] + term
    table = jnp.zeros((tok, tok), F32)
    for i, total in enumerate(totals):
        table = jnp.where(key == i, jnp.sum(total, axis=1, keepdims=True), table)
    sums = table.T[:8]
    for copy in range(sum_out.shape[0]):
        sum_out[copy] = sums


def backward_kernel(total_width, sum_ref, act_ref, slope_ref, lslope_ref, prob_ref, att_ref, dmix_ref, mixed_out, dpre_out):
    tok, width = act_ref.shape
    heads = width // (4 * HEADDIM)
    means = sum_ref[0]
    for part in range(1, sum_ref.shape[0]):
        means = means + sum_ref[part]
    means = means * (1.0 / total_width)
    row = lax.broadcasted_iota(jnp.int32, (tok, tok), 0)
    col = lax.broadcasted_iota(jnp.int32, (tok, tok), 1)
    cols = dot((row == col).astype(F32), means, LAST, lax.Precision.HIGHEST)
    mean, second, grad_one, grad_att = [cols[:, i : i + 1] for i in range(4)]
    rstd = lax.rsqrt(second - mean * mean + EPS)
    grad_two = (grad_att - mean * grad_one) * rstd
    for head in range(heads):
        at = head * 4 * HEADDIM
        gate, value, quer, keyk = [act_ref[:, at + i * HEADDIM : at + (i + 1) * HEADDIM] for i in range(4)]
        own = pl.ds(head * HEADDIM, HEADDIM)
        normed = (att_ref[:, own] - mean) * rstd
        dmix = dmix_ref[:, own]
        gate = gate.astype(F32)
        mixed_out[:, own] = (normed * gate).astype(BF)
        datt = (rstd * (dmix * gate - grad_one - normed * grad_two)).astype(BF)
        dvalue = dot(prob_ref[head], datt, FIRST)
        dlogit = (dot(datt, value, LAST) * lslope_ref[head]).astype(BF)
        dquer = dot(dlogit, keyk)
        dkey = dot(dlogit, quer, FIRST)
        for i, term in enumerate((dmix * normed, dvalue, dquer, dkey)):
            place = pl.ds(at + i * HEADDIM, HEADDIM)
            dpre_out[:, place] = (term * slope_ref[:, place]).astype(BF)


def attention_forward(starts, pre_parts, dmix_parts, tok, copies):
    n_part, rows, width = pre_parts.shape
    heads = width // (4 * HEADDIM)
    head_cols = heads * HEADDIM
    owners = rows // tok
    square = lambda kind: jax.ShapeDtypeStruct((owners, heads, tok, tok), kind)
    square_spec = pl.BlockSpec((None, heads, tok, tok), lambda b: (b, 0, 0, 0))
    wide_spec = pl.BlockSpec((tok, width), lambda b: (b, 0))
    thin_spec = pl.BlockSpec((tok, head_cols), lambda b: (b, 0))
    return pl.pallas_call(
        forward_kernel,
        grid=(owners,),
        in_specs=[
            pl.BlockSpec((tok, 1), lambda b: (b, 0)),
            pl.BlockSpec((n_part, tok, width), lambda b: (0, b, 0)),
        ]
        + [thin_spec] * n_part,
        out_specs=[wide_spec, wide_spec, square_spec, square_spec, thin_spec, thin_spec, pl.BlockSpec((copies, 8, tok), lambda b: (0, 0, b))],
        out_shape=[
            jax.ShapeDtypeStruct((rows, width), F32),
            jax.ShapeDtypeStruct((rows, width), BF),
            square(F32),
            square(BF),
            jax.ShapeDtypeStruct((rows, head_cols), F32),
            jax.ShapeDtypeStruct((rows, head_cols), F32),
            jax.ShapeDtypeStruct((copies, 8, rows), F32),
        ],
        cost_estimate=pl.CostEstimate(flops=4 * rows * tok * head_cols, bytes_accessed=8 << 20, transcendentals=rows * width),
    )(starts, pre_parts, *dmix_parts)


def attention_backward(sums, act, slope, lslope, prob, att, dmix, tok, total_width):
    rows, width = act.shape
    heads = width // (4 * HEADDIM)
    head_cols = heads * HEADDIM
    owners = rows // tok
    square_spec = pl.BlockSpec((None, heads, tok, tok), lambda b: (b, 0, 0, 0))
    wide_spec = pl.BlockSpec((tok, width), lambda b: (b, 0))
    thin_spec = pl.BlockSpec((tok, head_cols), lambda b: (b, 0))
    return pl.pallas_call(
        lambda *refs: backward_kernel(total_width, *refs),
        grid=(owners,),
        in_specs=[
            pl.BlockSpec((sums.shape[0], 8, tok), lambda b: (0, 0, b)),
            wide_spec, wide_spec, square_spec, square_spec, thin_spec, thin_spec,
        ],
        out_specs=[thin_spec, wide_spec],
        out_shape=[
            jax.ShapeDtypeStruct((rows, head_cols), BF),
            jax.ShapeDtypeStruct((rows, width), BF),
        ],
        cost_estimate=pl.CostEstimate(flops=8 * rows * tok * head_cols, bytes_accessed=4 << 20, transcendentals=rows),
    )(sums, act, slope, lslope, prob, att, dmix)


def widen_kernel(place_ref, half_ref, *refs):
    refs[-1][...] = half_ref[...].astype(F32)


def place_halves(place, value, into=None):
    rows, width = value.shape
    extra = [] if into is None else [into]
    return pl.pallas_call(
        widen_kernel,
        grid_spec=pltpu.PrefetchScalarGridSpec(
            num_scalar_prefetch=1,
            grid=(2,),
            in_specs=[pl.BlockSpec((rows, width // 2), lambda h, place: (0, h ^ place[1]))]
            + [pl.BlockSpec(memory_space=pl.ANY)] * len(extra),
            out_specs=pl.BlockSpec((rows, width // 2), lambda h, place: (0, 2 * h + place[0])),
        ),
        out_shape=jax.ShapeDtypeStruct((rows, 2 * width), F32),
        input_output_aliases={2: 0} if extra else {},
        cost_estimate=pl.CostEstimate(flops=0, bytes_accessed=rows * width * 6, transcendentals=0),
    )(place, value, *extra)


def grad_kernel(core_ref, x_ref, d_ref, *refs):
    out = refs[-1]
    grad = dot(x_ref[...], d_ref[...])
    if len(refs) == 1:
        out[...] = grad.astype(BF)
    else:
        there_ref, low_ref, high_ref = refs[:3]
        low, mid = low_ref.shape[0], grad.shape[0]
        out[:low] = low_ref[...]
        out[low : low + mid] = (grad + there_ref[...].astype(F32)).astype(BF)
        out[low + mid :] = high_ref[...]


def grad_columns(core, x_t, d_all, *more):
    depth, width = d_all.shape
    step = width // 4
    rows = x_t.shape[0] + sum(piece.shape[0] for piece in more[1:])
    return pl.pallas_call(
        grad_kernel,
        grid_spec=pltpu.PrefetchScalarGridSpec(
            num_scalar_prefetch=1,
            grid=(2,),
            in_specs=[
                pl.BlockSpec(x_t.shape, lambda i, core: (0, 0)),
                pl.BlockSpec((depth, step), lambda i, core: (0, core[0] * 2 + i)),
            ]
            + [pl.BlockSpec((piece.shape[0], step), lambda i, core: (0, i)) for piece in more],
            out_specs=pl.BlockSpec((rows, step), lambda i, core: (0, i)),
        ),
        out_shape=jax.ShapeDtypeStruct((rows, 2 * step), BF),
        compiler_params=pltpu.CompilerParams(vmem_limit_bytes=24 << 20),
        cost_estimate=pl.CostEstimate(
            flops=4 * x_t.size * step, bytes_accessed=4 << 20, transcendentals=0
        ),
    )(core, x_t, d_all, *more)


def x_exchange(blocks):
    groups = [[2 * x + y for x in range(N_X)] for y in range(2)]
    return lax.all_to_all(blocks, "col", 0, 0, axis_index_groups=groups, tiled=True)


def head_groups_gather(value):
    groups = [[r * 2 * N_X + 2 * x + y for r in range(N_Z) for y in range(2)] for x in range(N_X)]
    return lax.all_to_all(value, ("row", "col"), 0, 0, axis_index_groups=groups, tiled=True)


def halves(array, which, axis):
    size = array.shape[axis] // 2
    return (
        lax.dynamic_slice_in_dim(array, which * size, size, axis),
        lax.dynamic_slice_in_dim(array, (1 - which) * size, size, axis),
    )


def dp_exchange(value, count):
    parts = [value[:count]]
    parts += [dp_swap(value[j * count : (j + 1) * count], j) for j in range(1, 4)]
    return jnp.concatenate(parts, axis=0)


def local(events, out_grad, w_uvqk, w_output, hist_len, token_slot):
    n_dp, n_row, n_col = 4, N_Z, 2 * N_X
    tok_own, feat = events.shape
    send_count = tok_own // n_dp
    dp_at = lax.axis_index("dp")
    row_at = lax.axis_index("row")
    col_at = lax.axis_index("col")
    x_at, ylo_at, core_at = col_at // 2, col_at % 2, dp_at % 2
    owner_self = dp_at * n_row + row_at
    places = jnp.arange(tok_own, dtype=jnp.int32)

    events_other = ylo_swap(events)
    slots = token_slot.reshape(n_dp, n_row, tok_own)
    src_slots = lax.dynamic_index_in_dim(slots, row_at, 1, keepdims=False)
    own_slots = lax.dynamic_index_in_dim(src_slots, dp_at, 0, keepdims=False)
    send_rank = jnp.sum((own_slots[None, :] < own_slots[:, None]).astype(jnp.int32), axis=1)
    target = own_slots // (tok_own * n_row)
    send_place = (target ^ dp_at) * send_count + send_rank - target * send_count
    send_pick = (send_place[None, :] == places[:, None]).astype(BF)
    x_send = dot(send_pick, jnp.concatenate([events, events_other, out_grad], axis=1)).astype(BF)
    xg_recv = dp_exchange(x_send, send_count)
    sources = jnp.arange(n_dp, dtype=jnp.int32)
    to_self = src_slots // tok_own == owner_self
    before = jnp.sum(
        (to_self[:, None, :] & (src_slots[:, None, :] < src_slots[:, :, None])).astype(jnp.int32),
        axis=2,
    )
    recv_row = (sources ^ dp_at)[:, None] * send_count + before
    local_place = src_slots - owner_self * tok_own
    hits = to_self[:, :, None] & (recv_row[:, :, None] == places[None, None, :])
    row_place = jnp.sum(jnp.where(hits, local_place[:, :, None], 0), axis=(0, 1))
    own_pick = (row_place[None, :] == places[:, None]).astype(BF)
    xg_recv, w_later = lax.optimization_barrier((xg_recv, w_uvqk))
    xg_own = dot(own_pick, xg_recv).astype(BF)
    x_own, g_own = xg_own[:, :feat], xg_own[:, 2 * feat :]

    w_keep, w_send = halves(w_later, ylo_at, 1)
    w_pair = jnp.concatenate([w_keep, ylo_swap(w_send)], axis=0)

    tokens = n_row * tok_own
    rows_half = tok_own // 2
    ups, downs = [xg_own], [xg_own]
    for _ in range(3):
        ups, downs = ups + [z_shift(ups[-1], 1)], downs + [z_shift(downs[-1], -1)]
    far_low, far_high = z_shift(ups[3][:rows_half], 1), z_shift(downs[3][rows_half:], -1)
    row_place_at = row_at.astype(jnp.int32)[None]
    near_panels = place_blocks(row_place_at, [xg_own] + downs[1:] + ups[:0:-1], 2 * feat)
    wo_keep, wo_send = halves(w_output, ylo_at, 0)
    d_other = ylo_swap(dot(near_panels[1], wo_send, LAST).astype(BF))
    x_panel, g_panel = place_far(row_place_at, far_low, far_high, near_panels)
    g_far = jnp.concatenate([far_low[:, 2 * feat :], far_high[:, 2 * feat :]], axis=0)
    d_far = ylo_swap(dot(g_far, wo_send, LAST).astype(BF))
    rows_pair = 2 * tok_own

    def x_chunk(panel, k):
        return lax.dynamic_slice_in_dim(panel, (x_at + k) % N_X * rows_pair, rows_pair, 0)

    pre_part = product(x_panel, w_pair)
    pre_parts = x_exchange(pre_part.reshape(N_X, rows_pair, -1))
    far_here = jnp.arange(n_row) == (row_at + n_row // 2) % n_row
    d_far = jnp.where(far_here[:, None, None], d_far[None].astype(F32), 0.0)
    d_pair = dot(g_panel, wo_keep, LAST) + d_other.astype(F32) + d_far.reshape(d_other.shape)
    d_pair = d_pair.astype(BF)
    dmix_parts = [x_chunk(d_pair, 0)] + [x_shift(x_chunk(d_pair, k), k) for k in (1, -1, 2)]

    lengths = lax.dynamic_slice_in_dim(hist_len, dp_at * n_row + x_at * 2, 2, 0)
    starts = history_starts(lengths, tok_own).reshape(rows_pair, 1)
    preact, act, logits, probs, att, d_mixed, sums = attention_forward(
        starts, pre_parts, dmix_parts, tok_own, 2 * n_row
    )
    sums = head_groups_gather(sums)
    slope = silu_slope(preact)
    keys = jnp.arange(tok_own, dtype=jnp.int32)
    visible = (keys[None, None, :] >= starts.reshape(2, tok_own, 1)) & (
        keys[None, None, :] <= keys[None, :, None]
    )
    lslope = jnp.where(
        visible[:, None], silu_slope(logits) * (HEADDIM ** (-0.5) / HMAX), 0.0
    )
    total_width = att.shape[1] * n_row * 2
    mixed, d_pre = attention_backward(
        sums, act, slope, lslope, probs, att, d_mixed, tok_own, total_width
    )

    x_up, x_down = x_shift(d_pre, 1), x_shift(d_pre, -1)
    mixed_there = ylo_swap(mixed)
    mixed = jnp.where(
        ylo_at == 0,
        jnp.concatenate([mixed, mixed_there], axis=1),
        jnp.concatenate([mixed_there, mixed], axis=1),
    )
    x_up, x_down, mixed = lax.optimization_barrier((x_up, x_down, mixed))
    far_low, far_high = x_shift(x_up[:tok_own], 1), x_shift(x_down[tok_own:], -1)
    d_pre_all = pre_parts
    for k, piece in ((0, d_pre), (3, x_up), (1, x_down)):
        d_pre_all = lax.dynamic_update_slice(d_pre_all, piece[None], ((x_at + k) % N_X, 0, 0))
    d_far = jnp.concatenate([far_low, far_high], axis=0)
    d_pre_all = lax.dynamic_update_slice(d_pre_all, d_far[None], ((x_at + 2) % N_X, 0, 0))
    d_pre_all = d_pre_all.reshape(tokens, -1)
    mixed_all = x_exchange(jnp.broadcast_to(mixed[None], (N_X,) + mixed.shape))
    mixed_all = mixed_all.reshape(tokens, -1)

    def z_chunk(panel, k):
        return lax.dynamic_slice_in_dim(panel, (row_at + k) % n_row * tok_own, tok_own, 0)

    far = dot(z_chunk(d_pre_all, 4), w_pair, LAST).astype(BF)
    far, d_pre_all = lax.optimization_barrier((far, d_pre_all))
    up, down = z_shift(far[:, :feat], 1), z_shift(far[:, feat:], -1)

    half = feat // 2
    x_t = x_panel.T
    x_t = jnp.concatenate([x_t[:half], x_t[feat:], x_t[half:feat]], axis=0)
    x_t = lax.optimization_barrier(x_t)
    core = core_at.astype(jnp.int32)[None]
    ug_there, d_pre_all = lax.optimization_barrier(
        (grad_columns(1 - core, x_t, d_pre_all), d_pre_all)
    )
    ug_there = dp_swap(ug_there, 1)
    m_keep, m_send = halves(mixed_all, core_at, 1)
    og_there = dp_swap(dot(m_send.T, g_panel).astype(BF), 1)
    og_sum = dot(m_keep.T, g_panel) + og_there.astype(F32)
    og_mid = og_sum.shape[0] // 2
    og_low, og_high = og_sum[:og_mid].astype(BF), og_sum[og_mid:].astype(BF)
    grads = grad_columns(core, x_t, d_pre_all, ug_there, og_low, og_high)

    dx_all = dot(d_pre_all, w_pair, LAST).astype(BF)
    out_all = dot(mixed_all, w_output).astype(BF)
    part = feat // 2

    dx_terms = lax.optimization_barrier([z_chunk(dx_all, k) for k in range(n_row)])
    out_terms = lax.optimization_barrier([z_chunk(out_all, k) for k in range(n_row)])

    def term(k):
        return dx_terms[k].astype(F32)

    def out_term(k):
        return out_terms[k].astype(F32)

    def message(dx, out):
        return jnp.concatenate([dx.astype(BF), out.astype(BF)], axis=1)

    to_up, to_down = term(3), term(-3)
    to_up = jnp.concatenate([to_up[:, :feat] + up.astype(F32), to_up[:, feat:]], axis=1)
    to_down = jnp.concatenate([to_down[:, :feat], to_down[:, feat:] + down.astype(F32)], axis=1)
    out_far = out_term(4)
    up = z_shift(message(to_up, out_far[:, :part]), 1)
    down = z_shift(message(to_down, out_far[:, part:]), -1)
    y_up, y_down = grads[og_mid + half :], grads[: og_mid + half + feat]
    up, down, y_later = lax.optimization_barrier((up, down, (y_up, y_down)))
    y_up, y_down = y_shift(y_up, 1), y_shift(y_down, -1)
    wide = 2 * feat
    out_up, out_down = out_term(3), out_term(-3)
    out_up = jnp.concatenate([out_up[:, :part] + up[:, wide:].astype(F32), out_up[:, part:]], axis=1)
    out_down = jnp.concatenate([out_down[:, :part], out_down[:, part:] + down[:, wide:].astype(F32)], axis=1)
    up, down = (
        z_shift(message(term(2) + up[:, :wide].astype(F32), out_up), 1),
        z_shift(message(term(-2) + down[:, :wide].astype(F32), out_down), -1),
    )
    to_up = message(term(1) + up[:, :wide].astype(F32), out_term(2) + up[:, wide:].astype(F32))
    to_down = message(term(-1) + down[:, :wide].astype(F32), out_term(-2) + down[:, wide:].astype(F32))
    up, down = z_shift(to_up, 1), z_shift(to_down, -1)
    up, down, y_up, y_down = lax.optimization_barrier((up, down, y_up, y_down))
    far_up, far_down = y_shift(y_up[feat:], 1), y_shift(y_down[: og_mid + half], -1)
    ug_cross = y_up[:feat].astype(F32) + y_down[og_mid + half :].astype(F32)
    rows = term(0) + up[:, :wide].astype(F32) + down[:, :wide].astype(F32)
    dx_other = ylo_swap(rows[:, feat:].astype(BF))
    out_up = z_shift((out_term(1) + up[:, wide:].astype(F32)).astype(BF), 1)
    out_down = z_shift((out_term(-1) + down[:, wide:].astype(F32)).astype(BF), -1)
    out_rows = out_term(0) + out_up.astype(F32) + out_down.astype(F32)

    ug_stay = jnp.concatenate(
        [
            y_later[1][og_mid : og_mid + half].astype(F32) + far_down[og_mid:].astype(F32),
            y_later[0][feat:-og_mid].astype(F32) + far_up[:half].astype(F32),
        ],
        axis=0,
    )
    ug_half = jnp.concatenate([ug_stay.astype(BF), ug_cross.astype(BF)], axis=1)
    og_half = jnp.concatenate(
        [
            og_sum[:og_mid] + far_down[:og_mid].astype(F32),
            og_sum[og_mid:] + far_up[half:].astype(F32),
        ],
        axis=0,
    ).astype(BF)
    ug_there, og_there = dp_swap(ug_half, 1), dp_swap(og_half, 1)
    dx_own = (rows[:, :feat] + dx_other.astype(F32) + g_own.astype(F32)).astype(BF)
    y_own = (out_rows + x_own.astype(F32)).astype(BF)
    back = dot(own_pick, jnp.concatenate([y_own, dx_own], axis=1), FIRST).astype(BF)
    home = dp_exchange(back, send_count)
    layer_out = dot(send_pick, home[:, :feat], FIRST).astype(BF)
    event_grad = dot(send_pick, home[:, feat:], FIRST).astype(BF)
    output_grad = jnp.where(
        core_at == 0,
        jnp.concatenate([og_half, og_there], axis=0),
        jnp.concatenate([og_there, og_half], axis=0),
    ).astype(F32)
    ylo = ylo_at.astype(jnp.int32)[None]
    uvqk_grad = place_halves(jnp.concatenate([core, ylo]), ug_half)
    uvqk_grad = place_halves(jnp.concatenate([1 - core, ylo]), ug_there, uvqk_grad)
    return (layer_out, event_grad, uvqk_grad, output_grad)


def solution(mesh):
    in_specs = (
        P(("dp", "row"), "col"),
        P(("dp", "row"), "col"),
        P("col", "row"),
        P("row", "col"),
        P(),
        P(),
    )
    out_specs = (P(("dp", "row"), "col"), P(("dp", "row"), "col"), P("col", "row"), P("row", "col"))
    return jax.shard_map(local, mesh=mesh, in_specs=in_specs, out_specs=out_specs, check_vma=False)
```

```python
import jax
import jax.numpy as jnp
from jax import lax
from jax.experimental import pallas as pl
from jax.experimental.pallas import tpu as pltpu
from jax.sharding import PartitionSpec as P

HEADDIM = 128
HMAX = 64
EPS = 1e-06
LAST = (((1,), (1,)), ((), ()))
FIRST = (((0,), (0,)), ((), ()))
BF = jnp.bfloat16
F32 = jnp.float32

N_X = 4
N_Z = 8


def x_shift(value, step):
    pairs = [(c, (c // 2 + step) % N_X * 2 + c % 2) for c in range(2 * N_X)]
    return lax.ppermute(value, "col", pairs)


def z_shift(value, step):
    return lax.ppermute(value, "row", [(r, (r + step) % N_Z) for r in range(N_Z)])


def ylo_swap(value):
    return lax.ppermute(value, "col", [(c, c ^ 1) for c in range(2 * N_X)])


def dp_swap(value, bits):
    return lax.ppermute(value, "dp", [(d, d ^ bits) for d in range(4)])


def y_shift(value, step):
    pairs = []
    for d in range(4):
        for c in range(2 * N_X):
            y = (d // 2 * 2 + c % 2 + step) % 4
            pairs.append((d * 2 * N_X + c, (y // 2 * 2 + d % 2) * 2 * N_X + c // 2 * 2 + y % 2))
    return lax.ppermute(value, ("dp", "col"), pairs)


def place_kernel(count, at_ref, *refs):
    blocks, outs = refs[:count], refs[-2:]
    cut = outs[0].shape[1]
    k = pl.program_id(0)
    for i, block in enumerate(blocks):

        @pl.when(k == i)
        def _(block=block):
            outs[0][...] = block[:, :cut]
            outs[1][...] = block[:, cut:]

    @pl.when(k == count)
    def _():
        outs[0][...] = jnp.zeros(outs[0].shape, BF)
        outs[1][...] = jnp.zeros(outs[1].shape, BF)


def place_blocks(at, blocks, cut):
    rows, width = blocks[0].shape
    size = len(blocks) + 1
    order = blocks[:4] + blocks[4:]

    def where(k, at):
        return ((at[0] + jnp.where(k < 4, k, jnp.where(k < size - 1, k + 1, 4))) % size, 0)

    return pl.pallas_call(
        lambda *refs: place_kernel(len(order), *refs),
        grid_spec=pltpu.PrefetchScalarGridSpec(
            num_scalar_prefetch=1,
            grid=(size,),
            in_specs=[pl.BlockSpec((rows, width), lambda k, at: (0, 0)) for _ in order],
            out_specs=[pl.BlockSpec((rows, cut), where), pl.BlockSpec((rows, width - cut), where)],
        ),
        out_shape=[
            jax.ShapeDtypeStruct((size * rows, cut), BF),
            jax.ShapeDtypeStruct((size * rows, width - cut), BF),
        ],
        cost_estimate=pl.CostEstimate(flops=0, bytes_accessed=2 * size * rows * width * 2, transcendentals=0),
    )(at, *order)


def place_far_kernel(at_ref, low_ref, high_ref, x_in, g_in, x_out, g_out):
    half, cut = low_ref.shape[0], x_out.shape[1]
    x_out[:half], x_out[half:] = low_ref[:, :cut], high_ref[:, :cut]
    g_out[:half], g_out[half:] = low_ref[:, cut:], high_ref[:, cut:]


def place_far(at, low, high, panels):
    rows, width = 2 * low.shape[0], low.shape[1]
    size = panels[0].shape[0] // rows
    where = lambda i, at: ((at[0] + size // 2) % size, 0)
    return pl.pallas_call(
        place_far_kernel,
        grid_spec=pltpu.PrefetchScalarGridSpec(
            num_scalar_prefetch=1,
            grid=(1,),
            in_specs=[pl.BlockSpec(low.shape, lambda i, at: (0, 0))] * 2
            + [pl.BlockSpec(memory_space=pl.ANY)] * 2,
            out_specs=[pl.BlockSpec((rows, panel.shape[1]), where) for panel in panels],
        ),
        out_shape=[jax.ShapeDtypeStruct(panel.shape, BF) for panel in panels],
        input_output_aliases={3: 0, 4: 1},
        cost_estimate=pl.CostEstimate(flops=0, bytes_accessed=4 * rows * width, transcendentals=0),
    )(at, low, high, *panels)


def product_kernel(left_ref, right_ref, out_ref):
    out_ref[...] = dot(left_ref[...], right_ref[...]).astype(BF)


def product(left, right, step=256):
    rows, depth = left.shape
    columns = right.shape[1]
    return pl.pallas_call(
        product_kernel,
        grid=(columns // step,),
        in_specs=[
            pl.BlockSpec((rows, depth), lambda i: (0, 0)),
            pl.BlockSpec((depth, step), lambda i: (0, i)),
        ],
        out_specs=pl.BlockSpec((rows, step), lambda i: (0, i)),
        out_shape=jax.ShapeDtypeStruct((rows, columns), BF),
        compiler_params=pltpu.CompilerParams(vmem_limit_bytes=24 << 20),
        cost_estimate=pl.CostEstimate(
            flops=2 * rows * depth * columns, bytes_accessed=6 << 20, transcendentals=0
        ),
    )(left, right)


def silu_slope(inputs):
    sigma = jax.nn.sigmoid(inputs)
    return sigma * (1.0 + inputs * (1.0 - sigma))


def history_starts(lengths, width):
    history_ends = jnp.cumsum(lengths, axis=1)
    places = jnp.arange(width, dtype=jnp.int32)
    earlier = (history_ends[:, None, :] <= places[None, :, None]).astype(jnp.int32)
    return jnp.sum(lengths[:, None, :] * earlier, axis=2)


def dot(left, right, dims=(((1,), (0,)), ((), ())), precision=None):
    return lax.dot_general(left, right, dims, precision=precision, preferred_element_type=F32)


def forward_kernel(starts_ref, pre_ref, *refs):
    n_part, tok, width = pre_ref.shape
    heads = width // (4 * HEADDIM)
    dmix_refs, outs = refs[:n_part], refs[n_part:]
    pre_out, act_out, logit_out, prob_out, att_out, dmix_out, sum_out = outs
    pre = pre_ref[0].astype(F32)
    dmix = dmix_refs[0][...].astype(F32)
    for part in range(1, n_part):
        pre = pre + pre_ref[part].astype(F32)
        dmix = dmix + dmix_refs[part][...].astype(F32)
    pre_out[...] = pre
    dmix_out[...] = dmix
    act = (pre / (1.0 + jnp.exp(-pre))).astype(BF)
    act_out[...] = act
    query = lax.broadcasted_iota(jnp.int32, (tok, tok), 0)
    key = lax.broadcasted_iota(jnp.int32, (tok, tok), 1)
    visible = (key <= query) & (key >= starts_ref[...])
    totals = [0.0, 0.0, 0.0, 0.0]
    for head in range(heads):
        at = head * 4 * HEADDIM
        gate, value, quer, keyk = [act[:, at + i * HEADDIM : at + (i + 1) * HEADDIM] for i in range(4)]
        logit = dot(quer, keyk, LAST) * HEADDIM ** (-0.5)
        logit_out[head] = logit
        prob = jnp.where(visible, logit / (1.0 + jnp.exp(-logit)) * (1.0 / HMAX), 0.0).astype(BF)
        prob_out[head] = prob
        att = dot(prob, value)
        own = pl.ds(head * HEADDIM, HEADDIM)
        att_out[:, own] = att
        dnorm = dmix[:, head * HEADDIM : (head + 1) * HEADDIM] * gate.astype(F32)
        for i, term in enumerate((att, att * att, dnorm, dnorm * att)):
            totals[i] = totals[i] + term
    table = jnp.zeros((tok, tok), F32)
    for i, total in enumerate(totals):
        table = jnp.where(key == i, jnp.sum(total, axis=1, keepdims=True), table)
    sums = table.T[:8]
    for copy in range(sum_out.shape[0]):
        sum_out[copy] = sums


def backward_kernel(total_width, sum_ref, act_ref, slope_ref, lslope_ref, prob_ref, att_ref, dmix_ref, mixed_out, dpre_out):
    tok, width = act_ref.shape
    heads = width // (4 * HEADDIM)
    means = sum_ref[0]
    for part in range(1, sum_ref.shape[0]):
        means = means + sum_ref[part]
    means = means * (1.0 / total_width)
    row = lax.broadcasted_iota(jnp.int32, (tok, tok), 0)
    col = lax.broadcasted_iota(jnp.int32, (tok, tok), 1)
    cols = dot((row == col).astype(F32), means, LAST, lax.Precision.HIGHEST)
    mean, second, grad_one, grad_att = [cols[:, i : i + 1] for i in range(4)]
    rstd = lax.rsqrt(second - mean * mean + EPS)
    grad_two = (grad_att - mean * grad_one) * rstd
    for head in range(heads):
        at = head * 4 * HEADDIM
        gate, value, quer, keyk = [act_ref[:, at + i * HEADDIM : at + (i + 1) * HEADDIM] for i in range(4)]
        own = pl.ds(head * HEADDIM, HEADDIM)
        normed = (att_ref[:, own] - mean) * rstd
        dmix = dmix_ref[:, own]
        gate = gate.astype(F32)
        mixed_out[:, own] = (normed * gate).astype(BF)
        datt = (rstd * (dmix * gate - grad_one - normed * grad_two)).astype(BF)
        dvalue = dot(prob_ref[head], datt, FIRST)
        dlogit = (dot(datt, value, LAST) * lslope_ref[head]).astype(BF)
        dquer = dot(dlogit, keyk)
        dkey = dot(dlogit, quer, FIRST)
        for i, term in enumerate((dmix * normed, dvalue, dquer, dkey)):
            place = pl.ds(at + i * HEADDIM, HEADDIM)
            dpre_out[:, place] = (term * slope_ref[:, place]).astype(BF)


def attention_forward(starts, pre_parts, dmix_parts, tok, copies):
    n_part, rows, width = pre_parts.shape
    heads = width // (4 * HEADDIM)
    head_cols = heads * HEADDIM
    owners = rows // tok
    square = lambda kind: jax.ShapeDtypeStruct((owners, heads, tok, tok), kind)
    square_spec = pl.BlockSpec((None, heads, tok, tok), lambda b: (b, 0, 0, 0))
    wide_spec = pl.BlockSpec((tok, width), lambda b: (b, 0))
    thin_spec = pl.BlockSpec((tok, head_cols), lambda b: (b, 0))
    return pl.pallas_call(
        forward_kernel,
        grid=(owners,),
        in_specs=[
            pl.BlockSpec((tok, 1), lambda b: (b, 0)),
            pl.BlockSpec((n_part, tok, width), lambda b: (0, b, 0)),
        ]
        + [thin_spec] * n_part,
        out_specs=[wide_spec, wide_spec, square_spec, square_spec, thin_spec, thin_spec, pl.BlockSpec((copies, 8, tok), lambda b: (0, 0, b))],
        out_shape=[
            jax.ShapeDtypeStruct((rows, width), F32),
            jax.ShapeDtypeStruct((rows, width), BF),
            square(F32),
            square(BF),
            jax.ShapeDtypeStruct((rows, head_cols), F32),
            jax.ShapeDtypeStruct((rows, head_cols), F32),
            jax.ShapeDtypeStruct((copies, 8, rows), F32),
        ],
        cost_estimate=pl.CostEstimate(flops=4 * rows * tok * head_cols, bytes_accessed=8 << 20, transcendentals=rows * width),
    )(starts, pre_parts, *dmix_parts)


def attention_backward(sums, act, slope, lslope, prob, att, dmix, tok, total_width):
    rows, width = act.shape
    heads = width // (4 * HEADDIM)
    head_cols = heads * HEADDIM
    owners = rows // tok
    square_spec = pl.BlockSpec((None, heads, tok, tok), lambda b: (b, 0, 0, 0))
    wide_spec = pl.BlockSpec((tok, width), lambda b: (b, 0))
    thin_spec = pl.BlockSpec((tok, head_cols), lambda b: (b, 0))
    return pl.pallas_call(
        lambda *refs: backward_kernel(total_width, *refs),
        grid=(owners,),
        in_specs=[
            pl.BlockSpec((sums.shape[0], 8, tok), lambda b: (0, 0, b)),
            wide_spec, wide_spec, square_spec, square_spec, thin_spec, thin_spec,
        ],
        out_specs=[thin_spec, wide_spec],
        out_shape=[
            jax.ShapeDtypeStruct((rows, head_cols), BF),
            jax.ShapeDtypeStruct((rows, width), BF),
        ],
        cost_estimate=pl.CostEstimate(flops=8 * rows * tok * head_cols, bytes_accessed=4 << 20, transcendentals=rows),
    )(sums, act, slope, lslope, prob, att, dmix)


def widen_kernel(place_ref, half_ref, *refs):
    refs[-1][...] = half_ref[...].astype(F32)


def place_halves(place, value, into=None):
    rows, width = value.shape
    extra = [] if into is None else [into]
    return pl.pallas_call(
        widen_kernel,
        grid_spec=pltpu.PrefetchScalarGridSpec(
            num_scalar_prefetch=1,
            grid=(2,),
            in_specs=[pl.BlockSpec((rows, width // 2), lambda h, place: (0, h ^ place[1]))]
            + [pl.BlockSpec(memory_space=pl.ANY)] * len(extra),
            out_specs=pl.BlockSpec((rows, width // 2), lambda h, place: (0, 2 * h + place[0])),
        ),
        out_shape=jax.ShapeDtypeStruct((rows, 2 * width), F32),
        input_output_aliases={2: 0} if extra else {},
        cost_estimate=pl.CostEstimate(flops=0, bytes_accessed=rows * width * 6, transcendentals=0),
    )(place, value, *extra)


def grad_kernel(core_ref, x_ref, d_ref, *refs):
    out = refs[-1]
    grad = dot(x_ref[...], d_ref[...])
    if len(refs) == 1:
        out[...] = grad.astype(BF)
    else:
        out[...] = (grad + refs[0][...].astype(F32)).astype(BF)


def grad_columns(core, x_t, d_all, *more):
    depth, width = d_all.shape
    step = width // 4
    rows = x_t.shape[0]
    return pl.pallas_call(
        grad_kernel,
        grid_spec=pltpu.PrefetchScalarGridSpec(
            num_scalar_prefetch=1,
            grid=(2,),
            in_specs=[
                pl.BlockSpec(x_t.shape, lambda i, core: (0, 0)),
                pl.BlockSpec((depth, step), lambda i, core: (0, core[0] * 2 + i)),
            ]
            + [pl.BlockSpec((piece.shape[0], step), lambda i, core: (0, i)) for piece in more],
            out_specs=pl.BlockSpec((rows, step), lambda i, core: (0, i)),
        ),
        out_shape=jax.ShapeDtypeStruct((rows, 2 * step), BF),
        compiler_params=pltpu.CompilerParams(vmem_limit_bytes=24 << 20),
        cost_estimate=pl.CostEstimate(
            flops=4 * x_t.size * step, bytes_accessed=4 << 20, transcendentals=0
        ),
    )(core, x_t, d_all, *more)


def x_exchange(blocks):
    groups = [[2 * x + y for x in range(N_X)] for y in range(2)]
    return lax.all_to_all(blocks, "col", 0, 0, axis_index_groups=groups, tiled=True)


def head_groups_gather(value):
    groups = [[r * 2 * N_X + 2 * x + y for r in range(N_Z) for y in range(2)] for x in range(N_X)]
    return lax.all_to_all(value, ("row", "col"), 0, 0, axis_index_groups=groups, tiled=True)


def halves(array, which, axis):
    size = array.shape[axis] // 2
    return (
        lax.dynamic_slice_in_dim(array, which * size, size, axis),
        lax.dynamic_slice_in_dim(array, (1 - which) * size, size, axis),
    )


def dp_exchange(value, count):
    parts = [value[:count]]
    parts += [dp_swap(value[j * count : (j + 1) * count], j) for j in range(1, 4)]
    return jnp.concatenate(parts, axis=0)


def local(events, out_grad, w_uvqk, w_output, hist_len, token_slot):
    n_dp, n_row, n_col = 4, N_Z, 2 * N_X
    tok_own, feat = events.shape
    send_count = tok_own // n_dp
    dp_at = lax.axis_index("dp")
    row_at = lax.axis_index("row")
    col_at = lax.axis_index("col")
    x_at, ylo_at, core_at = col_at // 2, col_at % 2, dp_at % 2
    owner_self = dp_at * n_row + row_at
    places = jnp.arange(tok_own, dtype=jnp.int32)

    events_other = ylo_swap(events)
    slots = token_slot.reshape(n_dp, n_row, tok_own)
    src_slots = lax.dynamic_index_in_dim(slots, row_at, 1, keepdims=False)
    own_slots = lax.dynamic_index_in_dim(src_slots, dp_at, 0, keepdims=False)
    send_rank = jnp.sum((own_slots[None, :] < own_slots[:, None]).astype(jnp.int32), axis=1)
    target = own_slots // (tok_own * n_row)
    send_place = (target ^ dp_at) * send_count + send_rank - target * send_count
    send_pick = (send_place[None, :] == places[:, None]).astype(BF)
    x_send = dot(send_pick, jnp.concatenate([events, events_other, out_grad], axis=1)).astype(BF)
    xg_recv = dp_exchange(x_send, send_count)
    sources = jnp.arange(n_dp, dtype=jnp.int32)
    to_self = src_slots // tok_own == owner_self
    before = jnp.sum(
        (to_self[:, None, :] & (src_slots[:, None, :] < src_slots[:, :, None])).astype(jnp.int32),
        axis=2,
    )
    recv_row = (sources ^ dp_at)[:, None] * send_count + before
    local_place = src_slots - owner_self * tok_own
    hits = to_self[:, :, None] & (recv_row[:, :, None] == places[None, None, :])
    row_place = jnp.sum(jnp.where(hits, local_place[:, :, None], 0), axis=(0, 1))
    own_pick = (row_place[None, :] == places[:, None]).astype(BF)
    xg_recv, w_later = lax.optimization_barrier((xg_recv, w_uvqk))
    xg_own = dot(own_pick, xg_recv).astype(BF)
    x_own, g_own = xg_own[:, :feat], xg_own[:, 2 * feat :]

    w_keep, w_send = halves(w_later, ylo_at, 1)
    w_pair = jnp.concatenate([w_keep, ylo_swap(w_send)], axis=0)

    tokens = n_row * tok_own
    rows_half = tok_own // 2
    ups, downs = [xg_own], [xg_own]
    for _ in range(3):
        ups, downs = ups + [z_shift(ups[-1], 1)], downs + [z_shift(downs[-1], -1)]
    far_low, far_high = z_shift(ups[3][:rows_half], 1), z_shift(downs[3][rows_half:], -1)
    row_place_at = row_at.astype(jnp.int32)[None]
    near_panels = place_blocks(row_place_at, [xg_own] + downs[1:] + ups[:0:-1], 2 * feat)
    wo_keep, wo_send = halves(w_output, ylo_at, 0)
    d_other = ylo_swap(dot(near_panels[1], wo_send, LAST).astype(BF))
    x_panel, g_panel = place_far(row_place_at, far_low, far_high, near_panels)
    g_far = jnp.concatenate([far_low[:, 2 * feat :], far_high[:, 2 * feat :]], axis=0)
    d_far = ylo_swap(dot(g_far, wo_send, LAST).astype(BF))
    rows_pair = 2 * tok_own

    def x_chunk(panel, k):
        return lax.dynamic_slice_in_dim(panel, (x_at + k) % N_X * rows_pair, rows_pair, 0)

    pre_part = product(x_panel, w_pair)
    pre_part, d_other, d_far = lax.optimization_barrier((pre_part, d_other, d_far))
    pre_parts = x_exchange(pre_part.reshape(N_X, rows_pair, -1))
    far_here = jnp.arange(n_row) == (row_at + n_row // 2) % n_row
    d_far = jnp.where(far_here[:, None, None], d_far[None].astype(F32), 0.0)
    d_pair = dot(g_panel, wo_keep, LAST) + d_other.astype(F32) + d_far.reshape(d_other.shape)
    d_pair = d_pair.astype(BF)
    dmix_parts = [x_chunk(d_pair, 0)] + [x_shift(x_chunk(d_pair, k), k) for k in (1, -1, 2)]

    lengths = lax.dynamic_slice_in_dim(hist_len, dp_at * n_row + x_at * 2, 2, 0)
    starts = history_starts(lengths, tok_own).reshape(rows_pair, 1)
    preact, act, logits, probs, att, d_mixed, sums = attention_forward(
        starts, pre_parts, dmix_parts, tok_own, 2 * n_row
    )
    sums = head_groups_gather(sums)
    slope = silu_slope(preact)
    keys = jnp.arange(tok_own, dtype=jnp.int32)
    visible = (keys[None, None, :] >= starts.reshape(2, tok_own, 1)) & (
        keys[None, None, :] <= keys[None, :, None]
    )
    lslope = jnp.where(
        visible[:, None], silu_slope(logits) * (HEADDIM ** (-0.5) / HMAX), 0.0
    )
    total_width = att.shape[1] * n_row * 2
    mixed, d_pre = attention_backward(
        sums, act, slope, lslope, probs, att, d_mixed, tok_own, total_width
    )

    x_up, x_down = x_shift(d_pre, 1), x_shift(d_pre, -1)
    mixed_there = ylo_swap(mixed)
    mixed = jnp.where(
        ylo_at == 0,
        jnp.concatenate([mixed, mixed_there], axis=1),
        jnp.concatenate([mixed_there, mixed], axis=1),
    )
    x_up, x_down, mixed = lax.optimization_barrier((x_up, x_down, mixed))
    far_low, far_high = x_shift(x_up[:tok_own], 1), x_shift(x_down[tok_own:], -1)
    d_pre_all = pre_parts
    for k, piece in ((0, d_pre), (3, x_up), (1, x_down)):
        d_pre_all = lax.dynamic_update_slice(d_pre_all, piece[None], ((x_at + k) % N_X, 0, 0))
    d_far = jnp.concatenate([far_low, far_high], axis=0)
    d_pre_all = lax.dynamic_update_slice(d_pre_all, d_far[None], ((x_at + 2) % N_X, 0, 0))
    d_pre_all = d_pre_all.reshape(tokens, -1)
    mixed_all = x_exchange(jnp.broadcast_to(mixed[None], (N_X,) + mixed.shape))
    mixed_all = mixed_all.reshape(tokens, -1)

    def z_chunk(panel, k):
        return lax.dynamic_slice_in_dim(panel, (row_at + k) % n_row * tok_own, tok_own, 0)

    far = dot(z_chunk(d_pre_all, 4), w_pair, LAST).astype(BF)
    far, d_pre_all = lax.optimization_barrier((far, d_pre_all))
    up, down = z_shift(far[:, :feat], 1), z_shift(far[:, feat:], -1)

    half = feat // 2
    x_t = x_panel.T
    x_t = jnp.concatenate([x_t[:half], x_t[feat:], x_t[half:feat]], axis=0)
    x_t = lax.optimization_barrier(x_t)
    core = core_at.astype(jnp.int32)[None]
    ug_there, d_pre_all = lax.optimization_barrier(
        (grad_columns(1 - core, x_t, d_pre_all), d_pre_all)
    )
    ug_there = dp_swap(ug_there, 1)
    dx_all = dot(d_pre_all, w_pair, LAST).astype(BF)
    dx_terms = lax.optimization_barrier([z_chunk(dx_all, k) for k in range(n_row)])
    grads = grad_columns(core, x_t, d_pre_all, ug_there)
    y_up, y_down = grads[half:], grads[: half + feat]
    y_later, mixed_all = lax.optimization_barrier(((y_up, y_down), mixed_all))
    y_up, y_down = y_shift(y_up, 1), y_shift(y_down, -1)
    out_all = dot(mixed_all, w_output).astype(BF)
    m_keep, m_send = halves(mixed_all, core_at, 1)
    og_there = dp_swap(dot(m_send.T, g_panel).astype(BF), 1)
    og_sum = dot(m_keep.T, g_panel) + og_there.astype(F32)
    og_mid = og_sum.shape[0] // 2
    og_low, og_high = og_sum[:og_mid].astype(BF), og_sum[og_mid:].astype(BF)
    part = feat // 2

    out_terms = lax.optimization_barrier([z_chunk(out_all, k) for k in range(n_row)])

    def term(k):
        return dx_terms[k].astype(F32)

    def out_term(k):
        return out_terms[k].astype(F32)

    def message(dx, out):
        return jnp.concatenate([dx.astype(BF), out.astype(BF)], axis=1)

    to_up, to_down = term(3), term(-3)
    to_up = jnp.concatenate([to_up[:, :feat] + up.astype(F32), to_up[:, feat:]], axis=1)
    to_down = jnp.concatenate([to_down[:, :feat], to_down[:, feat:] + down.astype(F32)], axis=1)
    out_far = out_term(4)
    up = z_shift(message(to_up, out_far[:, :part]), 1)
    down = z_shift(message(to_down, out_far[:, part:]), -1)
    wide = 2 * feat
    out_up, out_down = out_term(3), out_term(-3)
    out_up = jnp.concatenate([out_up[:, :part] + up[:, wide:].astype(F32), out_up[:, part:]], axis=1)
    out_down = jnp.concatenate([out_down[:, :part], out_down[:, part:] + down[:, wide:].astype(F32)], axis=1)
    up, down = (
        z_shift(message(term(2) + up[:, :wide].astype(F32), out_up), 1),
        z_shift(message(term(-2) + down[:, :wide].astype(F32), out_down), -1),
    )
    up, down, y_up, y_down, og_low, og_high = lax.optimization_barrier(
        (up, down, y_up, y_down, og_low, og_high)
    )
    far_up, far_down = y_shift(y_up[feat:], 1), y_shift(y_down[:half], -1)
    og_low, og_high = y_shift(og_low, -1), y_shift(og_high, 1)
    to_up = message(term(1) + up[:, :wide].astype(F32), out_term(2) + up[:, wide:].astype(F32))
    to_down = message(term(-1) + down[:, :wide].astype(F32), out_term(-2) + down[:, wide:].astype(F32))
    up, down = z_shift(to_up, 1), z_shift(to_down, -1)
    ug_cross = y_up[:feat].astype(F32) + y_down[half:].astype(F32)
    rows = term(0) + up[:, :wide].astype(F32) + down[:, :wide].astype(F32)
    dx_other = ylo_swap(rows[:, feat:].astype(BF))
    out_up = z_shift((out_term(1) + up[:, wide:].astype(F32)).astype(BF), 1)
    out_down = z_shift((out_term(-1) + down[:, wide:].astype(F32)).astype(BF), -1)
    out_rows = out_term(0) + out_up.astype(F32) + out_down.astype(F32)

    ug_stay = jnp.concatenate(
        [
            y_later[1][:half].astype(F32) + far_down.astype(F32),
            y_later[0][feat:].astype(F32) + far_up.astype(F32),
        ],
        axis=0,
    )
    ug_half = jnp.concatenate([ug_stay.astype(BF), ug_cross.astype(BF)], axis=1)
    og_low, og_high = y_shift(og_low, -1), y_shift(og_high, 1)
    og_half = jnp.concatenate([og_low, og_high], axis=0).astype(F32) + og_sum
    og_half = og_half.astype(BF)
    ug_there, og_there = dp_swap(ug_half, 1), dp_swap(og_half, 1)
    dx_own = (rows[:, :feat] + dx_other.astype(F32) + g_own.astype(F32)).astype(BF)
    y_own = (out_rows + x_own.astype(F32)).astype(BF)
    back = dot(own_pick, jnp.concatenate([y_own, dx_own], axis=1), FIRST).astype(BF)
    home = dp_exchange(back, send_count)
    layer_out = dot(send_pick, home[:, :feat], FIRST).astype(BF)
    event_grad = dot(send_pick, home[:, feat:], FIRST).astype(BF)
    output_grad = jnp.where(
        core_at == 0,
        jnp.concatenate([og_half, og_there], axis=0),
        jnp.concatenate([og_there, og_half], axis=0),
    ).astype(F32)
    ylo = ylo_at.astype(jnp.int32)[None]
    uvqk_grad = place_halves(jnp.concatenate([core, ylo]), ug_half)
    uvqk_grad = place_halves(jnp.concatenate([1 - core, ylo]), ug_there, uvqk_grad)
    return (layer_out, event_grad, uvqk_grad, output_grad)


def solution(mesh):
    in_specs = (
        P(("dp", "row"), "col"),
        P(("dp", "row"), "col"),
        P("col", "row"),
        P("row", "col"),
        P(),
        P(),
    )
    out_specs = (P(("dp", "row"), "col"), P(("dp", "row"), "col"), P("col", "row"), P("row", "col"))
    return jax.shard_map(local, mesh=mesh, in_specs=in_specs, out_specs=out_specs, check_vma=False)
```

```python
import jax
import jax.numpy as jnp
from jax import lax
from jax.experimental import pallas as pl
from jax.experimental.pallas import tpu as pltpu
from jax.sharding import PartitionSpec as P

HEADDIM = 128
HMAX = 64
EPS = 1e-06
LAST = (((1,), (1,)), ((), ()))
FIRST = (((0,), (0,)), ((), ()))
BF = jnp.bfloat16
F32 = jnp.float32

N_X = 4
N_Z = 8


def x_shift(value, step):
    pairs = [(c, (c // 2 + step) % N_X * 2 + c % 2) for c in range(2 * N_X)]
    return lax.ppermute(value, "col", pairs)


def z_shift(value, step):
    return lax.ppermute(value, "row", [(r, (r + step) % N_Z) for r in range(N_Z)])


def ylo_swap(value):
    return lax.ppermute(value, "col", [(c, c ^ 1) for c in range(2 * N_X)])


def dp_swap(value, bits):
    return lax.ppermute(value, "dp", [(d, d ^ bits) for d in range(4)])


def y_shift(value, step):
    pairs = []
    for d in range(4):
        for c in range(2 * N_X):
            y = (d // 2 * 2 + c % 2 + step) % 4
            pairs.append((d * 2 * N_X + c, (y // 2 * 2 + d % 2) * 2 * N_X + c // 2 * 2 + y % 2))
    return lax.ppermute(value, ("dp", "col"), pairs)


def place_kernel(count, at_ref, *refs):
    blocks, outs = refs[:count], refs[-2:]
    cut = outs[0].shape[1]
    k = pl.program_id(0)
    for i, block in enumerate(blocks):

        @pl.when(k == i)
        def _(block=block):
            outs[0][...] = block[:, :cut]
            outs[1][...] = block[:, cut:]

    @pl.when(k == count)
    def _():
        outs[0][...] = jnp.zeros(outs[0].shape, BF)
        outs[1][...] = jnp.zeros(outs[1].shape, BF)


def place_blocks(at, blocks, cut):
    rows, width = blocks[0].shape
    size = len(blocks) + 1
    order = blocks[:4] + blocks[4:]

    def where(k, at):
        return ((at[0] + jnp.where(k < 4, k, jnp.where(k < size - 1, k + 1, 4))) % size, 0)

    return pl.pallas_call(
        lambda *refs: place_kernel(len(order), *refs),
        grid_spec=pltpu.PrefetchScalarGridSpec(
            num_scalar_prefetch=1,
            grid=(size,),
            in_specs=[pl.BlockSpec((rows, width), lambda k, at: (0, 0)) for _ in order],
            out_specs=[pl.BlockSpec((rows, cut), where), pl.BlockSpec((rows, width - cut), where)],
        ),
        out_shape=[
            jax.ShapeDtypeStruct((size * rows, cut), BF),
            jax.ShapeDtypeStruct((size * rows, width - cut), BF),
        ],
        cost_estimate=pl.CostEstimate(flops=0, bytes_accessed=2 * size * rows * width * 2, transcendentals=0),
    )(at, *order)


def place_far_kernel(at_ref, low_ref, high_ref, x_in, g_in, x_out, g_out):
    half, cut = low_ref.shape[0], x_out.shape[1]
    x_out[:half], x_out[half:] = low_ref[:, :cut], high_ref[:, :cut]
    g_out[:half], g_out[half:] = low_ref[:, cut:], high_ref[:, cut:]


def place_far(at, low, high, panels):
    rows, width = 2 * low.shape[0], low.shape[1]
    size = panels[0].shape[0] // rows
    where = lambda i, at: ((at[0] + size // 2) % size, 0)
    return pl.pallas_call(
        place_far_kernel,
        grid_spec=pltpu.PrefetchScalarGridSpec(
            num_scalar_prefetch=1,
            grid=(1,),
            in_specs=[pl.BlockSpec(low.shape, lambda i, at: (0, 0))] * 2
            + [pl.BlockSpec(memory_space=pl.ANY)] * 2,
            out_specs=[pl.BlockSpec((rows, panel.shape[1]), where) for panel in panels],
        ),
        out_shape=[jax.ShapeDtypeStruct(panel.shape, BF) for panel in panels],
        input_output_aliases={3: 0, 4: 1},
        cost_estimate=pl.CostEstimate(flops=0, bytes_accessed=4 * rows * width, transcendentals=0),
    )(at, low, high, *panels)


def product_kernel(left_ref, right_ref, out_ref):
    out_ref[...] = dot(left_ref[...], right_ref[...]).astype(BF)


def product(left, right, step=256):
    rows, depth = left.shape
    columns = right.shape[1]
    return pl.pallas_call(
        product_kernel,
        grid=(columns // step,),
        in_specs=[
            pl.BlockSpec((rows, depth), lambda i: (0, 0)),
            pl.BlockSpec((depth, step), lambda i: (0, i)),
        ],
        out_specs=pl.BlockSpec((rows, step), lambda i: (0, i)),
        out_shape=jax.ShapeDtypeStruct((rows, columns), BF),
        compiler_params=pltpu.CompilerParams(vmem_limit_bytes=24 << 20),
        cost_estimate=pl.CostEstimate(
            flops=2 * rows * depth * columns, bytes_accessed=6 << 20, transcendentals=0
        ),
    )(left, right)


def silu_slope(inputs):
    sigma = jax.nn.sigmoid(inputs)
    return sigma * (1.0 + inputs * (1.0 - sigma))


def history_starts(lengths, width):
    history_ends = jnp.cumsum(lengths, axis=1)
    places = jnp.arange(width, dtype=jnp.int32)
    earlier = (history_ends[:, None, :] <= places[None, :, None]).astype(jnp.int32)
    return jnp.sum(lengths[:, None, :] * earlier, axis=2)


def dot(left, right, dims=(((1,), (0,)), ((), ())), precision=None):
    return lax.dot_general(left, right, dims, precision=precision, preferred_element_type=F32)


def forward_kernel(starts_ref, pre_ref, *refs):
    n_part, tok, width = pre_ref.shape
    heads = width // (4 * HEADDIM)
    dmix_refs, outs = refs[:n_part], refs[n_part:]
    pre_out, act_out, logit_out, prob_out, att_out, dmix_out, sum_out = outs
    pre = pre_ref[0].astype(F32)
    dmix = dmix_refs[0][...].astype(F32)
    for part in range(1, n_part):
        pre = pre + pre_ref[part].astype(F32)
        dmix = dmix + dmix_refs[part][...].astype(F32)
    pre_out[...] = pre
    dmix_out[...] = dmix
    act = (pre / (1.0 + jnp.exp(-pre))).astype(BF)
    act_out[...] = act
    query = lax.broadcasted_iota(jnp.int32, (tok, tok), 0)
    key = lax.broadcasted_iota(jnp.int32, (tok, tok), 1)
    visible = (key <= query) & (key >= starts_ref[...])
    totals = [0.0, 0.0, 0.0, 0.0]
    for head in range(heads):
        at = head * 4 * HEADDIM
        gate, value, quer, keyk = [act[:, at + i * HEADDIM : at + (i + 1) * HEADDIM] for i in range(4)]
        logit = dot(quer, keyk, LAST) * HEADDIM ** (-0.5)
        logit_out[head] = logit
        prob = jnp.where(visible, logit / (1.0 + jnp.exp(-logit)) * (1.0 / HMAX), 0.0).astype(BF)
        prob_out[head] = prob
        att = dot(prob, value)
        own = pl.ds(head * HEADDIM, HEADDIM)
        att_out[:, own] = att
        dnorm = dmix[:, head * HEADDIM : (head + 1) * HEADDIM] * gate.astype(F32)
        for i, term in enumerate((att, att * att, dnorm, dnorm * att)):
            totals[i] = totals[i] + term
    table = jnp.zeros((tok, tok), F32)
    for i, total in enumerate(totals):
        table = jnp.where(key == i, jnp.sum(total, axis=1, keepdims=True), table)
    sums = table.T[:8]
    for copy in range(sum_out.shape[0]):
        sum_out[copy] = sums


def backward_kernel(total_width, sum_ref, act_ref, slope_ref, lslope_ref, prob_ref, att_ref, dmix_ref, mixed_out, dpre_out):
    tok, width = act_ref.shape
    heads = width // (4 * HEADDIM)
    means = sum_ref[0]
    for part in range(1, sum_ref.shape[0]):
        means = means + sum_ref[part]
    means = means * (1.0 / total_width)
    row = lax.broadcasted_iota(jnp.int32, (tok, tok), 0)
    col = lax.broadcasted_iota(jnp.int32, (tok, tok), 1)
    cols = dot((row == col).astype(F32), means, LAST, lax.Precision.HIGHEST)
    mean, second, grad_one, grad_att = [cols[:, i : i + 1] for i in range(4)]
    rstd = lax.rsqrt(second - mean * mean + EPS)
    grad_two = (grad_att - mean * grad_one) * rstd
    for head in range(heads):
        at = head * 4 * HEADDIM
        gate, value, quer, keyk = [act_ref[:, at + i * HEADDIM : at + (i + 1) * HEADDIM] for i in range(4)]
        own = pl.ds(head * HEADDIM, HEADDIM)
        normed = (att_ref[:, own] - mean) * rstd
        dmix = dmix_ref[:, own]
        gate = gate.astype(F32)
        mixed_out[:, own] = (normed * gate).astype(BF)
        datt = (rstd * (dmix * gate - grad_one - normed * grad_two)).astype(BF)
        dvalue = dot(prob_ref[head], datt, FIRST)
        dlogit = (dot(datt, value, LAST) * lslope_ref[head]).astype(BF)
        dquer = dot(dlogit, keyk)
        dkey = dot(dlogit, quer, FIRST)
        for i, term in enumerate((dmix * normed, dvalue, dquer, dkey)):
            place = pl.ds(at + i * HEADDIM, HEADDIM)
            dpre_out[:, place] = (term * slope_ref[:, place]).astype(BF)


def attention_forward(starts, pre_parts, dmix_parts, tok, copies):
    n_part, rows, width = pre_parts.shape
    heads = width // (4 * HEADDIM)
    head_cols = heads * HEADDIM
    owners = rows // tok
    square = lambda kind: jax.ShapeDtypeStruct((owners, heads, tok, tok), kind)
    square_spec = pl.BlockSpec((None, heads, tok, tok), lambda b: (b, 0, 0, 0))
    wide_spec = pl.BlockSpec((tok, width), lambda b: (b, 0))
    thin_spec = pl.BlockSpec((tok, head_cols), lambda b: (b, 0))
    return pl.pallas_call(
        forward_kernel,
        grid=(owners,),
        in_specs=[
            pl.BlockSpec((tok, 1), lambda b: (b, 0)),
            pl.BlockSpec((n_part, tok, width), lambda b: (0, b, 0)),
        ]
        + [thin_spec] * n_part,
        out_specs=[wide_spec, wide_spec, square_spec, square_spec, thin_spec, thin_spec, pl.BlockSpec((copies, 8, tok), lambda b: (0, 0, b))],
        out_shape=[
            jax.ShapeDtypeStruct((rows, width), F32),
            jax.ShapeDtypeStruct((rows, width), BF),
            square(F32),
            square(BF),
            jax.ShapeDtypeStruct((rows, head_cols), F32),
            jax.ShapeDtypeStruct((rows, head_cols), F32),
            jax.ShapeDtypeStruct((copies, 8, rows), F32),
        ],
        cost_estimate=pl.CostEstimate(flops=4 * rows * tok * head_cols, bytes_accessed=8 << 20, transcendentals=rows * width),
    )(starts, pre_parts, *dmix_parts)


def attention_backward(sums, act, slope, lslope, prob, att, dmix, tok, total_width):
    rows, width = act.shape
    heads = width // (4 * HEADDIM)
    head_cols = heads * HEADDIM
    owners = rows // tok
    square_spec = pl.BlockSpec((None, heads, tok, tok), lambda b: (b, 0, 0, 0))
    wide_spec = pl.BlockSpec((tok, width), lambda b: (b, 0))
    thin_spec = pl.BlockSpec((tok, head_cols), lambda b: (b, 0))
    return pl.pallas_call(
        lambda *refs: backward_kernel(total_width, *refs),
        grid=(owners,),
        in_specs=[
            pl.BlockSpec((sums.shape[0], 8, tok), lambda b: (0, 0, b)),
            wide_spec, wide_spec, square_spec, square_spec, thin_spec, thin_spec,
        ],
        out_specs=[thin_spec, wide_spec],
        out_shape=[
            jax.ShapeDtypeStruct((rows, head_cols), BF),
            jax.ShapeDtypeStruct((rows, width), BF),
        ],
        cost_estimate=pl.CostEstimate(flops=8 * rows * tok * head_cols, bytes_accessed=4 << 20, transcendentals=rows),
    )(sums, act, slope, lslope, prob, att, dmix)


def widen_kernel(place_ref, half_ref, *refs):
    refs[-1][...] = half_ref[...].astype(F32)


def place_halves(place, value, into=None):
    rows, width = value.shape
    extra = [] if into is None else [into]
    return pl.pallas_call(
        widen_kernel,
        grid_spec=pltpu.PrefetchScalarGridSpec(
            num_scalar_prefetch=1,
            grid=(2,),
            in_specs=[pl.BlockSpec((rows, width // 2), lambda h, place: (0, h ^ place[1]))]
            + [pl.BlockSpec(memory_space=pl.ANY)] * len(extra),
            out_specs=pl.BlockSpec((rows, width // 2), lambda h, place: (0, 2 * h + place[0])),
        ),
        out_shape=jax.ShapeDtypeStruct((rows, 2 * width), F32),
        input_output_aliases={2: 0} if extra else {},
        cost_estimate=pl.CostEstimate(flops=0, bytes_accessed=rows * width * 6, transcendentals=0),
    )(place, value, *extra)


def grad_kernel(core_ref, x_ref, d_ref, *refs):
    out = refs[-1]
    grad = dot(x_ref[...], d_ref[...])
    if len(refs) == 1:
        out[...] = grad.astype(BF)
    else:
        there_ref, low_ref, high_ref = refs[:3]
        low, mid = low_ref.shape[0], grad.shape[0]
        out[:low] = low_ref[...]
        out[low : low + mid] = (grad + there_ref[...].astype(F32)).astype(BF)
        out[low + mid :] = high_ref[...]


def grad_columns(core, x_t, d_all, *more):
    depth, width = d_all.shape
    step = width // 4
    rows = x_t.shape[0] + sum(piece.shape[0] for piece in more[1:])
    return pl.pallas_call(
        grad_kernel,
        grid_spec=pltpu.PrefetchScalarGridSpec(
            num_scalar_prefetch=1,
            grid=(2,),
            in_specs=[
                pl.BlockSpec(x_t.shape, lambda i, core: (0, 0)),
                pl.BlockSpec((depth, step), lambda i, core: (0, core[0] * 2 + i)),
            ]
            + [pl.BlockSpec((piece.shape[0], step), lambda i, core: (0, i)) for piece in more],
            out_specs=pl.BlockSpec((rows, step), lambda i, core: (0, i)),
        ),
        out_shape=jax.ShapeDtypeStruct((rows, 2 * step), BF),
        compiler_params=pltpu.CompilerParams(vmem_limit_bytes=24 << 20),
        cost_estimate=pl.CostEstimate(
            flops=4 * x_t.size * step, bytes_accessed=4 << 20, transcendentals=0
        ),
    )(core, x_t, d_all, *more)


def x_exchange(blocks):
    groups = [[2 * x + y for x in range(N_X)] for y in range(2)]
    return lax.all_to_all(blocks, "col", 0, 0, axis_index_groups=groups, tiled=True)


def head_groups_gather(value):
    groups = [[r * 2 * N_X + 2 * x + y for r in range(N_Z) for y in range(2)] for x in range(N_X)]
    return lax.all_to_all(value, ("row", "col"), 0, 0, axis_index_groups=groups, tiled=True)


def halves(array, which, axis):
    size = array.shape[axis] // 2
    return (
        lax.dynamic_slice_in_dim(array, which * size, size, axis),
        lax.dynamic_slice_in_dim(array, (1 - which) * size, size, axis),
    )


def dp_exchange(value, count):
    parts = [value[:count]]
    parts += [dp_swap(value[j * count : (j + 1) * count], j) for j in range(1, 4)]
    return jnp.concatenate(parts, axis=0)


def local(events, out_grad, w_uvqk, w_output, hist_len, token_slot):
    n_dp, n_row, n_col = 4, N_Z, 2 * N_X
    tok_own, feat = events.shape
    send_count = tok_own // n_dp
    dp_at = lax.axis_index("dp")
    row_at = lax.axis_index("row")
    col_at = lax.axis_index("col")
    x_at, ylo_at, core_at = col_at // 2, col_at % 2, dp_at % 2
    owner_self = dp_at * n_row + row_at
    places = jnp.arange(tok_own, dtype=jnp.int32)

    events_other = ylo_swap(events)
    slots = token_slot.reshape(n_dp, n_row, tok_own)
    src_slots = lax.dynamic_index_in_dim(slots, row_at, 1, keepdims=False)
    own_slots = lax.dynamic_index_in_dim(src_slots, dp_at, 0, keepdims=False)
    send_rank = jnp.sum((own_slots[None, :] < own_slots[:, None]).astype(jnp.int32), axis=1)
    target = own_slots // (tok_own * n_row)
    send_place = (target ^ dp_at) * send_count + send_rank - target * send_count
    send_pick = (send_place[None, :] == places[:, None]).astype(BF)
    x_send = dot(send_pick, jnp.concatenate([events, events_other, out_grad], axis=1)).astype(BF)
    xg_recv = dp_exchange(x_send, send_count)
    sources = jnp.arange(n_dp, dtype=jnp.int32)
    to_self = src_slots // tok_own == owner_self
    before = jnp.sum(
        (to_self[:, None, :] & (src_slots[:, None, :] < src_slots[:, :, None])).astype(jnp.int32),
        axis=2,
    )
    recv_row = (sources ^ dp_at)[:, None] * send_count + before
    local_place = src_slots - owner_self * tok_own
    hits = to_self[:, :, None] & (recv_row[:, :, None] == places[None, None, :])
    row_place = jnp.sum(jnp.where(hits, local_place[:, :, None], 0), axis=(0, 1))
    own_pick = (row_place[None, :] == places[:, None]).astype(BF)
    xg_recv, w_later = lax.optimization_barrier((xg_recv, w_uvqk))
    xg_own = dot(own_pick, xg_recv).astype(BF)
    x_own, g_own = xg_own[:, :feat], xg_own[:, 2 * feat :]

    w_keep, w_send = halves(w_later, ylo_at, 1)
    w_pair = jnp.concatenate([w_keep, ylo_swap(w_send)], axis=0)

    tokens = n_row * tok_own
    rows_half = tok_own // 2
    ups, downs = [xg_own], [xg_own]
    for _ in range(3):
        ups, downs = ups + [z_shift(ups[-1], 1)], downs + [z_shift(downs[-1], -1)]
    far_low, far_high = z_shift(ups[3][:rows_half], 1), z_shift(downs[3][rows_half:], -1)
    row_place_at = row_at.astype(jnp.int32)[None]
    near_panels = place_blocks(row_place_at, [xg_own] + downs[1:] + ups[:0:-1], 2 * feat)
    wo_keep, wo_send = halves(w_output, ylo_at, 0)
    d_other = ylo_swap(dot(near_panels[1], wo_send, LAST).astype(BF))
    x_panel, g_panel = place_far(row_place_at, far_low, far_high, near_panels)
    g_far = jnp.concatenate([far_low[:, 2 * feat :], far_high[:, 2 * feat :]], axis=0)
    d_far = ylo_swap(dot(g_far, wo_send, LAST).astype(BF))
    rows_pair = 2 * tok_own

    def x_chunk(panel, k):
        return lax.dynamic_slice_in_dim(panel, (x_at + k) % N_X * rows_pair, rows_pair, 0)

    pre_part = product(x_panel, w_pair)
    pre_parts = x_exchange(pre_part.reshape(N_X, rows_pair, -1))
    far_here = jnp.arange(n_row) == (row_at + n_row // 2) % n_row
    d_far = jnp.where(far_here[:, None, None], d_far[None].astype(F32), 0.0)
    d_pair = dot(g_panel, wo_keep, LAST) + d_other.astype(F32) + d_far.reshape(d_other.shape)
    d_pair = d_pair.astype(BF)
    dmix_parts = [x_chunk(d_pair, 0)] + [x_shift(x_chunk(d_pair, k), k) for k in (1, -1, 2)]

    lengths = lax.dynamic_slice_in_dim(hist_len, dp_at * n_row + x_at * 2, 2, 0)
    starts = history_starts(lengths, tok_own).reshape(rows_pair, 1)
    preact, act, logits, probs, att, d_mixed, sums = attention_forward(
        starts, pre_parts, dmix_parts, tok_own, 2 * n_row
    )
    sums = head_groups_gather(sums)
    slope = silu_slope(preact)
    keys = jnp.arange(tok_own, dtype=jnp.int32)
    visible = (keys[None, None, :] >= starts.reshape(2, tok_own, 1)) & (
        keys[None, None, :] <= keys[None, :, None]
    )
    lslope = jnp.where(
        visible[:, None], silu_slope(logits) * (HEADDIM ** (-0.5) / HMAX), 0.0
    )
    total_width = att.shape[1] * n_row * 2
    mixed, d_pre = attention_backward(
        sums, act, slope, lslope, probs, att, d_mixed, tok_own, total_width
    )

    x_up, x_down = x_shift(d_pre, 1), x_shift(d_pre, -1)
    mixed_there = ylo_swap(mixed)
    mixed = jnp.where(
        ylo_at == 0,
        jnp.concatenate([mixed, mixed_there], axis=1),
        jnp.concatenate([mixed_there, mixed], axis=1),
    )
    x_up, x_down, mixed = lax.optimization_barrier((x_up, x_down, mixed))
    far_low, far_high = x_shift(x_up[:tok_own], 1), x_shift(x_down[tok_own:], -1)
    d_pre_all = pre_parts
    for k, piece in ((0, d_pre), (3, x_up), (1, x_down)):
        d_pre_all = lax.dynamic_update_slice(d_pre_all, piece[None], ((x_at + k) % N_X, 0, 0))
    d_far = jnp.concatenate([far_low, far_high], axis=0)
    d_pre_all = lax.dynamic_update_slice(d_pre_all, d_far[None], ((x_at + 2) % N_X, 0, 0))
    d_pre_all = d_pre_all.reshape(tokens, -1)
    mixed_all = x_exchange(jnp.broadcast_to(mixed[None], (N_X,) + mixed.shape))
    mixed_all = mixed_all.reshape(tokens, -1)

    def z_chunk(panel, k):
        return lax.dynamic_slice_in_dim(panel, (row_at + k) % n_row * tok_own, tok_own, 0)

    far = dot(z_chunk(d_pre_all, 4), w_pair, LAST).astype(BF)
    far, d_pre_all = lax.optimization_barrier((far, d_pre_all))
    up, down = z_shift(far[:, :feat], 1), z_shift(far[:, feat:], -1)

    half = feat // 2
    x_t = x_panel.T
    x_t = jnp.concatenate([x_t[:half], x_t[feat:], x_t[half:feat]], axis=0)
    x_t = lax.optimization_barrier(x_t)
    core = core_at.astype(jnp.int32)[None]
    ug_there, d_pre_all = lax.optimization_barrier(
        (grad_columns(1 - core, x_t, d_pre_all), d_pre_all)
    )
    ug_there = dp_swap(ug_there, 1)
    m_keep, m_send = halves(mixed_all, core_at, 1)
    og_there = dp_swap(dot(m_send.T, g_panel).astype(BF), 1)
    og_sum = dot(m_keep.T, g_panel) + og_there.astype(F32)
    og_mid = og_sum.shape[0] // 2
    og_low, og_high = og_sum[:og_mid].astype(BF), og_sum[og_mid:].astype(BF)
    grads = grad_columns(core, x_t, d_pre_all, ug_there, og_low, og_high)

    dx_all = dot(d_pre_all, w_pair, LAST).astype(BF)
    out_all = dot(mixed_all, w_output).astype(BF)
    part = feat // 2

    dx_terms = lax.optimization_barrier([z_chunk(dx_all, k) for k in range(n_row)])
    out_terms = lax.optimization_barrier([z_chunk(out_all, k) for k in range(n_row)])

    def term(k):
        return dx_terms[k].astype(F32)

    def out_term(k):
        return out_terms[k].astype(F32)

    def message(dx, out):
        return jnp.concatenate([dx.astype(BF), out.astype(BF)], axis=1)

    to_up, to_down = term(3), term(-3)
    to_up = jnp.concatenate([to_up[:, :feat] + up.astype(F32), to_up[:, feat:]], axis=1)
    to_down = jnp.concatenate([to_down[:, :feat], to_down[:, feat:] + down.astype(F32)], axis=1)
    out_far = out_term(4)
    up = z_shift(message(to_up, out_far[:, :part]), 1)
    down = z_shift(message(to_down, out_far[:, part:]), -1)
    y_up, y_down = grads[og_mid + half :], grads[: og_mid + half + feat]
    up, down, y_later = lax.optimization_barrier((up, down, (y_up, y_down)))
    y_up, y_down = y_shift(y_up, 1), y_shift(y_down, -1)
    wide = 2 * feat
    out_up, out_down = out_term(3), out_term(-3)
    out_up = jnp.concatenate([out_up[:, :part] + up[:, wide:].astype(F32), out_up[:, part:]], axis=1)
    out_down = jnp.concatenate([out_down[:, :part], out_down[:, part:] + down[:, wide:].astype(F32)], axis=1)
    up, down = (
        z_shift(message(term(2) + up[:, :wide].astype(F32), out_up), 1),
        z_shift(message(term(-2) + down[:, :wide].astype(F32), out_down), -1),
    )
    up, down, y_up, y_down = lax.optimization_barrier((up, down, y_up, y_down))
    far_up, far_down = y_shift(y_up[feat:], 1), y_shift(y_down[: og_mid + half], -1)
    to_up = message(term(1) + up[:, :wide].astype(F32), out_term(2) + up[:, wide:].astype(F32))
    to_down = message(term(-1) + down[:, :wide].astype(F32), out_term(-2) + down[:, wide:].astype(F32))
    up, down = z_shift(to_up, 1), z_shift(to_down, -1)
    ug_cross = y_up[:feat].astype(F32) + y_down[og_mid + half :].astype(F32)
    rows = term(0) + up[:, :wide].astype(F32) + down[:, :wide].astype(F32)
    dx_other = ylo_swap(rows[:, feat:].astype(BF))
    out_up = z_shift((out_term(1) + up[:, wide:].astype(F32)).astype(BF), 1)
    out_down = z_shift((out_term(-1) + down[:, wide:].astype(F32)).astype(BF), -1)
    out_rows = out_term(0) + out_up.astype(F32) + out_down.astype(F32)

    ug_stay = jnp.concatenate(
        [
            y_later[1][og_mid : og_mid + half].astype(F32) + far_down[og_mid:].astype(F32),
            y_later[0][feat:-og_mid].astype(F32) + far_up[:half].astype(F32),
        ],
        axis=0,
    )
    ug_half = jnp.concatenate([ug_stay.astype(BF), ug_cross.astype(BF)], axis=1)
    og_half = jnp.concatenate(
        [
            og_sum[:og_mid] + far_down[:og_mid].astype(F32),
            og_sum[og_mid:] + far_up[half:].astype(F32),
        ],
        axis=0,
    ).astype(BF)
    ug_there, og_there = dp_swap(ug_half, 1), dp_swap(og_half, 1)
    dx_own = (rows[:, :feat] + dx_other.astype(F32) + g_own.astype(F32)).astype(BF)
    y_own = (out_rows + x_own.astype(F32)).astype(BF)
    back = dot(own_pick, jnp.concatenate([y_own, dx_own], axis=1), FIRST).astype(BF)
    home = dp_exchange(back, send_count)
    layer_out = dot(send_pick, home[:, :feat], FIRST).astype(BF)
    event_grad = dot(send_pick, home[:, feat:], FIRST).astype(BF)
    output_grad = jnp.where(
        core_at == 0,
        jnp.concatenate([og_half, og_there], axis=0),
        jnp.concatenate([og_there, og_half], axis=0),
    ).astype(F32)
    ylo = ylo_at.astype(jnp.int32)[None]
    uvqk_grad = place_halves(jnp.concatenate([core, ylo]), ug_half)
    uvqk_grad = place_halves(jnp.concatenate([1 - core, ylo]), ug_there, uvqk_grad)
    return (layer_out, event_grad, uvqk_grad, output_grad)


def solution(mesh):
    in_specs = (
        P(("dp", "row"), "col"),
        P(("dp", "row"), "col"),
        P("col", "row"),
        P("row", "col"),
        P(),
        P(),
    )
    out_specs = (P(("dp", "row"), "col"), P(("dp", "row"), "col"), P("col", "row"), P("row", "col"))
    return jax.shard_map(local, mesh=mesh, in_specs=in_specs, out_specs=out_specs, check_vma=False)
```

```python
import jax
import jax.numpy as jnp
from jax import lax
from jax.experimental import pallas as pl
from jax.experimental.pallas import tpu as pltpu
from jax.sharding import PartitionSpec as P

HEADDIM = 128
HMAX = 64
EPS = 1e-06
LAST = (((1,), (1,)), ((), ()))
FIRST = (((0,), (0,)), ((), ()))
BF = jnp.bfloat16
F32 = jnp.float32

N_X = 4
N_Z = 8


def x_shift(value, step):
    pairs = [(c, (c // 2 + step) % N_X * 2 + c % 2) for c in range(2 * N_X)]
    return lax.ppermute(value, "col", pairs)


def z_shift(value, step):
    return lax.ppermute(value, "row", [(r, (r + step) % N_Z) for r in range(N_Z)])


def ylo_swap(value):
    return lax.ppermute(value, "col", [(c, c ^ 1) for c in range(2 * N_X)])


def dp_swap(value, bits):
    return lax.ppermute(value, "dp", [(d, d ^ bits) for d in range(4)])


def y_shift(value, step):
    pairs = []
    for d in range(4):
        for c in range(2 * N_X):
            y = (d // 2 * 2 + c % 2 + step) % 4
            pairs.append((d * 2 * N_X + c, (y // 2 * 2 + d % 2) * 2 * N_X + c // 2 * 2 + y % 2))
    return lax.ppermute(value, ("dp", "col"), pairs)


def place_kernel(count, at_ref, *refs):
    blocks, outs = refs[:count], refs[-2:]
    cut = outs[0].shape[1]
    k = pl.program_id(0)
    for i, block in enumerate(blocks):

        @pl.when(k == i)
        def _(block=block):
            outs[0][...] = block[:, :cut]
            outs[1][...] = block[:, cut:]

    @pl.when(k == count)
    def _():
        outs[0][...] = jnp.zeros(outs[0].shape, BF)
        outs[1][...] = jnp.zeros(outs[1].shape, BF)


def place_blocks(at, blocks, cut):
    rows, width = blocks[0].shape
    size = len(blocks) + 1
    order = blocks[:4] + blocks[4:]

    def where(k, at):
        return ((at[0] + jnp.where(k < 4, k, jnp.where(k < size - 1, k + 1, 4))) % size, 0)

    return pl.pallas_call(
        lambda *refs: place_kernel(len(order), *refs),
        grid_spec=pltpu.PrefetchScalarGridSpec(
            num_scalar_prefetch=1,
            grid=(size,),
            in_specs=[pl.BlockSpec((rows, width), lambda k, at: (0, 0)) for _ in order],
            out_specs=[pl.BlockSpec((rows, cut), where), pl.BlockSpec((rows, width - cut), where)],
        ),
        out_shape=[
            jax.ShapeDtypeStruct((size * rows, cut), BF),
            jax.ShapeDtypeStruct((size * rows, width - cut), BF),
        ],
        cost_estimate=pl.CostEstimate(flops=0, bytes_accessed=2 * size * rows * width * 2, transcendentals=0),
    )(at, *order)


def place_far_kernel(at_ref, low_ref, high_ref, x_in, g_in, x_out, g_out):
    half, cut = low_ref.shape[0], x_out.shape[1]
    x_out[:half], x_out[half:] = low_ref[:, :cut], high_ref[:, :cut]
    g_out[:half], g_out[half:] = low_ref[:, cut:], high_ref[:, cut:]


def place_far(at, low, high, panels):
    rows, width = 2 * low.shape[0], low.shape[1]
    size = panels[0].shape[0] // rows
    where = lambda i, at: ((at[0] + size // 2) % size, 0)
    return pl.pallas_call(
        place_far_kernel,
        grid_spec=pltpu.PrefetchScalarGridSpec(
            num_scalar_prefetch=1,
            grid=(1,),
            in_specs=[pl.BlockSpec(low.shape, lambda i, at: (0, 0))] * 2
            + [pl.BlockSpec(memory_space=pl.ANY)] * 2,
            out_specs=[pl.BlockSpec((rows, panel.shape[1]), where) for panel in panels],
        ),
        out_shape=[jax.ShapeDtypeStruct(panel.shape, BF) for panel in panels],
        input_output_aliases={3: 0, 4: 1},
        cost_estimate=pl.CostEstimate(flops=0, bytes_accessed=4 * rows * width, transcendentals=0),
    )(at, low, high, *panels)


def product_kernel(left_ref, right_ref, out_ref):
    out_ref[...] = dot(left_ref[...], right_ref[...]).astype(BF)


def product(left, right, step=256):
    rows, depth = left.shape
    columns = right.shape[1]
    return pl.pallas_call(
        product_kernel,
        grid=(columns // step,),
        in_specs=[
            pl.BlockSpec((rows, depth), lambda i: (0, 0)),
            pl.BlockSpec((depth, step), lambda i: (0, i)),
        ],
        out_specs=pl.BlockSpec((rows, step), lambda i: (0, i)),
        out_shape=jax.ShapeDtypeStruct((rows, columns), BF),
        compiler_params=pltpu.CompilerParams(vmem_limit_bytes=24 << 20),
        cost_estimate=pl.CostEstimate(
            flops=2 * rows * depth * columns, bytes_accessed=6 << 20, transcendentals=0
        ),
    )(left, right)


def silu_slope(inputs):
    sigma = jax.nn.sigmoid(inputs)
    return sigma * (1.0 + inputs * (1.0 - sigma))


def history_starts(lengths, width):
    history_ends = jnp.cumsum(lengths, axis=1)
    places = jnp.arange(width, dtype=jnp.int32)
    earlier = (history_ends[:, None, :] <= places[None, :, None]).astype(jnp.int32)
    return jnp.sum(lengths[:, None, :] * earlier, axis=2)


def dot(left, right, dims=(((1,), (0,)), ((), ())), precision=None):
    return lax.dot_general(left, right, dims, precision=precision, preferred_element_type=F32)


def forward_kernel(starts_ref, pre_ref, *refs):
    n_part, tok, width = pre_ref.shape
    heads = width // (4 * HEADDIM)
    dmix_refs, outs = refs[:n_part], refs[n_part:]
    pre_out, act_out, logit_out, prob_out, att_out, dmix_out, sum_out = outs
    pre = pre_ref[0].astype(F32)
    dmix = dmix_refs[0][...].astype(F32)
    for part in range(1, n_part):
        pre = pre + pre_ref[part].astype(F32)
        dmix = dmix + dmix_refs[part][...].astype(F32)
    pre_out[...] = pre
    dmix_out[...] = dmix
    act = (pre / (1.0 + jnp.exp(-pre))).astype(BF)
    act_out[...] = act
    query = lax.broadcasted_iota(jnp.int32, (tok, tok), 0)
    key = lax.broadcasted_iota(jnp.int32, (tok, tok), 1)
    visible = (key <= query) & (key >= starts_ref[...])
    totals = [0.0, 0.0, 0.0, 0.0]
    for head in range(heads):
        at = head * 4 * HEADDIM
        gate, value, quer, keyk = [act[:, at + i * HEADDIM : at + (i + 1) * HEADDIM] for i in range(4)]
        logit = dot(quer, keyk, LAST) * HEADDIM ** (-0.5)
        logit_out[head] = logit
        prob = jnp.where(visible, logit / (1.0 + jnp.exp(-logit)) * (1.0 / HMAX), 0.0).astype(BF)
        prob_out[head] = prob
        att = dot(prob, value)
        own = pl.ds(head * HEADDIM, HEADDIM)
        att_out[:, own] = att
        dnorm = dmix[:, head * HEADDIM : (head + 1) * HEADDIM] * gate.astype(F32)
        for i, term in enumerate((att, att * att, dnorm, dnorm * att)):
            totals[i] = totals[i] + term
    table = jnp.zeros((tok, tok), F32)
    for i, total in enumerate(totals):
        table = jnp.where(key == i, jnp.sum(total, axis=1, keepdims=True), table)
    sums = table.T[:8]
    for copy in range(sum_out.shape[0]):
        sum_out[copy] = sums


def backward_kernel(total_width, sum_ref, act_ref, slope_ref, lslope_ref, prob_ref, att_ref, dmix_ref, mixed_out, dpre_out):
    tok, width = act_ref.shape
    heads = width // (4 * HEADDIM)
    means = sum_ref[0]
    for part in range(1, sum_ref.shape[0]):
        means = means + sum_ref[part]
    means = means * (1.0 / total_width)
    row = lax.broadcasted_iota(jnp.int32, (tok, tok), 0)
    col = lax.broadcasted_iota(jnp.int32, (tok, tok), 1)
    cols = dot((row == col).astype(F32), means, LAST, lax.Precision.HIGHEST)
    mean, second, grad_one, grad_att = [cols[:, i : i + 1] for i in range(4)]
    rstd = lax.rsqrt(second - mean * mean + EPS)
    grad_two = (grad_att - mean * grad_one) * rstd
    for head in range(heads):
        at = head * 4 * HEADDIM
        gate, value, quer, keyk = [act_ref[:, at + i * HEADDIM : at + (i + 1) * HEADDIM] for i in range(4)]
        own = pl.ds(head * HEADDIM, HEADDIM)
        normed = (att_ref[:, own] - mean) * rstd
        dmix = dmix_ref[:, own]
        gate = gate.astype(F32)
        mixed_out[:, own] = (normed * gate).astype(BF)
        datt = (rstd * (dmix * gate - grad_one - normed * grad_two)).astype(BF)
        dvalue = dot(prob_ref[head], datt, FIRST)
        dlogit = (dot(datt, value, LAST) * lslope_ref[head]).astype(BF)
        dquer = dot(dlogit, keyk)
        dkey = dot(dlogit, quer, FIRST)
        for i, term in enumerate((dmix * normed, dvalue, dquer, dkey)):
            place = pl.ds(at + i * HEADDIM, HEADDIM)
            dpre_out[:, place] = (term * slope_ref[:, place]).astype(BF)


def attention_forward(starts, pre_parts, dmix_parts, tok, copies):
    n_part, rows, width = pre_parts.shape
    heads = width // (4 * HEADDIM)
    head_cols = heads * HEADDIM
    owners = rows // tok
    square = lambda kind: jax.ShapeDtypeStruct((owners, heads, tok, tok), kind)
    square_spec = pl.BlockSpec((None, heads, tok, tok), lambda b: (b, 0, 0, 0))
    wide_spec = pl.BlockSpec((tok, width), lambda b: (b, 0))
    thin_spec = pl.BlockSpec((tok, head_cols), lambda b: (b, 0))
    return pl.pallas_call(
        forward_kernel,
        grid=(owners,),
        in_specs=[
            pl.BlockSpec((tok, 1), lambda b: (b, 0)),
            pl.BlockSpec((n_part, tok, width), lambda b: (0, b, 0)),
        ]
        + [thin_spec] * n_part,
        out_specs=[wide_spec, wide_spec, square_spec, square_spec, thin_spec, thin_spec, pl.BlockSpec((copies, 8, tok), lambda b: (0, 0, b))],
        out_shape=[
            jax.ShapeDtypeStruct((rows, width), F32),
            jax.ShapeDtypeStruct((rows, width), BF),
            square(F32),
            square(BF),
            jax.ShapeDtypeStruct((rows, head_cols), F32),
            jax.ShapeDtypeStruct((rows, head_cols), F32),
            jax.ShapeDtypeStruct((copies, 8, rows), F32),
        ],
        cost_estimate=pl.CostEstimate(flops=4 * rows * tok * head_cols, bytes_accessed=8 << 20, transcendentals=rows * width),
    )(starts, pre_parts, *dmix_parts)


def attention_backward(sums, act, slope, lslope, prob, att, dmix, tok, total_width):
    rows, width = act.shape
    heads = width // (4 * HEADDIM)
    head_cols = heads * HEADDIM
    owners = rows // tok
    square_spec = pl.BlockSpec((None, heads, tok, tok), lambda b: (b, 0, 0, 0))
    wide_spec = pl.BlockSpec((tok, width), lambda b: (b, 0))
    thin_spec = pl.BlockSpec((tok, head_cols), lambda b: (b, 0))
    return pl.pallas_call(
        lambda *refs: backward_kernel(total_width, *refs),
        grid=(owners,),
        in_specs=[
            pl.BlockSpec((sums.shape[0], 8, tok), lambda b: (0, 0, b)),
            wide_spec, wide_spec, square_spec, square_spec, thin_spec, thin_spec,
        ],
        out_specs=[thin_spec, wide_spec],
        out_shape=[
            jax.ShapeDtypeStruct((rows, head_cols), BF),
            jax.ShapeDtypeStruct((rows, width), BF),
        ],
        cost_estimate=pl.CostEstimate(flops=8 * rows * tok * head_cols, bytes_accessed=4 << 20, transcendentals=rows),
    )(sums, act, slope, lslope, prob, att, dmix)


def widen_kernel(place_ref, half_ref, *refs):
    refs[-1][...] = half_ref[...].astype(F32)


def place_columns(block, value, into, blocks):
    rows, width = value.shape
    extra = [] if into is None else [into]
    return pl.pallas_call(
        widen_kernel,
        grid_spec=pltpu.PrefetchScalarGridSpec(
            num_scalar_prefetch=1,
            grid=(2,),
            in_specs=[pl.BlockSpec((rows // 2, width), lambda i, block: (i, 0))]
            + [pl.BlockSpec(memory_space=pl.ANY)] * len(extra),
            out_specs=pl.BlockSpec((rows // 2, width), lambda i, block: (i, block[0])),
        ),
        out_shape=jax.ShapeDtypeStruct((rows, blocks * width), F32),
        input_output_aliases={2: 0} if extra else {},
        cost_estimate=pl.CostEstimate(flops=0, bytes_accessed=rows * width * 6, transcendentals=0),
    )(block, value, *extra)


def grad_kernel(core_ref, x_ref, d_ref, *refs):
    out = refs[-1]
    grad = dot(x_ref[...], d_ref[...])
    if len(refs) == 1:
        out[...] = grad.astype(BF)
    else:
        there_ref, low_ref, high_ref = refs[:3]
        low, mid = low_ref.shape[0], grad.shape[0]
        out[:low] = low_ref[...]
        out[low : low + mid] = (grad + there_ref[...].astype(F32)).astype(BF)
        out[low + mid :] = high_ref[...]


def grad_columns(core, x_t, d_all, *more):
    depth, width = d_all.shape
    step = width // 4
    rows = x_t.shape[0] + sum(piece.shape[0] for piece in more[1:])
    return pl.pallas_call(
        grad_kernel,
        grid_spec=pltpu.PrefetchScalarGridSpec(
            num_scalar_prefetch=1,
            grid=(2,),
            in_specs=[
                pl.BlockSpec(x_t.shape, lambda i, core: (0, 0)),
                pl.BlockSpec((depth, step), lambda i, core: (0, core[0] * 2 + i)),
            ]
            + [pl.BlockSpec((piece.shape[0], step), lambda i, core: (0, i)) for piece in more],
            out_specs=pl.BlockSpec((rows, step), lambda i, core: (0, i)),
        ),
        out_shape=jax.ShapeDtypeStruct((rows, 2 * step), BF),
        compiler_params=pltpu.CompilerParams(vmem_limit_bytes=24 << 20),
        cost_estimate=pl.CostEstimate(
            flops=4 * x_t.size * step, bytes_accessed=4 << 20, transcendentals=0
        ),
    )(core, x_t, d_all, *more)


def x_exchange(blocks):
    groups = [[2 * x + y for x in range(N_X)] for y in range(2)]
    return lax.all_to_all(blocks, "col", 0, 0, axis_index_groups=groups, tiled=True)


def head_groups_gather(value):
    groups = [[r * 2 * N_X + 2 * x + y for r in range(N_Z) for y in range(2)] for x in range(N_X)]
    return lax.all_to_all(value, ("row", "col"), 0, 0, axis_index_groups=groups, tiled=True)


def halves(array, which, axis):
    size = array.shape[axis] // 2
    return (
        lax.dynamic_slice_in_dim(array, which * size, size, axis),
        lax.dynamic_slice_in_dim(array, (1 - which) * size, size, axis),
    )


def dp_exchange(value, count):
    parts = [value[:count]]
    parts += [dp_swap(value[j * count : (j + 1) * count], j) for j in range(1, 4)]
    return jnp.concatenate(parts, axis=0)


def local(events, out_grad, w_uvqk, w_output, hist_len, token_slot):
    n_dp, n_row, n_col = 4, N_Z, 2 * N_X
    tok_own, feat = events.shape
    send_count = tok_own // n_dp
    dp_at = lax.axis_index("dp")
    row_at = lax.axis_index("row")
    col_at = lax.axis_index("col")
    x_at, ylo_at, core_at = col_at // 2, col_at % 2, dp_at % 2
    owner_self = dp_at * n_row + row_at
    places = jnp.arange(tok_own, dtype=jnp.int32)

    events_other = ylo_swap(events)
    slots = token_slot.reshape(n_dp, n_row, tok_own)
    src_slots = lax.dynamic_index_in_dim(slots, row_at, 1, keepdims=False)
    own_slots = lax.dynamic_index_in_dim(src_slots, dp_at, 0, keepdims=False)
    send_rank = jnp.sum((own_slots[None, :] < own_slots[:, None]).astype(jnp.int32), axis=1)
    target = own_slots // (tok_own * n_row)
    send_place = (target ^ dp_at) * send_count + send_rank - target * send_count
    send_pick = (send_place[None, :] == places[:, None]).astype(BF)
    x_send = dot(send_pick, jnp.concatenate([events, events_other, out_grad], axis=1)).astype(BF)
    xg_recv = dp_exchange(x_send, send_count)
    sources = jnp.arange(n_dp, dtype=jnp.int32)
    to_self = src_slots // tok_own == owner_self
    before = jnp.sum(
        (to_self[:, None, :] & (src_slots[:, None, :] < src_slots[:, :, None])).astype(jnp.int32),
        axis=2,
    )
    recv_row = (sources ^ dp_at)[:, None] * send_count + before
    local_place = src_slots - owner_self * tok_own
    hits = to_self[:, :, None] & (recv_row[:, :, None] == places[None, None, :])
    row_place = jnp.sum(jnp.where(hits, local_place[:, :, None], 0), axis=(0, 1))
    own_pick = (row_place[None, :] == places[:, None]).astype(BF)
    xg_recv, w_later = lax.optimization_barrier((xg_recv, w_uvqk))
    xg_own = dot(own_pick, xg_recv).astype(BF)
    x_own, g_own = xg_own[:, :feat], xg_own[:, 2 * feat :]

    w_keep, w_send = halves(w_later, ylo_at, 1)
    w_pair = jnp.concatenate([w_keep, ylo_swap(w_send)], axis=0)

    tokens = n_row * tok_own
    rows_half = tok_own // 2
    ups, downs = [xg_own], [xg_own]
    for _ in range(3):
        ups, downs = ups + [z_shift(ups[-1], 1)], downs + [z_shift(downs[-1], -1)]
    far_low, far_high = z_shift(ups[3][:rows_half], 1), z_shift(downs[3][rows_half:], -1)
    row_place_at = row_at.astype(jnp.int32)[None]
    near_panels = place_blocks(row_place_at, [xg_own] + downs[1:] + ups[:0:-1], 2 * feat)
    wo_keep, wo_send = halves(w_output, ylo_at, 0)
    d_other = ylo_swap(dot(near_panels[1], wo_send, LAST).astype(BF))
    x_panel, g_panel = place_far(row_place_at, far_low, far_high, near_panels)
    g_far = jnp.concatenate([far_low[:, 2 * feat :], far_high[:, 2 * feat :]], axis=0)
    d_far = ylo_swap(dot(g_far, wo_send, LAST).astype(BF))
    rows_pair = 2 * tok_own

    def x_chunk(panel, k):
        return lax.dynamic_slice_in_dim(panel, (x_at + k) % N_X * rows_pair, rows_pair, 0)

    pre_part = product(x_panel, w_pair)
    pre_parts = x_exchange(pre_part.reshape(N_X, rows_pair, -1))
    far_here = jnp.arange(n_row) == (row_at + n_row // 2) % n_row
    d_far = jnp.where(far_here[:, None, None], d_far[None].astype(F32), 0.0)
    d_pair = dot(g_panel, wo_keep, LAST) + d_other.astype(F32) + d_far.reshape(d_other.shape)
    d_pair = d_pair.astype(BF)
    dmix_parts = [x_chunk(d_pair, 0)] + [x_shift(x_chunk(d_pair, k), k) for k in (1, -1, 2)]

    lengths = lax.dynamic_slice_in_dim(hist_len, dp_at * n_row + x_at * 2, 2, 0)
    starts = history_starts(lengths, tok_own).reshape(rows_pair, 1)
    preact, act, logits, probs, att, d_mixed, sums = attention_forward(
        starts, pre_parts, dmix_parts, tok_own, 2 * n_row
    )
    sums = head_groups_gather(sums)
    slope = silu_slope(preact)
    keys = jnp.arange(tok_own, dtype=jnp.int32)
    visible = (keys[None, None, :] >= starts.reshape(2, tok_own, 1)) & (
        keys[None, None, :] <= keys[None, :, None]
    )
    lslope = jnp.where(
        visible[:, None], silu_slope(logits) * (HEADDIM ** (-0.5) / HMAX), 0.0
    )
    total_width = att.shape[1] * n_row * 2
    mixed, d_pre = attention_backward(
        sums, act, slope, lslope, probs, att, d_mixed, tok_own, total_width
    )

    x_up, x_down = x_shift(d_pre, 1), x_shift(d_pre, -1)
    mixed_there = ylo_swap(mixed)
    mixed = jnp.where(
        ylo_at == 0,
        jnp.concatenate([mixed, mixed_there], axis=1),
        jnp.concatenate([mixed_there, mixed], axis=1),
    )
    x_up, x_down, mixed = lax.optimization_barrier((x_up, x_down, mixed))
    far_low, far_high = x_shift(x_up[:tok_own], 1), x_shift(x_down[tok_own:], -1)
    d_pre_all = pre_parts
    for k, piece in ((0, d_pre), (3, x_up), (1, x_down)):
        d_pre_all = lax.dynamic_update_slice(d_pre_all, piece[None], ((x_at + k) % N_X, 0, 0))
    d_far = jnp.concatenate([far_low, far_high], axis=0)
    d_pre_all = lax.dynamic_update_slice(d_pre_all, d_far[None], ((x_at + 2) % N_X, 0, 0))
    d_pre_all = d_pre_all.reshape(tokens, -1)
    mixed_all = x_exchange(jnp.broadcast_to(mixed[None], (N_X,) + mixed.shape))
    mixed_all = mixed_all.reshape(tokens, -1)

    def z_chunk(panel, k):
        return lax.dynamic_slice_in_dim(panel, (row_at + k) % n_row * tok_own, tok_own, 0)

    far = dot(z_chunk(d_pre_all, 4), w_pair, LAST).astype(BF)
    far, d_pre_all = lax.optimization_barrier((far, d_pre_all))
    up, down = z_shift(far[:, :feat], 1), z_shift(far[:, feat:], -1)

    half = feat // 2
    x_t = x_panel.T
    x_t = jnp.concatenate([x_t[:half], x_t[feat:], x_t[half:feat]], axis=0)
    x_t = lax.optimization_barrier(x_t)
    core = core_at.astype(jnp.int32)[None]
    ug_there, d_pre_all = lax.optimization_barrier(
        (grad_columns(1 - core, x_t, d_pre_all), d_pre_all)
    )
    ug_there = dp_swap(ug_there, 1)
    m_keep, m_send = halves(mixed_all, core_at, 1)
    og_there = dp_swap(dot(m_send.T, g_panel).astype(BF), 1)
    og_sum = dot(m_keep.T, g_panel) + og_there.astype(F32)
    og_mid = og_sum.shape[0] // 2
    og_low, og_high = og_sum[:og_mid].astype(BF), og_sum[og_mid:].astype(BF)
    grads = grad_columns(core, x_t, d_pre_all, ug_there, og_low, og_high)

    dx_all = dot(d_pre_all, w_pair, LAST).astype(BF)
    out_all = dot(mixed_all, w_output).astype(BF)
    part = feat // 2

    dx_terms = lax.optimization_barrier([z_chunk(dx_all, k) for k in range(n_row)])
    out_terms = lax.optimization_barrier([z_chunk(out_all, k) for k in range(n_row)])

    def term(k):
        return dx_terms[k].astype(F32)

    def out_term(k):
        return out_terms[k].astype(F32)

    def message(dx, out):
        return jnp.concatenate([dx.astype(BF), out.astype(BF)], axis=1)

    to_up, to_down = term(3), term(-3)
    to_up = jnp.concatenate([to_up[:, :feat] + up.astype(F32), to_up[:, feat:]], axis=1)
    to_down = jnp.concatenate([to_down[:, :feat], to_down[:, feat:] + down.astype(F32)], axis=1)
    out_far = out_term(4)
    up = z_shift(message(to_up, out_far[:, :part]), 1)
    down = z_shift(message(to_down, out_far[:, part:]), -1)
    y_up, y_down = grads[og_mid + half :], grads[: og_mid + half + feat]
    up, down, y_later = lax.optimization_barrier((up, down, (y_up, y_down)))
    y_up, y_down = y_shift(y_up, 1), y_shift(y_down, -1)
    wide = 2 * feat
    out_up, out_down = out_term(3), out_term(-3)
    out_up = jnp.concatenate([out_up[:, :part] + up[:, wide:].astype(F32), out_up[:, part:]], axis=1)
    out_down = jnp.concatenate([out_down[:, :part], out_down[:, part:] + down[:, wide:].astype(F32)], axis=1)
    up, down = (
        z_shift(message(term(2) + up[:, :wide].astype(F32), out_up), 1),
        z_shift(message(term(-2) + down[:, :wide].astype(F32), out_down), -1),
    )
    to_up = message(term(1) + up[:, :wide].astype(F32), out_term(2) + up[:, wide:].astype(F32))
    to_down = message(term(-1) + down[:, :wide].astype(F32), out_term(-2) + down[:, wide:].astype(F32))
    up, down = z_shift(to_up, 1), z_shift(to_down, -1)
    up, down, y_up, y_down = lax.optimization_barrier((up, down, y_up, y_down))
    far_up, far_down = y_shift(y_up[feat:], 1), y_shift(y_down[: og_mid + half], -1)
    ug_cross = y_up[:feat].astype(F32) + y_down[og_mid + half :].astype(F32)
    rows = term(0) + up[:, :wide].astype(F32) + down[:, :wide].astype(F32)
    dx_other = ylo_swap(rows[:, feat:].astype(BF))
    out_up = z_shift((out_term(1) + up[:, wide:].astype(F32)).astype(BF), 1)
    out_down = z_shift((out_term(-1) + down[:, wide:].astype(F32)).astype(BF), -1)
    out_rows = out_term(0) + out_up.astype(F32) + out_down.astype(F32)

    ug_stay = jnp.concatenate(
        [
            y_later[1][og_mid : og_mid + half].astype(F32) + far_down[og_mid:].astype(F32),
            y_later[0][feat:-og_mid].astype(F32) + far_up[:half].astype(F32),
        ],
        axis=0,
    )
    ug_stay, ug_cross = ug_stay.astype(BF), ug_cross.astype(BF)
    og_half = jnp.concatenate(
        [
            og_sum[:og_mid] + far_down[:og_mid].astype(F32),
            og_sum[og_mid:] + far_up[half:].astype(F32),
        ],
        axis=0,
    ).astype(BF)
    cross_there, stay_there, og_there = dp_swap(ug_cross, 1), dp_swap(ug_stay, 1), dp_swap(og_half, 1)
    dx_own = (rows[:, :feat] + dx_other.astype(F32) + g_own.astype(F32)).astype(BF)
    y_own = (out_rows + x_own.astype(F32)).astype(BF)
    back = dot(own_pick, jnp.concatenate([y_own, dx_own], axis=1), FIRST).astype(BF)
    home = dp_exchange(back, send_count)
    layer_out = dot(send_pick, home[:, :feat], FIRST).astype(BF)
    event_grad = dot(send_pick, home[:, feat:], FIRST).astype(BF)
    output_grad = jnp.where(
        core_at == 0,
        jnp.concatenate([og_half, og_there], axis=0),
        jnp.concatenate([og_there, og_half], axis=0),
    ).astype(F32)
    ylo = ylo_at.astype(jnp.int32)[None]
    near, other = 2 * ylo, 2 * (1 - ylo)
    uvqk_grad = place_columns(other + core, ug_cross, None, 4)
    uvqk_grad = place_columns(other + 1 - core, cross_there, uvqk_grad, 4)
    uvqk_grad = place_columns(near + core, ug_stay, uvqk_grad, 4)
    uvqk_grad = place_columns(near + 1 - core, stay_there, uvqk_grad, 4)
    return (layer_out, event_grad, uvqk_grad, output_grad)


def solution(mesh):
    in_specs = (
        P(("dp", "row"), "col"),
        P(("dp", "row"), "col"),
        P("col", "row"),
        P("row", "col"),
        P(),
        P(),
    )
    out_specs = (P(("dp", "row"), "col"), P(("dp", "row"), "col"), P("col", "row"), P("row", "col"))
    return jax.shard_map(local, mesh=mesh, in_specs=in_specs, out_specs=out_specs, check_vma=False)
```
